512 devices in a mesh: dp: 64 (over z, y_lo, core), tensor: 8 (over y_hi, x).
Axes of the slice: x: 4, y: 4 (y_hi: 2, y_lo: 2; y = y_hi * 2 + y_lo), z: 16, core: 2. Of those that a mesh axis runs over, the one named last changes fastest.
Arguments:
- hidden: bfloat16 [65536, 8192], P(('dp', 'tensor')), may hold values from -6 to 6
- norm_gain: bfloat16 [8192], replicated, may hold values from 0.25 to 1.75
- teacher_k: bfloat16 [8192, 512], P('dp', 'tensor'), may hold values from -0.0625 to 0.0625
- student_k: bfloat16 [8192, 512], P('dp', 'tensor'), may hold values from -0.0625 to 0.0625
- keep_pattern: int32 [2048, 512], P(None, 'tensor'), may hold values from 0 to 5
Outputs:
- grad: float32 [8192, 512], P('dp', 'tensor')
- loss: float32 [], replicated
The draws below stay inside these ranges and needn't reach their ends.
All inputs are finite; a program needn't handle non-finite values.
Results may differ from the reference program's by a relative error of at most 0.0016.
Values may be sent and summed in bfloat16 or wider, within the bound.
No kernel may reach another device: no remote copies, remote signals or barrier semaphores. Data moves between devices by JAX's collectives and lax.ppermute only.
A program may use at most 128 MiB of HBM per device.

```python
import jax
import jax.numpy as jnp
from jax import lax

D = 8192
KVW = 512
TOKENS = 65536


def with_ends(drawn, own_key, smallest, high):
    longest = drawn.shape.index(max(drawn.shape))
    spots = []
    for shift in (0, 1):
        where = [jax.random.randint(jax.random.fold_in(own_key, axis), (), 0, length) for axis, length in enumerate(drawn.shape)]
        where[longest] = (where[longest] + shift) % drawn.shape[longest]
        spots.append(tuple(where))
    return drawn.at[spots[0]].set(smallest).at[spots[1]].set(high)


def block_levels(own_key, dims, split, smallest, top_value):
    def one(dim, blocks):
        heights = jax.random.uniform(jax.random.fold_in(jax.random.fold_in(own_key, 6), dim), (blocks,), jnp.float32, smallest / len(split), top_value / len(split))
        return jnp.repeat(jnp.exp(heights), dims[dim] // blocks).reshape((-1,) + (1,) * (len(dims) - dim - 1))

    level = one(*split[0])
    for cut in split[1:]:
        level = level * one(*cut)
    return level


def noise(stream_key, dims, deviation, limit, split=(), kind=jnp.bfloat16):
    drawn = jax.random.normal(stream_key, dims, jnp.float32) * deviation
    if len(split) > 0:
        drawn = block_levels(stream_key, dims, split, -0.22, 0.18) * drawn
    return jnp.clip(drawn, min=-limit, max=limit).astype(kind)


def setup_inputs(seed: int = 0) -> dict:
    arg_keys = jax.random.split(jax.random.key(seed), 6)
    return {
        "hidden": noise(arg_keys[0], (TOKENS, D), 1.0, 6.0, ((0, 512),)),
        "norm_gain": jnp.clip(1.0 + 0.15 * jax.random.normal(arg_keys[1], (D,), jnp.float32), 0.25, 1.75).astype(jnp.bfloat16),
        "teacher_k": noise(arg_keys[2], (D, KVW), D ** -0.5, 0.0625, ((0, 64), (1, 8))),
        "student_k": noise(arg_keys[3], (D, KVW), D ** -0.5, 0.0625, ((0, 64), (1, 8))),
        "keep_pattern": with_ends(jax.random.randint(arg_keys[4], (D // 4, KVW), 0, 6), jax.random.fold_in(arg_keys[4], 1), 0, 5).astype(jnp.int32),
    }


def keep_table(keep_pattern):
    first = (keep_pattern > 2).astype(jnp.int32) + (keep_pattern > 4).astype(jnp.int32)
    second = jnp.where(keep_pattern < 3, keep_pattern + 1, jnp.where(keep_pattern == 3, 2, 3)).astype(jnp.int32)
    spots = jnp.arange(4, dtype=jnp.int32)[None, :, None]
    keep = (first[:, None, :] == spots) | (second[:, None, :] == spots)
    return keep.reshape(keep_pattern.shape[0] * 4, keep_pattern.shape[1]).astype(jnp.bfloat16)

def reference(hidden, norm_gain, teacher_k, student_k, keep_pattern):
    x32 = hidden.astype(jnp.float32)
    scale = jax.lax.rsqrt(lax.optimization_barrier(jnp.mean(x32 * x32, axis=-1, keepdims=True)) + 1e-05)
    normed = (x32 * scale * norm_gain.astype(jnp.float32)).astype(jnp.bfloat16)
    target = jnp.dot(normed, teacher_k, preferred_element_type=jnp.float32).astype(jnp.bfloat16)
    keep = keep_table(keep_pattern)
    masked = student_k * keep
    diff = jnp.dot(normed, masked, preferred_element_type=jnp.float32) - target.astype(jnp.float32)
    loss = jnp.sum(diff * diff) / (TOKENS * KVW)
    slope = diff.astype(jnp.bfloat16)
    summed = jnp.dot(normed.T, slope, preferred_element_type=jnp.float32)
    grad = keep.astype(jnp.float32) * summed / jnp.sqrt(jnp.float32(TOKENS))
    return (grad, loss)
```

```python
import jax
import jax.numpy as jnp
from jax import lax
from jax.experimental import pallas as pl
from jax.experimental.pallas import tpu as pltpu
from jax.sharding import Mesh, PartitionSpec as P

F32 = jnp.float32
BF16 = jnp.bfloat16
NZ, NYL, NC, NYH, NX = 16, 2, 2, 2, 4
AXES = ("z", "yl", "core", "yh", "x")
Y = ("yl", "yh")
ZCX = ("z", "core", "x")
D, KVW, TOKENS = 8192, 512, 65536
SHIFT = 34
VMEM = pl.BlockSpec(memory_space=pltpu.VMEM)


def call(kernel, out_shape, *args, scratch=(), flops=0, name=None):
    size = sum(a.size * a.dtype.itemsize for a in args)
    for o in jax.tree.leaves(out_shape):
        size += o.size * o.dtype.itemsize
    return pl.pallas_call(
        kernel,
        out_shape=out_shape,
        in_specs=[VMEM] * len(args),
        out_specs=jax.tree.map(lambda _: VMEM, out_shape),
        scratch_shapes=list(scratch),
        name=name,
        cost_estimate=pl.CostEstimate(flops=flops, bytes_accessed=size, transcendentals=0),
        compiler_params=pltpu.CompilerParams(vmem_limit_bytes=48 * 1024 * 1024),
    )(*args)


def shape(dims, dtype):
    return jax.ShapeDtypeStruct(dims, dtype)


def lane_group(dims):
    return lax.broadcasted_iota(jnp.int32, dims, len(dims) - 1) // 32


def swap_groups(parts, place):
    total = None
    for b, part in enumerate(parts):
        shift = (b - place) * 32 % 128
        moved = pltpu.roll(part, shift, part.ndim - 1) if shift else part
        here = jnp.where(lane_group(part.shape) == b, moved, 0.0)
        total = here if total is None else total + here
    return total


def keep_of(patterns):
    row = lax.broadcasted_iota(jnp.int32, (128, 32), 0)
    col = lax.broadcasted_iota(jnp.int32, (128, 32), 1)
    spread = jnp.where(row // 4 == col, 1.0, 0.0)
    pat = jnp.dot(spread.astype(BF16), patterns.astype(F32).astype(BF16), preferred_element_type=F32)
    first = jnp.where(pat > 2.5, 1.0, 0.0) + jnp.where(pat > 4.5, 1.0, 0.0)
    second = jnp.where(pat < 2.5, pat + 1.0, jnp.where(pat < 3.5, 2.0, 3.0))
    spot = (lax.broadcasted_iota(jnp.int32, pat.shape, 0) % 4).astype(F32)
    return jnp.where((spot == first) | (spot == second), 1.0, 0.0)


def norm_kernel(x_ref, gain_ref, out_ref, rows_ref):
    total = jnp.zeros((128, 512), F32)
    for g in range(16):
        part = x_ref[:, g * 512 : (g + 1) * 512].astype(F32)
        total += part * part
    factor = lax.rsqrt(jnp.sum(total, axis=1, keepdims=True) / D + 1e-05)
    for yl in range(2):
        for m in range(8):
            for half in range(2):
                at = (8 * m + 4 * half + 2 * yl) * 128
                part = x_ref[:, at : at + 256].astype(F32)
                gain = gain_ref[:, at : at + 256].astype(F32)
                tile = yl * 8 + m
                rows_ref[tile * 128 : (tile + 1) * 128, half * 256 : (half + 1) * 256] = (
                    part * factor * gain
                ).astype(BF16)
    src = lax.broadcasted_iota(jnp.int32, (512, 512), 0)
    dst = lax.broadcasted_iota(jnp.int32, (512, 512), 1)
    goal = (src // 32 % 4) * 128 + src // 128 * 32 + src % 32
    move = jnp.where(goal == dst, 1.0, 0.0).astype(BF16)
    for tile in range(16):
        seg = jnp.dot(
            rows_ref[tile * 128 : (tile + 1) * 128, :], move, preferred_element_type=F32
        ).astype(BF16)
        for x in range(NX):
            out_ref[x, :, tile * 128 : (tile + 1) * 128] = seg[:, x * 128 : (x + 1) * 128]


def pack_kernel(teacher_ref, student_ref, pat_ref, out_ref):
    keep = keep_of(pat_ref[...])
    delta = student_ref[...].astype(F32) * keep - teacher_ref[...].astype(F32)
    delta = delta * 2.0**SHIFT
    delta = (delta * jnp.abs(delta)) * (delta * delta)
    row = lax.broadcasted_iota(jnp.int32, (64, 128), 0)
    col = lax.broadcasted_iota(jnp.int32, (64, 128), 1)
    widen = jnp.where(row == col, 1.0, 0.0).astype(BF16)
    wide = jnp.dot(delta.astype(BF16), widen, preferred_element_type=F32).reshape(4, 4, 8, 128)
    for c in range(NC):
        piece = swap_groups([wide[:, q] for q in range(4)], c).reshape(32, 128).astype(BF16)
        for z in range(NZ):
            out_ref[z, c * 32 : (c + 1) * 32, :] = piece


def spread_kernel(got_ref, out_ref, mid_ref):
    got = got_ref[...].astype(F32).reshape(32, 4, 8, 128)
    for q in range(4):
        mid_ref[:, q] = swap_groups([got[:, x] for x in range(NX)], q)
    rows = mid_ref[...].reshape(1024, 128).astype(BF16)
    for y in range(4):
        out_ref[y] = rows


def forward_kernel(own_ref, pair_ref, w_ref, out_ref, high_ref, low_ref):
    for y in range(4):
        for k in range(4):
            sent = w_ref[y, k * 256 : (k + 1) * 256, :].astype(F32)
            size = jnp.sqrt(jnp.sqrt(jnp.abs(sent))) * 2.0**-SHIFT
            delta = jnp.where(sent < 0, -size, size)
            high = delta.astype(BF16)
            at = (y // 2) * 1024 + k * 256
            lane = (y % 2) * 128
            high_ref[at : at + 256, lane : lane + 128] = high
            low_ref[at : at + 256, lane : lane + 128] = (delta - high.astype(F32)).astype(BF16)
    for x in range(NX):
        for ref, row in ((own_ref, 0), (pair_ref, 128)):
            part = jnp.dot(ref[x], high_ref[...], preferred_element_type=F32)
            part += jnp.dot(ref[x], low_ref[...], preferred_element_type=F32)
            out_ref[x, row : row + 128] = part.astype(BF16)


def slope_kernel(part_ref, out_ref, loss_ref):
    diff = part_ref[0].astype(F32)
    for x in range(1, NX):
        diff = diff + part_ref[x].astype(F32)
    slope = diff.astype(BF16)
    for x in range(NX):
        out_ref[x] = slope
    square = diff * diff
    lanes = square[:, :128] + square[:, 128:]
    loss_ref[...] = jnp.sum(lanes.reshape(32, 8, 128), axis=0)


def grad_kernel(own_ref, pair_ref, slope_ref, out_ref):
    contract = (((0,), (0,)), ((), ()))
    own_s = slope_ref[:, :128, :].reshape(512, 256)
    pair_s = slope_ref[:, 128:, :].reshape(512, 256)
    for k in range(8):
        at = k * 256
        own = own_ref[:, :, at : at + 256].reshape(512, 256)
        pair = pair_ref[:, :, at : at + 256].reshape(512, 256)
        term = lax.dot_general(own, own_s, contract, preferred_element_type=F32)
        term += lax.dot_general(pair, pair_s, contract, preferred_element_type=F32)
        term = term.astype(BF16)
        for yh in range(2):
            out_ref[(k // 4) * 2 + yh, (k % 4) * 256 : (k % 4 + 1) * 256, :] = term[
                :, yh * 128 : (yh + 1) * 128
            ]


def gather_kernel(got_ref, out_ref, mid_ref):
    total = got_ref[0].astype(F32)
    for y in range(1, 4):
        total = total + got_ref[y].astype(F32)
    total = total.reshape(32, 4, 8, 128)
    for x in range(NX):
        mid_ref[:, x] = swap_groups([total[:, q] for q in range(4)], x)
    out_ref[...] = mid_ref[...].reshape(1024, 128).astype(BF16)


def final_kernel(got_ref, pat_ref, out_ref, mid_ref):
    total = got_ref[0].astype(F32)
    for z in range(1, NZ):
        total = total + got_ref[z].astype(F32)
    total = total.reshape(2, 4, 8, 128)
    for q in range(4):
        mid_ref[:, q] = swap_groups([total[0], total[1]], q)
    rows = mid_ref[...].reshape(128, 128)[:, :64]
    out_ref[...] = keep_of(pat_ref[...]) * rows / jnp.sqrt(F32(TOKENS))


def shards(hidden, norm_gain, teacher_k, student_k, keep_pattern):
    z, yl, core = (lax.axis_index(a) for a in ("z", "yl", "core"))
    place = (z * NYL + yl) * NC + core
    pat = lax.dynamic_slice_in_dim(keep_pattern, place * 32, 32, 0)

    packed = call(pack_kernel, shape((NZ, 64, 128), BF16), teacher_k, student_k, pat, name="pack")
    got_w = lax.all_to_all(packed.reshape(128, 8, 128), ZCX, 0, 0, tiled=True)

    split = call(
        norm_kernel,
        shape((NX, 128, 2048), BF16),
        hidden,
        norm_gain.reshape(1, D),
        scratch=[pltpu.VMEM((2048, 512), BF16)],
        flops=2 * 2048 * 512 * 512,
        name="norm",
    )
    own = lax.all_to_all(split, "x", 0, 0, tiled=True)
    pair = lax.ppermute(own, "core", [(0, 1), (1, 0)])

    rows_w = call(
        spread_kernel,
        shape((4, 1024, 128), BF16),
        got_w.reshape(1024, 128),
        scratch=[pltpu.VMEM((32, 4, 8, 128), F32)],
        name="spread",
    )
    all_w = lax.all_to_all(rows_w, Y, 0, 0, tiled=True)

    flops = 2 * 1024 * 2048 * 256
    part = call(
        forward_kernel,
        shape((NX, 256, 256), BF16),
        own,
        pair,
        all_w,
        scratch=[pltpu.VMEM((2048, 256), BF16)] * 2,
        flops=2 * flops,
        name="forward",
    )
    got_part = lax.all_to_all(part, "x", 0, 0, tiled=True)
    slope, loss_part = call(
        slope_kernel, (shape((NX, 256, 256), BF16), shape((8, 128), F32)), got_part, name="slope"
    )
    slopes = lax.all_to_all(slope, "x", 0, 0, tiled=True)
    term = call(
        grad_kernel, shape((4, 1024, 128), BF16), own, pair, slopes, flops=flops, name="grad"
    )
    got_term = lax.all_to_all(term, Y, 0, 0, tiled=True)
    packed_term = call(
        gather_kernel,
        shape((1024, 128), BF16),
        got_term,
        scratch=[pltpu.VMEM((32, 4, 8, 128), F32)],
        name="gather",
    )
    got_sum = lax.all_to_all(packed_term.reshape(128, 8, 128), ZCX, 0, 0, tiled=True)
    grad = call(
        final_kernel,
        shape((128, 64), F32),
        got_sum.reshape(NZ, 64, 128),
        pat,
        scratch=[pltpu.VMEM((4, 4, 8, 128), F32)],
        name="final",
    )

    plane = ("yl", "core", "yh", "x")
    loss_plane = lax.all_to_all(
        jnp.broadcast_to(loss_part, (32, 8, 128)), plane, 0, 0, tiled=True
    ).sum(0)
    loss_all = lax.all_to_all(jnp.broadcast_to(loss_plane, (NZ, 8, 128)), "z", 0, 0, tiled=True)
    loss = jnp.sum(loss_all) / (TOKENS * KVW)
    return grad, loss


def solution(mesh):
    fine = Mesh(mesh.devices.reshape(NZ, NYL, NC, NYH, NX), AXES)
    dp, tensor = ("z", "yl", "core"), ("yh", "x")
    in_specs = (P(AXES, None), P(), P(dp, tensor), P(dp, tensor), P(None, tensor))
    out_specs = (P(dp, tensor), P())
    return jax.shard_map(shards, mesh=fine, in_specs=in_specs, out_specs=out_specs, check_vma=False)
```

```python
import jax
import jax.numpy as jnp
from jax import lax
from jax.experimental import pallas as pl
from jax.experimental.pallas import tpu as pltpu
from jax.sharding import Mesh, PartitionSpec as P

F32 = jnp.float32
BF16 = jnp.bfloat16
NZ, NYL, NC, NYH, NX = 16, 2, 2, 2, 4
AXES = ("z", "yl", "core", "yh", "x")
Y = ("yl", "yh")
ZCX = ("z", "core", "x")
D, KVW, TOKENS = 8192, 512, 65536
SHIFT = 34
VMEM = pl.BlockSpec(memory_space=pltpu.VMEM)
SMEM = pl.BlockSpec(memory_space=pltpu.SMEM)
BACK = (0, 3, 2, 1)


def call(kernel, out_shape, *args, scratch=(), flops=0, name=None):
    size = sum(a.size * a.dtype.itemsize for a in args)
    for o in jax.tree.leaves(out_shape):
        size += o.size * o.dtype.itemsize
    return pl.pallas_call(
        kernel,
        out_shape=out_shape,
        in_specs=[SMEM if a.shape == (1,) else VMEM for a in args],
        out_specs=jax.tree.map(lambda _: VMEM, out_shape),
        scratch_shapes=list(scratch),
        name=name,
        cost_estimate=pl.CostEstimate(flops=flops, bytes_accessed=size, transcendentals=0),
        compiler_params=pltpu.CompilerParams(vmem_limit_bytes=48 * 1024 * 1024),
    )(*args)


def shape(dims, dtype):
    return jax.ShapeDtypeStruct(dims, dtype)


def lane_group(dims):
    return lax.broadcasted_iota(jnp.int32, dims, len(dims) - 1) // 32


def swap_groups(parts, place):
    total = None
    for b, part in enumerate(parts):
        shift = (b - place) * 32 % 128
        moved = pltpu.roll(part, shift, part.ndim - 1) if shift else part
        here = jnp.where(lane_group(part.shape) == b, moved, 0.0)
        total = here if total is None else total + here
    return total


def keep_of(patterns):
    row = lax.broadcasted_iota(jnp.int32, (128, 32), 0)
    col = lax.broadcasted_iota(jnp.int32, (128, 32), 1)
    spread = jnp.where(row // 4 == col, 1.0, 0.0)
    pat = jnp.dot(spread.astype(BF16), patterns.astype(F32).astype(BF16), preferred_element_type=F32)
    first = jnp.where(pat > 2.5, 1.0, 0.0) + jnp.where(pat > 4.5, 1.0, 0.0)
    second = jnp.where(pat < 2.5, pat + 1.0, jnp.where(pat < 3.5, 2.0, 3.0))
    spot = (lax.broadcasted_iota(jnp.int32, pat.shape, 0) % 4).astype(F32)
    return jnp.where((spot == first) | (spot == second), 1.0, 0.0)


def norm_kernel(x_ref, gain_ref, me_ref, *rest):
    outs, rows_ref = rest[:NX], rest[NX]
    total = jnp.zeros((128, 512), F32)
    for g in range(16):
        part = x_ref[:, g * 512 : (g + 1) * 512].astype(F32)
        total += part * part
    factor = lax.rsqrt(jnp.sum(total, axis=1, keepdims=True) / D + 1e-05)
    for yl in range(2):
        for m in range(8):
            for half in range(2):
                at = (8 * m + 4 * half + 2 * yl) * 128
                part = x_ref[:, at : at + 256].astype(F32)
                gain = gain_ref[:, at : at + 256].astype(F32)
                tile = yl * 8 + m
                rows_ref[tile * 128 : (tile + 1) * 128, half * 256 : (half + 1) * 256] = (
                    part * factor * gain
                ).astype(BF16)
    src = lax.broadcasted_iota(jnp.int32, (512, 512), 0)
    dst = lax.broadcasted_iota(jnp.int32, (512, 512), 1)
    ahead = (src // 32 + NX - me_ref[0]) % NX
    goal = ahead * 128 + src // 128 * 32 + src % 32
    move = jnp.where(goal == dst, 1.0, 0.0).astype(BF16)
    for tile in range(16):
        seg = jnp.dot(
            rows_ref[tile * 128 : (tile + 1) * 128, :], move, preferred_element_type=F32
        ).astype(BF16)
        for x in range(NX):
            outs[x][:, tile * 128 : (tile + 1) * 128] = seg[:, x * 128 : (x + 1) * 128]


def pack_kernel(teacher_ref, student_ref, pat_ref, out_ref):
    keep = keep_of(pat_ref[...])
    delta = student_ref[...].astype(F32) * keep - teacher_ref[...].astype(F32)
    delta = delta * 2.0**SHIFT
    delta = (delta * jnp.abs(delta)) * (delta * delta)
    row = lax.broadcasted_iota(jnp.int32, (64, 128), 0)
    col = lax.broadcasted_iota(jnp.int32, (64, 128), 1)
    widen = jnp.where(row == col, 1.0, 0.0).astype(BF16)
    wide = jnp.dot(delta.astype(BF16), widen, preferred_element_type=F32).reshape(4, 4, 8, 128)
    for c in range(NC):
        piece = swap_groups([wide[:, q] for q in range(4)], c).reshape(32, 128).astype(BF16)
        for z in range(NZ):
            out_ref[z, c * 32 : (c + 1) * 32, :] = piece


def spread_kernel(got_ref, out_ref, mid_ref):
    got = got_ref[...].astype(F32).reshape(32, 4, 8, 128)
    for q in range(4):
        mid_ref[:, q] = swap_groups([got[:, x] for x in range(NX)], q)
    rows = mid_ref[...].reshape(1024, 128).astype(BF16)
    for y in range(4):
        out_ref[y] = rows


def forward_kernel(*refs):
    pieces, (w_ref, me_ref, out_ref, high_ref, low_ref) = refs[: 2 * NX], refs[2 * NX :]
    for y in range(4):
        for k in range(4):
            sent = w_ref[y, k * 256 : (k + 1) * 256, :].astype(F32)
            size = jnp.sqrt(jnp.sqrt(jnp.abs(sent))) * 2.0**-SHIFT
            delta = jnp.where(sent < 0, -size, size)
            high = delta.astype(BF16)
            at = (y // 2) * 1024 + k * 256
            lane = (y % 2) * 128
            high_ref[at : at + 256, lane : lane + 128] = high
            low_ref[at : at + 256, lane : lane + 128] = (delta - high.astype(F32)).astype(BF16)
    for i in range(NX):
        x = (me_ref[0] + BACK[i]) % NX
        for ref, row in ((pieces[i], 0), (pieces[NX + i], 128)):
            part = jnp.dot(ref[...], high_ref[...], preferred_element_type=F32)
            part += jnp.dot(ref[...], low_ref[...], preferred_element_type=F32)
            out_ref[x, row : row + 128] = part.astype(BF16)


def thirds(value, rows):
    high = value.astype(BF16).astype(F32)
    mid = (value - high).astype(BF16).astype(F32)
    low = value - high - mid
    row = lax.broadcasted_iota(jnp.int32, (rows, value.shape[1]), 0)
    return jnp.where(row == 0, high, jnp.where(row == 1, mid, jnp.where(row == 2, low, 0.0)))


def slope_kernel(part_ref, out_ref, loss_ref):
    diff = part_ref[0].astype(F32)
    for x in range(1, NX):
        diff = diff + part_ref[x].astype(F32)
    slope = diff.astype(BF16)
    for x in range(NX):
        out_ref[x] = slope
    square = diff * diff
    loss_ref[...] = jnp.sum(square[:, :128] + square[:, 128:], axis=0, keepdims=True)


def grad_kernel(*refs):
    pieces, (slope_ref, loss_ref, me_ref, out_ref, s_ref) = refs[: 2 * NX], refs[2 * NX :]
    contract = (((0,), (0,)), ((), ()))
    for i in range(NX):
        x = (me_ref[0] + BACK[i]) % NX
        s_ref[i * 128 : (i + 1) * 128] = slope_ref[x, :128]
        s_ref[512 + i * 128 : 512 + (i + 1) * 128] = slope_ref[x, 128:]
    for k in range(8):
        at = k * 256
        rows = jnp.concatenate([p[:, at : at + 256] for p in pieces], axis=0)
        term = lax.dot_general(rows, s_ref[...], contract, preferred_element_type=F32)
        term = term.astype(BF16)
        for yh in range(2):
            out_ref[(k // 4) * 2 + yh, (k % 4) * 256 : (k % 4 + 1) * 256, :] = term[
                :, yh * 128 : (yh + 1) * 128
            ]
    loss = thirds(loss_ref[...], 16).astype(BF16)
    for y in range(4):
        out_ref[y, 1024:, :] = loss


def gather_kernel(got_ref, out_ref, mid_ref):
    total = got_ref[0].astype(F32)
    for y in range(1, 4):
        total = total + got_ref[y].astype(F32)
    loss = jnp.sum(total[1024:], axis=0, keepdims=True)
    mid_ref[:, :, 8:, :] = jnp.broadcast_to(thirds(loss, 8), (32, 4, 8, 128))
    total = total[:1024].reshape(32, 4, 8, 128)
    for x in range(NX):
        mid_ref[:, x, :8, :] = swap_groups([total[:, q] for q in range(4)], x)
    out_ref[...] = mid_ref[...].reshape(128, 16, 128).astype(BF16)


def final_kernel(got_ref, pat_ref, out_ref, loss_ref, mid_ref):
    total = got_ref[0].astype(F32)
    for z in range(1, NZ):
        total = total + got_ref[z].astype(F32)
    loss = jnp.sum(jnp.sum(total[:, 8:], axis=0), axis=0, keepdims=True)
    loss_ref[...] = jnp.sum(loss, axis=1, keepdims=True) / (TOKENS * KVW)
    total = total[:, :8].reshape(2, 4, 8, 128)
    for q in range(4):
        mid_ref[:, q] = swap_groups([total[0], total[1]], q)
    rows = mid_ref[...].reshape(128, 128)[:, :64]
    out_ref[...] = keep_of(pat_ref[...]) * rows / jnp.sqrt(F32(TOKENS))


def ring(step):
    return [(i, (i + step) % NX) for i in range(NX)]


def shards(hidden, norm_gain, teacher_k, student_k, keep_pattern):
    z, yl, core, x = (lax.axis_index(a) for a in ("z", "yl", "core", "x"))
    place = (z * NYL + yl) * NC + core
    me = x.reshape(1).astype(jnp.int32)
    pat = lax.dynamic_slice_in_dim(keep_pattern, place * 32, 32, 0)

    packed = call(pack_kernel, shape((NZ, 64, 128), BF16), teacher_k, student_k, pat, name="pack")
    got_w = lax.all_to_all(packed.reshape(128, 8, 128), ZCX, 0, 0, tiled=True)

    split = call(
        norm_kernel,
        (shape((128, 2048), BF16),) * NX,
        hidden,
        norm_gain.reshape(1, D),
        me,
        scratch=[pltpu.VMEM((2048, 512), BF16)],
        flops=2 * 2048 * 512 * 512,
        name="norm",
    )
    own = [split[0]] + [lax.ppermute(split[i], "x", ring(i)) for i in range(1, NX)]
    pair = [lax.ppermute(piece, "core", [(0, 1), (1, 0)]) for piece in own]

    rows_w = call(
        spread_kernel,
        shape((4, 1024, 128), BF16),
        got_w.reshape(1024, 128),
        scratch=[pltpu.VMEM((32, 4, 8, 128), F32)],
        name="spread",
    )
    all_w = lax.all_to_all(rows_w, Y, 0, 0, tiled=True)

    flops = 2 * 1024 * 2048 * 256
    part = call(
        forward_kernel,
        shape((NX, 256, 256), BF16),
        *own,
        *pair,
        all_w,
        me,
        scratch=[pltpu.VMEM((2048, 256), BF16)] * 2,
        flops=2 * flops,
        name="forward",
    )
    got_part = lax.all_to_all(part, "x", 0, 0, tiled=True)
    slope, loss_part = call(
        slope_kernel, (shape((NX, 256, 256), BF16), shape((1, 128), F32)), got_part, name="slope"
    )
    slopes = lax.all_to_all(slope, "x", 0, 0, tiled=True)
    term = call(
        grad_kernel,
        shape((4, 1040, 128), BF16),
        *own,
        *pair,
        slopes,
        loss_part,
        me,
        scratch=[pltpu.VMEM((1024, 256), BF16)],
        flops=flops,
        name="grad",
    )
    got_term = lax.all_to_all(term, Y, 0, 0, tiled=True)
    packed_term = call(
        gather_kernel,
        shape((128, 16, 128), BF16),
        got_term,
        scratch=[pltpu.VMEM((32, 4, 16, 128), F32)],
        name="gather",
    )
    got_sum = lax.all_to_all(packed_term, ZCX, 0, 0, tiled=True)
    grad, loss = call(
        final_kernel,
        (shape((128, 64), F32), shape((1, 1), F32)),
        got_sum.reshape(NZ, 8, 16, 128),
        pat,
        scratch=[pltpu.VMEM((4, 4, 8, 128), F32)],
        name="final",
    )
    return grad, loss.reshape(())


def solution(mesh):
    fine = Mesh(mesh.devices.reshape(NZ, NYL, NC, NYH, NX), AXES)
    dp, tensor = ("z", "yl", "core"), ("yh", "x")
    in_specs = (P(AXES, None), P(), P(dp, tensor), P(dp, tensor), P(None, tensor))
    out_specs = (P(dp, tensor), P())
    return jax.shard_map(shards, mesh=fine, in_specs=in_specs, out_specs=out_specs, check_vma=False)
```

```python
import jax
import jax.numpy as jnp
from jax import lax
from jax.experimental import pallas as pl
from jax.experimental.pallas import tpu as pltpu
from jax.sharding import Mesh, PartitionSpec as P

F32 = jnp.float32
BF16 = jnp.bfloat16
NZ, NYL, NC, NYH, NX = 16, 2, 2, 2, 4
AXES = ("z", "yl", "core", "yh", "x")
Y = ("yl", "yh")
ZCX = ("z", "core", "x")
D, KVW, TOKENS = 8192, 512, 65536
SHIFT = 34
VMEM = pl.BlockSpec(memory_space=pltpu.VMEM)
SMEM = pl.BlockSpec(memory_space=pltpu.SMEM)
BACK = (0, 3, 2, 1)


def call(kernel, out_shape, *args, scratch=(), flops=0, name=None):
    size = sum(a.size * a.dtype.itemsize for a in args)
    for o in jax.tree.leaves(out_shape):
        size += o.size * o.dtype.itemsize
    return pl.pallas_call(
        kernel,
        out_shape=out_shape,
        in_specs=[SMEM if a.shape == (3,) else VMEM for a in args],
        out_specs=jax.tree.map(lambda _: VMEM, out_shape),
        scratch_shapes=list(scratch),
        name=name,
        cost_estimate=pl.CostEstimate(flops=flops, bytes_accessed=size, transcendentals=0),
        compiler_params=pltpu.CompilerParams(vmem_limit_bytes=24 * 1024 * 1024),
    )(*args)


def shape(dims, dtype):
    return jax.ShapeDtypeStruct(dims, dtype)


def lane_group(dims):
    return lax.broadcasted_iota(jnp.int32, dims, len(dims) - 1) // 32


def swap_groups(parts, place):
    total = None
    for b, part in enumerate(parts):
        shift = (b - place) * 32 % 128
        moved = pltpu.roll(part, shift, part.ndim - 1) if shift else part
        here = jnp.where(lane_group(part.shape) == b, moved, 0.0)
        total = here if total is None else total + here
    return total


def kept_rows(pat):
    first = jnp.where(pat > 2.5, 1.0, 0.0) + jnp.where(pat > 4.5, 1.0, 0.0)
    second = jnp.where(pat < 2.5, pat + 1.0, jnp.where(pat < 3.5, 2.0, 3.0))
    return first, second


def per_row(patterns):
    row = lax.broadcasted_iota(jnp.int32, (32, 128), 0)
    col = lax.broadcasted_iota(jnp.int32, (32, 128), 1)
    spread = jnp.where(col // 4 == row, 1.0, 0.0).astype(BF16)
    pat = jnp.dot(patterns.astype(F32).astype(BF16), spread, preferred_element_type=F32)
    first, second = kept_rows(pat)
    spot = (lax.broadcasted_iota(jnp.int32, pat.shape, 1) % 4).astype(F32)
    return first, second, spot


def shuffled(place):
    return place % 4 * 8 + place // 4


def norm_kernel(x_ref, gain_ref, pat_ref, at_ref, *rest):
    outs, rows_ref, pick_ref = rest[:NX], rest[NX], rest[NX + 1]
    me, core, own_yl = at_ref[0], at_ref[1], at_ref[2]
    total = jnp.zeros((128, 512), F32)
    for g in range(16):
        part = x_ref[:, g * 512 : (g + 1) * 512].astype(F32)
        total += part * part
    factor = lax.rsqrt(jnp.sum(total, axis=1, keepdims=True) / D + 1e-05)
    for yl in range(2):
        for m in range(8):
            for half in range(2):
                at = (8 * m + 4 * half + 2 * yl) * 128
                part = x_ref[:, at : at + 256].astype(F32)
                gain = gain_ref[:, at : at + 256].astype(F32)
                tile = yl * 8 + m
                rows_ref[tile * 128 : (tile + 1) * 128, half * 256 : (half + 1) * 256] = (
                    part * factor * gain
                ).astype(BF16)
    src = lax.broadcasted_iota(jnp.int32, (512, 512), 0)
    dst = lax.broadcasted_iota(jnp.int32, (512, 512), 1)
    ahead = (src // 32 + NX - me) % NX
    goal = ahead * 128 + src // 128 * 32 + shuffled(src % 32)
    move = jnp.where(goal == dst, 1.0, 0.0).astype(BF16)
    for tile in range(16):
        seg = jnp.dot(
            rows_ref[tile * 128 : (tile + 1) * 128, :], move, preferred_element_type=F32
        ).astype(BF16)
        for x in range(NX):
            outs[x][:128, tile * 128 : (tile + 1) * 128] = seg[:, x * 128 : (x + 1) * 128]
    col = lax.broadcasted_iota(jnp.int32, (64, 128), 0)
    lane = lax.broadcasted_iota(jnp.int32, (64, 128), 1)
    pick = jnp.where((col - core * 32 == lane - me * 32) & (lane // 32 == me), 1.0, 0.0)
    chosen = lax.dot_general(
        pat_ref[...].astype(F32).astype(BF16),
        pick.astype(BF16),
        (((0,), (0,)), ((), ())),
        preferred_element_type=F32,
    )
    pick_ref[...] = chosen.reshape(NZ, NYL, NC, NX, 8, 128)
    for x in range(NX):
        rows = pick_ref[:, own_yl, :, (me + x) % NX].reshape(256, 128).astype(BF16)
        for tile in range(16):
            outs[x][128:, tile * 128 : (tile + 1) * 128] = rows[tile * 16 : (tile + 1) * 16]


def pack_kernel(teacher_ref, student_ref, pat_ref, out_ref):
    first, second, spot = per_row(pat_ref[...])
    keep = jnp.where((spot == first) | (spot == second), 1.0, 0.0)
    delta = student_ref[...].astype(F32) * keep - teacher_ref[...].astype(F32)
    delta = delta * 2.0**SHIFT
    delta = ((delta * jnp.abs(delta)) * (delta * delta)).astype(BF16)
    row = lax.broadcasted_iota(jnp.int32, (64, 128), 0)
    col = lax.broadcasted_iota(jnp.int32, (64, 128), 1)
    widen = jnp.where(row == col, 1.0, 0.0).astype(BF16)
    rows = lax.dot_general(
        delta, widen, (((0,), (0,)), ((), ())), preferred_element_type=F32
    ).astype(BF16)
    dst = lax.broadcasted_iota(jnp.int32, (128, 128), 0)
    src = lax.broadcasted_iota(jnp.int32, (128, 128), 1)
    move = jnp.where(src // 32 * 32 + shuffled(src % 32) == dst, 1.0, 0.0).astype(BF16)
    wide = jnp.dot(move, rows, preferred_element_type=F32).reshape(4, 4, 8, 128)
    for c in range(NC):
        piece = swap_groups([wide[:, q] for q in range(4)], c).reshape(32, 128).astype(BF16)
        for z in range(NZ):
            out_ref[z, c * 32 : (c + 1) * 32, :] = piece


def spread_kernel(got_ref, out_ref, mid_ref):
    got = got_ref[...].astype(F32).reshape(32, 4, 8, 128)
    for q in range(4):
        mid_ref[:, q] = swap_groups([got[:, x] for x in range(NX)], q)
    rows = mid_ref[...].reshape(1024, 128).astype(BF16)
    for y in range(4):
        out_ref[y] = rows


def forward_kernel(*refs):
    pieces, (w_ref, me_ref, out_ref, high_ref, low_ref) = refs[: 2 * NX], refs[2 * NX :]
    for y in range(4):
        for k in range(4):
            sent = w_ref[y, k * 256 : (k + 1) * 256, :].astype(F32)
            size = jnp.sqrt(jnp.sqrt(jnp.abs(sent))) * 2.0**-SHIFT
            delta = jnp.where(sent < 0, -size, size)
            high = delta.astype(BF16)
            at = (y // 2) * 1024 + k * 256
            lane = (y % 2) * 128
            high_ref[at : at + 256, lane : lane + 128] = high
            low_ref[at : at + 256, lane : lane + 128] = (delta - high.astype(F32)).astype(BF16)
    for i in range(NX):
        x = (me_ref[0] + BACK[i]) % NX
        for ref, row in ((pieces[i], 0), (pieces[NX + i], 128)):
            part = jnp.dot(ref[:128, :], high_ref[...], preferred_element_type=F32)
            part += jnp.dot(ref[:128, :], low_ref[...], preferred_element_type=F32)
            out_ref[x, row : row + 128] = part.astype(BF16)


def thirds(value, rows):
    high = value.astype(BF16).astype(F32)
    mid = (value - high).astype(BF16).astype(F32)
    low = value - high - mid
    row = lax.broadcasted_iota(jnp.int32, (rows, value.shape[1]), 0)
    return jnp.where(row == 0, high, jnp.where(row == 1, mid, jnp.where(row == 2, low, 0.0)))


def slope_kernel(part_ref, out_ref, loss_ref):
    diff = part_ref[0].astype(F32)
    for x in range(1, NX):
        diff = diff + part_ref[x].astype(F32)
    slope = diff.astype(BF16)
    for x in range(NX):
        out_ref[x] = slope
    square = diff * diff
    loss_ref[...] = jnp.sum(square[:, :128] + square[:, 128:], axis=0, keepdims=True)


def grad_kernel(*refs):
    pieces, (slope_ref, loss_ref, me_ref, out_ref, pat_ref, s_ref) = refs[: 2 * NX], refs[2 * NX :]
    contract = (((0,), (0,)), ((), ()))
    for i in range(NX):
        x = (me_ref[0] + BACK[i]) % NX
        s_ref[i * 128 : (i + 1) * 128] = slope_ref[x, :128]
        s_ref[512 + i * 128 : 512 + (i + 1) * 128] = slope_ref[x, 128:]
    for k in range(8):
        at = k * 256
        rows = jnp.concatenate([p[:128, at : at + 256] for p in pieces], axis=0)
        term = lax.dot_general(rows, s_ref[...], contract, preferred_element_type=F32)
        term = term.astype(BF16)
        for yh in range(2):
            out_ref[(k // 4) * 2 + yh, (k % 4) * 256 : (k % 4 + 1) * 256, :] = term[
                :, yh * 128 : (yh + 1) * 128
            ]
    loss = thirds(loss_ref[...], 16).astype(BF16)
    for y in range(4):
        out_ref[y, 1024:, :] = loss
    for tile in range(16):
        pat = pieces[0][128:, tile * 128 : (tile + 1) * 128].astype(F32)
        for i in range(1, NX):
            pat += pieces[i][128:, tile * 128 : (tile + 1) * 128].astype(F32)
        pat_ref[tile * 16 : (tile + 1) * 16, :] = pat.astype(BF16)


def gather_kernel(got_ref, pat_ref, out_ref, mid_ref):
    total = got_ref[0].astype(F32)
    for y in range(1, 4):
        total = total + got_ref[y].astype(F32)
    loss = jnp.sum(total[1024:], axis=0, keepdims=True)
    loss = thirds(jnp.broadcast_to(jnp.sum(loss, axis=1, keepdims=True), (1, 128)), 8)
    row = lax.broadcasted_iota(jnp.int32, (8, 128), 0)
    lane = lax.broadcasted_iota(jnp.int32, (8, 128), 1)
    loss = jnp.where(lane == 64 + row, loss, 0.0)
    total = total[:1024].reshape(32, 4, 8, 128)
    first, second = kept_rows(pat_ref[...].astype(F32).reshape(32, 8, 128))
    kept = [jnp.zeros_like(first), jnp.zeros_like(first)]
    for k in range(4):
        for i, which in enumerate((first, second)):
            kept[i] += jnp.where(which == k, total[:, k], 0.0)
    group = lane_group((32, 8, 128))
    for x in range(NX):
        one = pltpu.roll(kept[0], (4 - x) % 4 * 32, 2)
        two = pltpu.roll(kept[1], (5 - x) % 4 * 32, 2)
        mid_ref[:, x] = jnp.where(group == 0, one, jnp.where(group == 1, two, loss[None]))
    out_ref[...] = mid_ref[...].reshape(1024, 128).astype(BF16)


def final_kernel(got_ref, pat_ref, out_ref, loss_ref):
    total = got_ref[0].astype(F32)
    for z in range(1, NZ):
        total = total + got_ref[z].astype(F32)
    loss = jnp.where(lane_group(total.shape) == 2, total, 0.0)
    loss = jnp.sum(jnp.sum(loss, axis=0, keepdims=True), axis=1, keepdims=True)
    loss_ref[...] = loss / (TOKENS * KVW)
    one, two = total[:32], total[32:]
    group = lane_group((32, 128))
    near = jnp.where(group == 0, one, pltpu.roll(two, 32, 1))
    far = jnp.where(group == 2, pltpu.roll(one, 32, 1), pltpu.roll(two, 64, 1))
    kept = jnp.where(group < 2, near, far)
    row = lax.broadcasted_iota(jnp.int32, (32, 128), 0)
    col = lax.broadcasted_iota(jnp.int32, (32, 128), 1)
    spread = jnp.where(col // 4 == row, 1.0, 0.0).astype(BF16)
    wide = jnp.zeros((128, 128), F32)
    for _ in range(3):
        part = kept.astype(BF16)
        kept = kept - part.astype(F32)
        wide += lax.dot_general(
            part, spread, (((0,), (0,)), ((), ())), preferred_element_type=F32
        )
    first, second, spot = per_row(pat_ref[...])
    grad = jnp.where(spot == first, wide[:64], 0.0) + jnp.where(spot == second, wide[64:], 0.0)
    out_ref[...] = grad / jnp.sqrt(F32(TOKENS))


def ring(step):
    return [(i, (i + step) % NX) for i in range(NX)]


def shards(hidden, norm_gain, teacher_k, student_k, keep_pattern):
    z, yl, core, x = (lax.axis_index(a) for a in ("z", "yl", "core", "x"))
    place = (z * NYL + yl) * NC + core
    at = jnp.stack([x, core, yl]).astype(jnp.int32)
    patterns = keep_pattern.T
    pat = lax.dynamic_slice_in_dim(patterns, place * 32, 32, 1)

    packed = call(
        pack_kernel, shape((NZ, 64, 128), BF16), teacher_k.T, student_k.T, pat, name="pack"
    )
    got_w = lax.all_to_all(packed.reshape(128, 8, 128), ZCX, 0, 0, tiled=True)

    split = call(
        norm_kernel,
        (shape((144, 2048), BF16),) * NX,
        hidden,
        norm_gain.reshape(1, D),
        patterns,
        at,
        scratch=[pltpu.VMEM((2048, 512), BF16), pltpu.VMEM((NZ, NYL, NC, NX, 8, 128), F32)],
        flops=2 * 2048 * 512 * 512,
        name="norm",
    )
    own = [split[0]] + [lax.ppermute(split[i], "x", ring(i)) for i in range(1, NX)]
    pair = [lax.ppermute(piece, "core", [(0, 1), (1, 0)]) for piece in own]

    rows_w = call(
        spread_kernel,
        shape((4, 1024, 128), BF16),
        got_w.reshape(1024, 128),
        scratch=[pltpu.VMEM((32, 4, 8, 128), F32)],
        name="spread",
    )
    all_w = lax.all_to_all(rows_w, Y, 0, 0, tiled=True)

    flops = 2 * 1024 * 2048 * 256
    part = call(
        forward_kernel,
        shape((NX, 256, 256), BF16),
        *own,
        *pair,
        all_w,
        at,
        scratch=[pltpu.VMEM((2048, 256), BF16)] * 2,
        flops=2 * flops,
        name="forward",
    )
    got_part = lax.all_to_all(part, "x", 0, 0, tiled=True)
    slope, loss_part = call(
        slope_kernel, (shape((NX, 256, 256), BF16), shape((1, 128), F32)), got_part, name="slope"
    )
    slopes = lax.all_to_all(slope, "x", 0, 0, tiled=True)
    term, pat_x = call(
        grad_kernel,
        (shape((4, 1040, 128), BF16), shape((256, 128), BF16)),
        *own,
        *pair,
        slopes,
        loss_part,
        at,
        scratch=[pltpu.VMEM((1024, 256), BF16)],
        flops=flops,
        name="grad",
    )
    got_term = lax.all_to_all(term, Y, 0, 0, tiled=True)
    packed_term = call(
        gather_kernel,
        shape((1024, 128), BF16),
        got_term,
        pat_x,
        scratch=[pltpu.VMEM((32, 4, 8, 128), F32)],
        name="gather",
    )
    got_sum = lax.all_to_all(packed_term.reshape(128, 8, 128), ZCX, 0, 0, tiled=True)
    grad, loss = call(
        final_kernel,
        (shape((64, 128), F32), shape((1, 1), F32)),
        got_sum.reshape(NZ, 64, 128),
        pat,
        name="final",
    )
    return grad.T, loss.reshape(())


def solution(mesh):
    fine = Mesh(mesh.devices.reshape(NZ, NYL, NC, NYH, NX), AXES)
    dp, tensor = ("z", "yl", "core"), ("yh", "x")
    in_specs = (P(AXES, None), P(), P(dp, tensor), P(dp, tensor), P(None, tensor))
    out_specs = (P(dp, tensor), P())
    return jax.shard_map(shards, mesh=fine, in_specs=in_specs, out_specs=out_specs, check_vma=False)
```

```python
import jax
import jax.numpy as jnp
from jax import lax
from jax.experimental import pallas as pl
from jax.experimental.pallas import tpu as pltpu
from jax.sharding import Mesh, PartitionSpec as P

F32 = jnp.float32
BF16 = jnp.bfloat16
NZ, NYL, NC, NYH, NX = 16, 2, 2, 2, 4
AXES = ("z", "yl", "core", "yh", "x")
Y = ("yl", "yh")
ZCX = ("z", "core", "x")
D, KVW, TOKENS = 8192, 512, 65536
SHIFT = 34
VMEM = pl.BlockSpec(memory_space=pltpu.VMEM)
SMEM = pl.BlockSpec(memory_space=pltpu.SMEM)
STEP = (0, 2, 1, 3)
BACK = (0, 2, 3, 1)


def call(kernel, out_shape, *args, scratch=(), flops=0, name=None, far=(), space=pltpu.HBM, held=True, grant=24):
    size = sum(a.size * a.dtype.itemsize for a in args)
    for o in jax.tree.leaves(out_shape):
        size += o.size * o.dtype.itemsize
    specs = [SMEM if a.shape == (4,) else VMEM for a in args]
    for i in far:
        specs[i] = pl.BlockSpec(memory_space=space)
    return pl.pallas_call(
        kernel,
        out_shape=jax.tree.map(lambda o: pltpu.VMEM(o.shape, o.dtype), out_shape) if held else out_shape,
        in_specs=specs,
        out_specs=jax.tree.map(lambda _: VMEM, out_shape),
        scratch_shapes=list(scratch),
        name=name,
        cost_estimate=pl.CostEstimate(flops=flops, bytes_accessed=size, transcendentals=0),
        compiler_params=pltpu.CompilerParams(vmem_limit_bytes=grant * 1024 * 1024),
    )(*args)


def shape(dims, dtype):
    return jax.ShapeDtypeStruct(dims, dtype)


def lane_group(dims):
    return lax.broadcasted_iota(jnp.int32, dims, len(dims) - 1) // 32


def swap_groups(parts, place):
    total = None
    for b, part in enumerate(parts):
        shift = (b - place) * 32 % 128
        moved = pltpu.roll(part, shift, part.ndim - 1) if shift else part
        here = jnp.where(lane_group(part.shape) == b, moved, 0.0)
        total = here if total is None else total + here
    return total


def kept_rows(pat):
    first = jnp.where(pat > 2.5, 1.0, 0.0) + jnp.where(pat > 4.5, 1.0, 0.0)
    second = jnp.where(pat < 2.5, pat + 1.0, jnp.where(pat < 3.5, 2.0, 3.0))
    return first, second


def row_of_four(dims):
    return (lax.broadcasted_iota(jnp.int32, dims, 1) % 4).astype(F32)


def shuffled(place):
    return place % 4 * 8 + place // 4


def norm_kernel(x_hbm, gain_ref, pat_hbm, at_ref, *rest):
    outs, (rows_ref, pick_ref, x_ref, pat_ref, sems) = rest[:NX], rest[NX:]
    me, core, own_yl = at_ref[0], at_ref[1], at_ref[2]
    cuts = [pl.ds(i * 2048, 2048) for i in range(4)]
    loads = [
        pltpu.make_async_copy(x_hbm.at[:, cut], x_ref.at[:, cut], sems.at[i])
        for i, cut in enumerate(cuts)
    ]
    loads.append(pltpu.make_async_copy(pat_hbm, pat_ref, sems.at[4]))
    for load in loads:
        load.start()
    total = jnp.zeros((128, 512), F32)
    for g in range(16):
        if g % 4 == 0:
            loads[g // 4].wait()
        part = x_ref[:, g * 512 : (g + 1) * 512].astype(F32)
        total += part * part
    factor = lax.rsqrt(jnp.sum(total, axis=1, keepdims=True) / D + 1e-05)
    gain = gain_ref[...].astype(F32)
    for yl in range(2):
        for m in range(8):
            tile = yl * 8 + m
            for b in range(4):
                block = 8 * m + 4 * (b // 2) + 2 * yl + b % 2
                part = x_ref[:, block * 128 : (block + 1) * 128].astype(F32)
                rows_ref[tile * 128 : (tile + 1) * 128, b * 128 : (b + 1) * 128] = (
                    part * factor * gain[block : block + 1, :]
                ).astype(BF16)
    src = lax.broadcasted_iota(jnp.int32, (512, 512), 0)
    dst = lax.broadcasted_iota(jnp.int32, (512, 512), 1)
    ahead = (src // 32 + NX - me) % NX
    goal = ahead * 128 + src // 128 * 32 + shuffled(src % 32)
    move = jnp.where(goal == dst, 1.0, 0.0).astype(BF16)
    for tile in range(16):
        seg = jnp.dot(
            rows_ref[tile * 128 : (tile + 1) * 128, :], move, preferred_element_type=F32
        ).astype(BF16)
        for i, x in enumerate(STEP):
            outs[i][:128, tile * 128 : (tile + 1) * 128] = seg[:, x * 128 : (x + 1) * 128]
    col = lax.broadcasted_iota(jnp.int32, (64, 128), 0)
    lane = lax.broadcasted_iota(jnp.int32, (64, 128), 1)
    loads[4].wait()
    pick = jnp.where((col - core * 32 == lane - me * 32) & (lane // 32 == me), 1.0, 0.0)
    chosen = lax.dot_general(
        pat_ref[...].astype(F32).astype(BF16),
        pick.astype(BF16),
        (((0,), (0,)), ((), ())),
        preferred_element_type=F32,
    )
    pick_ref[...] = chosen.reshape(NZ, NYL, NC, NX, 8, 128)
    for i, x in enumerate(STEP):
        rows = pick_ref[:, own_yl, :, (me + x) % NX].reshape(256, 128).astype(BF16)
        for tile in range(16):
            outs[i][128:, tile * 128 : (tile + 1) * 128] = rows[tile * 16 : (tile + 1) * 16]


def pack_kernel(teacher_hbm, student_hbm, pat_hbm, at_ref, out_ref, rows_ref, *scratch):
    teacher_ref, student_ref, pat_ref, sems = scratch
    place = at_ref[3]
    window = pl.ds(pl.multiple_of(place // 4 * 128, 128), 128)
    loads = [
        pltpu.make_async_copy(pat_hbm.at[:, window], pat_ref, sems.at[0]),
        pltpu.make_async_copy(teacher_hbm, teacher_ref, sems.at[1]),
        pltpu.make_async_copy(student_hbm, student_ref, sems.at[2]),
    ]
    for load in loads:
        load.start()
    for load in loads:
        load.wait()
    row = lax.broadcasted_iota(jnp.int32, (128, 128), 0)
    col = lax.broadcasted_iota(jnp.int32, (128, 128), 1)
    spread = jnp.where(col // 4 + place % 4 * 32 == row, 1.0, 0.0).astype(BF16)
    pat = jnp.dot(pat_ref[...].astype(F32).astype(BF16), spread, preferred_element_type=F32)
    rows_ref[...] = pat
    first, second = kept_rows(pat)
    spot = row_of_four(pat.shape)
    keep = jnp.where((spot == first) | (spot == second), 1.0, 0.0)
    delta = student_ref[...].astype(F32) * keep - teacher_ref[...].astype(F32)
    delta = delta * 2.0**SHIFT
    delta = ((delta * jnp.abs(delta)) * (delta * delta)).astype(BF16)
    row = lax.broadcasted_iota(jnp.int32, (64, 128), 0)
    col = lax.broadcasted_iota(jnp.int32, (64, 128), 1)
    widen = jnp.where(row == col, 1.0, 0.0).astype(BF16)
    rows = lax.dot_general(
        delta, widen, (((0,), (0,)), ((), ())), preferred_element_type=F32
    ).astype(BF16)
    dst = lax.broadcasted_iota(jnp.int32, (128, 128), 0)
    src = lax.broadcasted_iota(jnp.int32, (128, 128), 1)
    move = jnp.where(src // 32 * 32 + shuffled(src % 32) == dst, 1.0, 0.0).astype(BF16)
    wide = jnp.dot(move, rows, preferred_element_type=F32).reshape(4, 4, 8, 128)
    for c in range(NC):
        piece = swap_groups([wide[:, q] for q in range(4)], c).reshape(32, 128).astype(BF16)
        for z in range(NZ):
            out_ref[z, c * 32 : (c + 1) * 32, :] = piece


def spread_kernel(got_ref, out_ref, mid_ref):
    got = got_ref[...].astype(F32).reshape(32, 4, 8, 128)
    for q in range(4):
        mid_ref[:, q] = swap_groups([got[:, x] for x in range(NX)], q)
    rows = mid_ref[...].reshape(1024, 128).astype(BF16)
    for y in range(4):
        out_ref[y] = rows


def forward_kernel(*refs):
    pieces, (w_ref, me_ref, out_ref, high_ref, low_ref, held_ref, sems) = refs[: 2 * NX], refs[2 * NX :]
    loads = [
        pltpu.make_async_copy(p.at[pl.ds(0, 128)], held_ref.at[i], sems.at[i])
        for i, p in enumerate(pieces)
    ]
    for load in loads:
        load.start()
    for y in range(4):
        for k in range(4):
            sent = w_ref[y, k * 256 : (k + 1) * 256, :].astype(F32)
            size = jnp.sqrt(jnp.sqrt(jnp.abs(sent))) * 2.0**-SHIFT
            delta = jnp.where(sent < 0, -size, size)
            high = delta.astype(BF16)
            at = (y // 2) * 1024 + k * 256
            lane = (y % 2) * 128
            high_ref[at : at + 256, lane : lane + 128] = high
            low_ref[at : at + 256, lane : lane + 128] = (delta - high.astype(F32)).astype(BF16)
    for i in range(NX):
        x = (me_ref[0] + BACK[i]) % NX
        for piece, row in ((i, 0), (NX + i, 128)):
            loads[piece].wait()
            part = jnp.dot(held_ref[piece], high_ref[...], preferred_element_type=F32)
            part += jnp.dot(held_ref[piece], low_ref[...], preferred_element_type=F32)
            out_ref[x, row : row + 128] = part.astype(BF16)


def thirds(value, rows):
    high = value.astype(BF16).astype(F32)
    mid = (value - high).astype(BF16).astype(F32)
    low = value - high - mid
    row = lax.broadcasted_iota(jnp.int32, (rows, value.shape[1]), 0)
    return jnp.where(row == 0, high, jnp.where(row == 1, mid, jnp.where(row == 2, low, 0.0)))


def slope_kernel(part_ref, out_ref, loss_ref):
    diff = part_ref[0].astype(F32)
    for x in range(1, NX):
        diff = diff + part_ref[x].astype(F32)
    slope = diff.astype(BF16)
    for x in range(NX):
        out_ref[x] = slope
    square = diff * diff
    loss_ref[...] = jnp.sum(square[:, :128] + square[:, 128:], axis=0, keepdims=True)


def grad_kernel(*refs):
    pieces, (slope_ref, loss_ref, me_ref, out_ref, pat_ref, s_ref) = refs[: 2 * NX], refs[2 * NX :]
    contract = (((0,), (0,)), ((), ()))
    for i in range(NX):
        x = (me_ref[0] + BACK[i]) % NX
        s_ref[i * 128 : (i + 1) * 128] = slope_ref[x, :128]
        s_ref[512 + i * 128 : 512 + (i + 1) * 128] = slope_ref[x, 128:]
    for k in range(8):
        at = k * 256
        rows = jnp.concatenate([p[:128, at : at + 256] for p in pieces], axis=0)
        term = lax.dot_general(rows, s_ref[...], contract, preferred_element_type=F32)
        term = term.astype(BF16)
        for yh in range(2):
            out_ref[(k // 4) * 2 + yh, (k % 4) * 256 : (k % 4 + 1) * 256, :] = term[
                :, yh * 128 : (yh + 1) * 128
            ]
    loss = thirds(loss_ref[...], 16).astype(BF16)
    for y in range(4):
        out_ref[y, 1024:, :] = loss
    for tile in range(16):
        pat = pieces[0][128:, tile * 128 : (tile + 1) * 128].astype(F32)
        for i in range(1, NX):
            pat += pieces[i][128:, tile * 128 : (tile + 1) * 128].astype(F32)
        pat_ref[tile * 16 : (tile + 1) * 16, :] = pat.astype(BF16)


def gather_kernel(got_ref, pat_ref, out_ref, mid_ref):
    total = got_ref[0].astype(F32)
    for y in range(1, 4):
        total = total + got_ref[y].astype(F32)
    loss = jnp.sum(total[1024:], axis=0, keepdims=True)
    loss = thirds(jnp.broadcast_to(jnp.sum(loss, axis=1, keepdims=True), (1, 128)), 8)
    row = lax.broadcasted_iota(jnp.int32, (8, 128), 0)
    lane = lax.broadcasted_iota(jnp.int32, (8, 128), 1)
    loss = jnp.where(lane == 64 + row, loss, 0.0)
    total = total[:1024].reshape(32, 4, 8, 128)
    first, second = kept_rows(pat_ref[...].astype(F32).reshape(32, 8, 128))
    kept = [jnp.zeros_like(first), jnp.zeros_like(first)]
    for k in range(4):
        for i, which in enumerate((first, second)):
            kept[i] += jnp.where(which == k, total[:, k], 0.0)
    group = lane_group((32, 8, 128))
    for x in range(NX):
        one = pltpu.roll(kept[0], (4 - x) % 4 * 32, 2)
        two = pltpu.roll(kept[1], (5 - x) % 4 * 32, 2)
        mid_ref[:, x] = jnp.where(group == 0, one, jnp.where(group == 1, two, loss[None]))
    out_ref[...] = mid_ref[...].reshape(1024, 128).astype(BF16)


def final_kernel(got_ref, pat_ref, out_ref, loss_ref):
    total = got_ref[0].astype(F32)
    for z in range(1, NZ):
        total = total + got_ref[z].astype(F32)
    loss = jnp.where(lane_group(total.shape) == 2, total, 0.0)
    loss = jnp.sum(jnp.sum(loss, axis=0, keepdims=True), axis=1, keepdims=True)
    loss_ref[...] = loss / (TOKENS * KVW)
    one, two = total[:32], total[32:]
    group = lane_group((32, 128))
    near = jnp.where(group == 0, one, pltpu.roll(two, 32, 1))
    far = jnp.where(group == 2, pltpu.roll(one, 32, 1), pltpu.roll(two, 64, 1))
    kept = jnp.where(group < 2, near, far)
    row = lax.broadcasted_iota(jnp.int32, (32, 128), 0)
    col = lax.broadcasted_iota(jnp.int32, (32, 128), 1)
    spread = jnp.where(col // 4 == row, 1.0, 0.0).astype(BF16)
    wide = jnp.zeros((128, 128), F32)
    for _ in range(3):
        part = kept.astype(BF16)
        kept = kept - part.astype(F32)
        wide += lax.dot_general(
            part, spread, (((0,), (0,)), ((), ())), preferred_element_type=F32
        )
    first, second = kept_rows(pat_ref[...])
    spot = row_of_four(wide[:64].shape)
    grad = jnp.where(spot == first, wide[:64], 0.0) + jnp.where(spot == second, wide[64:], 0.0)
    out_ref[...] = grad / jnp.sqrt(F32(TOKENS))


def ring(step):
    return [(i, (i + step) % NX) for i in range(NX)]


def shards(hidden, norm_gain, teacher_k, student_k, keep_pattern):
    z, yl, core, x = (lax.axis_index(a) for a in ("z", "yl", "core", "x"))
    place = (z * NYL + yl) * NC + core
    at = jnp.stack([x, core, yl, place]).astype(jnp.int32)
    patterns = keep_pattern.T

    packed, pat = call(
        pack_kernel,
        (shape((NZ, 64, 128), BF16), shape((64, 128), F32)),
        teacher_k.T,
        student_k.T,
        patterns,
        at,
        scratch=[
            pltpu.VMEM((64, 128), BF16),
            pltpu.VMEM((64, 128), BF16),
            pltpu.VMEM((64, 128), jnp.int32),
            pltpu.SemaphoreType.DMA((3,)),
        ],
        far=(0, 1, 2),
        grant=60,
        name="pack",
    )
    got_w = lax.all_to_all(packed.reshape(128, 8, 128), ZCX, 0, 0, tiled=True)

    split = call(
        norm_kernel,
        (shape((144, 2048), BF16),) * NX,
        hidden,
        norm_gain.reshape(64, 128),
        patterns,
        at,
        scratch=[
            pltpu.VMEM((2048, 512), BF16),
            pltpu.VMEM((NZ, NYL, NC, NX, 8, 128), F32),
            pltpu.VMEM((128, D), BF16),
            pltpu.VMEM((64, 2048), jnp.int32),
            pltpu.SemaphoreType.DMA((5,)),
        ],
        far=(0, 2),
        grant=60,
        flops=2 * 2048 * 512 * 512,
        name="norm",
    )
    own = [split[0]] + [lax.ppermute(split[i], "x", ring(STEP[i])) for i in range(1, NX)]
    pair = [lax.ppermute(piece, "core", [(0, 1), (1, 0)]) for piece in own]

    rows_w = call(
        spread_kernel,
        shape((4, 1024, 128), BF16),
        got_w.reshape(1024, 128),
        scratch=[pltpu.VMEM((32, 4, 8, 128), F32)],
        name="spread",
    )
    all_w = lax.all_to_all(rows_w, Y, 0, 0, tiled=True)

    flops = 2 * 1024 * 2048 * 256
    part = call(
        forward_kernel,
        shape((NX, 256, 256), BF16),
        *own,
        *pair,
        all_w,
        at,
        scratch=[
            pltpu.VMEM((2048, 256), BF16),
            pltpu.VMEM((2048, 256), BF16),
            pltpu.VMEM((2 * NX, 128, 2048), BF16),
            pltpu.SemaphoreType.DMA((2 * NX,)),
        ],
        far=range(2 * NX),
        grant=60,
        space=pl.ANY,
        flops=2 * flops,
        name="forward",
    )
    got_part = lax.all_to_all(part, "x", 0, 0, tiled=True)
    slope, loss_part = call(
        slope_kernel, (shape((NX, 256, 256), BF16), shape((1, 128), F32)), got_part, name="slope"
    )
    slopes = lax.all_to_all(slope, "x", 0, 0, tiled=True)
    term, pat_x = call(
        grad_kernel,
        (shape((4, 1040, 128), BF16), shape((256, 128), BF16)),
        *own,
        *pair,
        slopes,
        loss_part,
        at,
        scratch=[pltpu.VMEM((1024, 256), BF16)],
        flops=flops,
        name="grad",
    )
    got_term = lax.all_to_all(term, Y, 0, 0, tiled=True)
    packed_term = call(
        gather_kernel,
        shape((1024, 128), BF16),
        got_term,
        pat_x,
        scratch=[pltpu.VMEM((32, 4, 8, 128), F32)],
        name="gather",
    )
    got_sum = lax.all_to_all(packed_term.reshape(128, 8, 128), ZCX, 0, 0, tiled=True)
    grad, loss = call(
        final_kernel,
        (shape((64, 128), F32), shape((1, 1), F32)),
        got_sum.reshape(NZ, 64, 128),
        pat,
        held=False,
        name="final",
    )
    return grad.T, loss.reshape(())


def solution(mesh):
    fine = Mesh(mesh.devices.reshape(NZ, NYL, NC, NYH, NX), AXES)
    dp, tensor = ("z", "yl", "core"), ("yh", "x")
    in_specs = (P(AXES, None), P(), P(dp, tensor), P(dp, tensor), P(None, tensor))
    out_specs = (P(dp, tensor), P())
    return jax.shard_map(shards, mesh=fine, in_specs=in_specs, out_specs=out_specs, check_vma=False)
```

```python
import jax
import jax.numpy as jnp
from jax import lax
from jax.experimental import pallas as pl
from jax.experimental.pallas import tpu as pltpu
from jax.sharding import Mesh, PartitionSpec as P

F32 = jnp.float32
BF16 = jnp.bfloat16
NZ, NYL, NC, NYH, NX = 16, 2, 2, 2, 4
AXES = ("z", "yl", "core", "yh", "x")
Y = ("yl", "yh")
ZCX = ("z", "core", "x")
D, KVW, TOKENS = 8192, 512, 65536
SHIFT = 34
VMEM = pl.BlockSpec(memory_space=pltpu.VMEM)
SMEM = pl.BlockSpec(memory_space=pltpu.SMEM)
STEP = (0, 2, 1, 3)
BACK = (0, 2, 3, 1)


def call(kernel, out_shape, *args, scratch=(), flops=0, name=None, far=(), grant=24):
    size = sum(a.size * a.dtype.itemsize for a in args)
    for o in jax.tree.leaves(out_shape):
        size += o.size * o.dtype.itemsize
    specs = [SMEM if a.shape == (5,) else VMEM for a in args]
    for i in far:
        specs[i] = pl.BlockSpec(memory_space=pl.ANY)
    return pl.pallas_call(
        kernel,
        out_shape=out_shape,
        in_specs=specs,
        out_specs=jax.tree.map(lambda _: VMEM, out_shape),
        scratch_shapes=list(scratch),
        name=name,
        cost_estimate=pl.CostEstimate(flops=flops, bytes_accessed=size, transcendentals=0),
        compiler_params=pltpu.CompilerParams(vmem_limit_bytes=grant * 1024 * 1024),
    )(*args)


def shape(dims, dtype):
    return jax.ShapeDtypeStruct(dims, dtype)


def lane_group(dims):
    return lax.broadcasted_iota(jnp.int32, dims, len(dims) - 1) // 32


def swap_groups(parts, place):
    total = None
    for b, part in enumerate(parts):
        shift = (b - place) * 32 % 128
        moved = pltpu.roll(part, shift, part.ndim - 1) if shift else part
        here = jnp.where(lane_group(part.shape) == b, moved, 0.0)
        total = here if total is None else total + here
    return total


def kept_rows(pat):
    first = jnp.where(pat > 2.5, 1.0, 0.0) + jnp.where(pat > 4.5, 1.0, 0.0)
    second = jnp.where(pat < 2.5, pat + 1.0, jnp.where(pat < 3.5, 2.0, 3.0))
    return first, second


def row_of_four(dims):
    return (lax.broadcasted_iota(jnp.int32, dims, 1) % 4).astype(F32)


def shuffled(place):
    return place % 4 * 8 + place // 4


def norm_kernel(x_hbm, gain_ref, at_ref, *rest):
    outs, (rows_ref, x_ref, sems) = rest[:NX], rest[NX:]
    me = at_ref[0]
    cuts = [pl.ds(i * 2048, 2048) for i in range(4)]
    loads = [
        pltpu.make_async_copy(x_hbm.at[:, cut], x_ref.at[:, cut], sems.at[i])
        for i, cut in enumerate(cuts)
    ]
    for load in loads:
        load.start()
    total = jnp.zeros((128, 512), F32)
    for g in range(16):
        if g % 4 == 0:
            loads[g // 4].wait()
        part = x_ref[:, g * 512 : (g + 1) * 512].astype(F32)
        total += part * part
    factor = lax.rsqrt(jnp.sum(total, axis=1, keepdims=True) / D + 1e-05)
    gain = gain_ref[...].astype(F32)
    for yl in range(2):
        for m in range(8):
            tile = yl * 8 + m
            for b in range(4):
                block = 8 * m + 4 * (b // 2) + 2 * yl + b % 2
                part = x_ref[:, block * 128 : (block + 1) * 128].astype(F32)
                rows_ref[tile * 128 : (tile + 1) * 128, b * 128 : (b + 1) * 128] = (
                    part * factor * gain[block : block + 1, :]
                ).astype(BF16)
    src = lax.broadcasted_iota(jnp.int32, (512, 512), 0)
    dst = lax.broadcasted_iota(jnp.int32, (512, 512), 1)
    ahead = (src // 32 + NX - me) % NX
    goal = ahead * 128 + src // 128 * 32 + shuffled(src % 32)
    move = jnp.where(goal == dst, 1.0, 0.0).astype(BF16)
    for tile in range(16):
        seg = jnp.dot(
            rows_ref[tile * 128 : (tile + 1) * 128, :], move, preferred_element_type=F32
        ).astype(BF16)
        for i, x in enumerate(STEP):
            outs[i][:, tile * 128 : (tile + 1) * 128] = seg[:, x * 128 : (x + 1) * 128]


def choose_kernel(pat_ref, at_ref, *outs):
    me, core, own_yl = at_ref[0], at_ref[1], at_ref[2]
    outs, pick_ref = outs[:NX], outs[NX]
    col = lax.broadcasted_iota(jnp.int32, (64, 128), 0)
    lane = lax.broadcasted_iota(jnp.int32, (64, 128), 1)
    pick = jnp.where((col - core * 32 == lane - me * 32) & (lane // 32 == me), 1.0, 0.0)
    chosen = lax.dot_general(
        pat_ref[...].astype(F32).astype(BF16),
        pick.astype(BF16),
        (((0,), (0,)), ((), ())),
        preferred_element_type=F32,
    )
    pick_ref[...] = chosen.reshape(NZ, NYL, NC, NX, 8, 128)
    for i, x in enumerate(STEP):
        outs[i][...] = pick_ref[:, own_yl, :, (me + x) % NX].reshape(256, 128).astype(BF16)


def join_kernel(*refs):
    total = refs[0][...].astype(F32)
    for ref in refs[1:NX]:
        total += ref[...].astype(F32)
    refs[NX][...] = total.astype(BF16)


def pack_kernel(teacher_hbm, student_hbm, pat_hbm, at_ref, out_ref, rows_ref, *scratch):
    teacher_ref, student_ref, pat_ref, sems = scratch
    place = at_ref[3]
    window = pl.ds(pl.multiple_of(place // 4 * 128, 128), 128)
    loads = [
        pltpu.make_async_copy(pat_hbm.at[:, window], pat_ref, sems.at[0]),
        pltpu.make_async_copy(teacher_hbm, teacher_ref, sems.at[1]),
        pltpu.make_async_copy(student_hbm, student_ref, sems.at[2]),
    ]
    for load in loads:
        load.start()
    for load in loads:
        load.wait()
    row = lax.broadcasted_iota(jnp.int32, (128, 128), 0)
    col = lax.broadcasted_iota(jnp.int32, (128, 128), 1)
    spread = jnp.where(col // 4 + place % 4 * 32 == row, 1.0, 0.0).astype(BF16)
    pat = jnp.dot(pat_ref[...].astype(F32).astype(BF16), spread, preferred_element_type=F32)
    rows_ref[...] = pat
    first, second = kept_rows(pat)
    spot = row_of_four(pat.shape)
    keep = jnp.where((spot == first) | (spot == second), 1.0, 0.0)
    delta = student_ref[...].astype(F32) * keep - teacher_ref[...].astype(F32)
    delta = delta * 2.0**SHIFT
    delta = ((delta * jnp.abs(delta)) * (delta * delta)).astype(BF16)
    row = lax.broadcasted_iota(jnp.int32, (64, 128), 0)
    col = lax.broadcasted_iota(jnp.int32, (64, 128), 1)
    widen = jnp.where(row == col, 1.0, 0.0).astype(BF16)
    rows = lax.dot_general(
        delta, widen, (((0,), (0,)), ((), ())), preferred_element_type=F32
    ).astype(BF16)
    dst = lax.broadcasted_iota(jnp.int32, (128, 128), 0)
    src = lax.broadcasted_iota(jnp.int32, (128, 128), 1)
    move = jnp.where(src // 32 * 32 + shuffled(src % 32) == dst, 1.0, 0.0).astype(BF16)
    wide = jnp.dot(move, rows, preferred_element_type=F32).reshape(4, 4, 8, 128)
    for c in range(NC):
        piece = swap_groups([wide[:, q] for q in range(4)], c).reshape(32, 128).astype(BF16)
        for z in range(NZ):
            out_ref[z, c * 32 : (c + 1) * 32, :] = piece


def spread_kernel(got_ref, out_ref, mid_ref):
    got = got_ref[...].astype(F32).reshape(32, 4, 8, 128)
    for q in range(4):
        mid_ref[:, q] = swap_groups([got[:, x] for x in range(NX)], q)
    rows = mid_ref[...].reshape(1024, 128).astype(BF16)
    for y in range(4):
        out_ref[y] = rows


def decode_kernel(w_ref, high_ref, low_ref):
    for y in range(4):
        for k in range(4):
            sent = w_ref[y, k * 256 : (k + 1) * 256, :].astype(F32)
            size = jnp.sqrt(jnp.sqrt(jnp.abs(sent))) * 2.0**-SHIFT
            delta = jnp.where(sent < 0, -size, size)
            high = delta.astype(BF16)
            at = (y // 2) * 1024 + k * 256
            lane = (y % 2) * 128
            high_ref[at : at + 256, lane : lane + 128] = high
            low_ref[at : at + 256, lane : lane + 128] = (delta - high.astype(F32)).astype(BF16)


def forward_kernel(*refs):
    pieces, (high_ref, low_ref, at_ref, out_ref) = refs[: 2 * NX], refs[2 * NX :]
    for i in range(NX):
        x = (at_ref[0] + BACK[i]) % NX
        for ref, row in ((pieces[i], 0), (pieces[NX + i], 128)):
            part = jnp.dot(ref[...], high_ref[...], preferred_element_type=F32)
            part += jnp.dot(ref[...], low_ref[...], preferred_element_type=F32)
            out_ref[x, row : row + 128] = part.astype(BF16)


def thirds(value, rows):
    high = value.astype(BF16).astype(F32)
    mid = (value - high).astype(BF16).astype(F32)
    low = value - high - mid
    row = lax.broadcasted_iota(jnp.int32, (rows, value.shape[1]), 0)
    return jnp.where(row == 0, high, jnp.where(row == 1, mid, jnp.where(row == 2, low, 0.0)))


def slope_kernel(part_ref, out_ref, loss_ref):
    diff = part_ref[0].astype(F32)
    for x in range(1, NX):
        diff = diff + part_ref[x].astype(F32)
    slope = diff.astype(BF16)
    for x in range(NX):
        out_ref[x] = slope
    square = diff * diff
    loss_ref[...] = jnp.sum(square[:, :128] + square[:, 128:], axis=0, keepdims=True)


def grad_kernel(*refs):
    pieces, pats, rest = refs[: 2 * NX], refs[2 * NX : 2 * NX + 4], refs[2 * NX + 4 :]
    slope_ref, loss_ref, at_ref, out_ref, s_ref, term_ref = rest
    contract = (((0,), (0,)), ((), ()))
    for i in range(NX):
        x = (at_ref[0] + BACK[i]) % NX
        s_ref[i * 128 : (i + 1) * 128] = slope_ref[x, :128]
        s_ref[512 + i * 128 : 512 + (i + 1) * 128] = slope_ref[x, 128:]
    for k in range(8):
        at = k * 256
        rows = jnp.concatenate([p[:, at : at + 256] for p in pieces], axis=0)
        term = lax.dot_general(rows, s_ref[...], contract, preferred_element_type=F32)
        for yh in range(2):
            term_ref[(k // 4) * 2 + yh, (k % 4) * 8 : (k % 4 + 1) * 8] = term[
                :, yh * 128 : (yh + 1) * 128
            ].reshape(8, 4, 8, 128)
    loss = thirds(loss_ref[...], 16).astype(BF16)
    for i in range(4):
        y = at_ref[4] ^ i
        first, second = kept_rows(pats[i][...].astype(F32).reshape(32, 8, 128))
        for row, which in ((0, first), (256, second)):
            kept = jnp.zeros_like(which)
            for k in range(4):
                kept += jnp.where(which == k, term_ref[y, :, k], 0.0)
            out_ref[y, row : row + 256] = kept.reshape(256, 128).astype(BF16)
        out_ref[y, 512:] = loss


def gather_kernel(got_ref, out_ref, mid_ref):
    total = got_ref[0].astype(F32)
    for y in range(1, 4):
        total = total + got_ref[y].astype(F32)
    loss = jnp.sum(total[512:], axis=0, keepdims=True)
    loss = thirds(jnp.broadcast_to(jnp.sum(loss, axis=1, keepdims=True), (1, 128)), 8)
    row = lax.broadcasted_iota(jnp.int32, (8, 128), 0)
    lane = lax.broadcasted_iota(jnp.int32, (8, 128), 1)
    loss = jnp.where(lane == 64 + row, loss, 0.0)
    kept = [total[:256].reshape(32, 8, 128), total[256:512].reshape(32, 8, 128)]
    group = lane_group((32, 8, 128))
    for x in range(NX):
        one = pltpu.roll(kept[0], (4 - x) % 4 * 32, 2)
        two = pltpu.roll(kept[1], (5 - x) % 4 * 32, 2)
        mid_ref[:, x] = jnp.where(group == 0, one, jnp.where(group == 1, two, loss[None]))
    out_ref[...] = mid_ref[...].reshape(1024, 128).astype(BF16)


def final_kernel(got_ref, pat_ref, out_ref, loss_ref):
    total = got_ref[0].astype(F32)
    for z in range(1, NZ):
        total = total + got_ref[z].astype(F32)
    loss = jnp.where(lane_group(total.shape) == 2, total, 0.0)
    loss = jnp.sum(jnp.sum(loss, axis=0, keepdims=True), axis=1, keepdims=True)
    loss_ref[...] = loss / (TOKENS * KVW)
    one, two = total[:32], total[32:]
    group = lane_group((32, 128))
    near = jnp.where(group == 0, one, pltpu.roll(two, 32, 1))
    far = jnp.where(group == 2, pltpu.roll(one, 32, 1), pltpu.roll(two, 64, 1))
    kept = jnp.where(group < 2, near, far)
    row = lax.broadcasted_iota(jnp.int32, (32, 128), 0)
    col = lax.broadcasted_iota(jnp.int32, (32, 128), 1)
    spread = jnp.where(col // 4 == row, 1.0, 0.0).astype(BF16)
    wide = jnp.zeros((128, 128), F32)
    for _ in range(3):
        part = kept.astype(BF16)
        kept = kept - part.astype(F32)
        wide += lax.dot_general(
            part, spread, (((0,), (0,)), ((), ())), preferred_element_type=F32
        )
    first, second = kept_rows(pat_ref[...])
    spot = row_of_four(wide[:64].shape)
    grad = jnp.where(spot == first, wide[:64], 0.0) + jnp.where(spot == second, wide[64:], 0.0)
    out_ref[...] = grad / jnp.sqrt(F32(TOKENS))


def ring(step):
    return [(i, (i + step) % NX) for i in range(NX)]


def shards(hidden, norm_gain, teacher_k, student_k, keep_pattern):
    z, yl, core, yh, x = (lax.axis_index(a) for a in AXES)
    place = (z * NYL + yl) * NC + core
    at = jnp.stack([x, core, yl, place, yl * NYH + yh]).astype(jnp.int32)
    patterns = keep_pattern.T

    packed, pat = call(
        pack_kernel,
        (shape((NZ, 64, 128), BF16), shape((64, 128), F32)),
        teacher_k.T,
        student_k.T,
        patterns,
        at,
        scratch=[
            pltpu.VMEM((64, 128), BF16),
            pltpu.VMEM((64, 128), BF16),
            pltpu.VMEM((64, 128), jnp.int32),
            pltpu.SemaphoreType.DMA((3,)),
        ],
        far=(0, 1, 2),
        grant=60,
        name="pack",
    )
    got_w = lax.all_to_all(packed.reshape(128, 8, 128), ZCX, 0, 0, tiled=True)

    split = call(
        norm_kernel,
        (shape((128, 2048), BF16),) * NX,
        hidden,
        norm_gain.reshape(64, 128),
        at,
        scratch=[
            pltpu.VMEM((2048, 512), BF16),
            pltpu.VMEM((128, D), BF16),
            pltpu.SemaphoreType.DMA((4,)),
        ],
        flops=2 * 2048 * 512 * 512,
        far=(0,),
        grant=60,
        name="norm",
    )
    own = [split[0]] + [lax.ppermute(split[i], "x", ring(STEP[i])) for i in range(1, NX)]
    pair = [lax.ppermute(piece, "core", [(0, 1), (1, 0)]) for piece in own]

    rows_w = call(
        spread_kernel,
        shape((4, 1024, 128), BF16),
        got_w.reshape(1024, 128),
        scratch=[pltpu.VMEM((32, 4, 8, 128), F32)],
        name="spread",
    )
    all_w = lax.all_to_all(rows_w, Y, 0, 0, tiled=True)
    high, low = call(decode_kernel, (shape((2048, 256), BF16),) * 2, all_w, name="decode")

    late, _ = lax.optimization_barrier((patterns, rows_w))
    chosen = call(
        choose_kernel,
        (shape((256, 128), BF16),) * NX,
        late,
        at,
        scratch=[pltpu.VMEM((NZ, NYL, NC, NX, 8, 128), F32)],
        name="choose",
    )

    flops = 2 * 1024 * 2048 * 256
    part = call(
        forward_kernel,
        shape((NX, 256, 256), BF16),
        *own,
        *pair,
        high,
        low,
        at,
        flops=2 * flops,
        name="forward",
    )
    part, chosen = lax.optimization_barrier((part, chosen))
    got_part = lax.all_to_all(part, "x", 0, 0, tiled=True)
    line = [chosen[0]] + [lax.ppermute(chosen[i], "x", ring(STEP[i])) for i in range(1, NX)]
    slope, loss_part = call(
        slope_kernel, (shape((NX, 256, 256), BF16), shape((1, 128), F32)), got_part, name="slope"
    )
    slope, line = lax.optimization_barrier((slope, line))
    slopes = lax.all_to_all(slope, "x", 0, 0, tiled=True)
    joined = call(join_kernel, shape((256, 128), BF16), *line, name="join")
    pats = [joined] + [lax.ppermute(joined, Y, [(y, y ^ i) for y in range(4)]) for i in range(1, 4)]

    term = call(
        grad_kernel,
        shape((4, 528, 128), BF16),
        *own,
        *pair,
        *pats,
        slopes,
        loss_part,
        at,
        scratch=[pltpu.VMEM((1024, 256), BF16), pltpu.VMEM((4, 32, 4, 8, 128), F32)],
        flops=flops,
        name="grad",
    )
    got_term = lax.all_to_all(term, Y, 0, 0, tiled=True)
    packed_term = call(
        gather_kernel,
        shape((1024, 128), BF16),
        got_term,
        scratch=[pltpu.VMEM((32, 4, 8, 128), F32)],
        name="gather",
    )
    got_sum = lax.all_to_all(packed_term.reshape(128, 8, 128), ZCX, 0, 0, tiled=True)
    grad, loss = call(
        final_kernel,
        (shape((64, 128), F32), shape((1, 1), F32)),
        got_sum.reshape(NZ, 64, 128),
        pat,
        name="final",
    )
    return grad.T, loss.reshape(())


def solution(mesh):
    fine = Mesh(mesh.devices.reshape(NZ, NYL, NC, NYH, NX), AXES)
    dp, tensor = ("z", "yl", "core"), ("yh", "x")
    in_specs = (P(AXES, None), P(), P(dp, tensor), P(dp, tensor), P(None, tensor))
    out_specs = (P(dp, tensor), P())
    return jax.shard_map(shards, mesh=fine, in_specs=in_specs, out_specs=out_specs, check_vma=False)
```

```python
import jax
import jax.numpy as jnp
from jax import lax
from jax.experimental import pallas as pl
from jax.experimental.pallas import tpu as pltpu
from jax.sharding import Mesh, PartitionSpec as P

F32 = jnp.float32
BF16 = jnp.bfloat16
NZ, NYL, NC, NYH, NX = 16, 2, 2, 2, 4
AXES = ("z", "yl", "core", "yh", "x")
Y = ("yl", "yh")
ZCX = ("z", "core", "x")
D, KVW, TOKENS = 8192, 512, 65536
SHIFT = 34
VMEM = pl.BlockSpec(memory_space=pltpu.VMEM)
SMEM = pl.BlockSpec(memory_space=pltpu.SMEM)
STEP = (0, 2, 1, 3)
BACK = (0, 2, 3, 1)


def call(kernel, out_shape, *args, scratch=(), flops=0, name=None, far=(), grant=24):
    size = sum(a.size * a.dtype.itemsize for a in args)
    for o in jax.tree.leaves(out_shape):
        size += o.size * o.dtype.itemsize
    specs = [SMEM if a.shape == (5,) else VMEM for a in args]
    for i in far:
        specs[i] = pl.BlockSpec(memory_space=pl.ANY)
    return pl.pallas_call(
        kernel,
        out_shape=out_shape,
        in_specs=specs,
        out_specs=jax.tree.map(lambda _: VMEM, out_shape),
        scratch_shapes=list(scratch),
        name=name,
        cost_estimate=pl.CostEstimate(flops=flops, bytes_accessed=size, transcendentals=0),
        compiler_params=pltpu.CompilerParams(vmem_limit_bytes=grant * 1024 * 1024),
    )(*args)


def shape(dims, dtype):
    return jax.ShapeDtypeStruct(dims, dtype)


def lane_group(dims):
    return lax.broadcasted_iota(jnp.int32, dims, len(dims) - 1) // 32


def swap_groups(parts, place):
    total = None
    for b, part in enumerate(parts):
        shift = (b - place) * 32 % 128
        moved = pltpu.roll(part, shift, part.ndim - 1) if shift else part
        here = jnp.where(lane_group(part.shape) == b, moved, 0.0)
        total = here if total is None else total + here
    return total


def kept_rows(pat):
    first = jnp.where(pat > 2.5, 1.0, 0.0) + jnp.where(pat > 4.5, 1.0, 0.0)
    second = jnp.where(pat < 2.5, pat + 1.0, jnp.where(pat < 3.5, 2.0, 3.0))
    return first, second


def row_of_four(dims):
    return (lax.broadcasted_iota(jnp.int32, dims, 1) % 4).astype(F32)


def shuffled(place):
    return place % 4 * 8 + place // 4


def norm_kernel(x_hbm, gain_ref, at_ref, *rest):
    outs, (rows_ref, x_ref, sems) = rest[:NX], rest[NX:]
    me = at_ref[0]
    cuts = [pl.ds(i * 2048, 2048) for i in range(4)]
    loads = [
        pltpu.make_async_copy(x_hbm.at[:, cut], x_ref.at[:, cut], sems.at[i])
        for i, cut in enumerate(cuts)
    ]
    for load in loads:
        load.start()
    total = jnp.zeros((128, 512), F32)
    for g in range(16):
        if g % 4 == 0:
            loads[g // 4].wait()
        part = x_ref[:, g * 512 : (g + 1) * 512].astype(F32)
        total += part * part
    factor = lax.rsqrt(jnp.sum(total, axis=1, keepdims=True) / D + 1e-05)
    gain = gain_ref[...].astype(F32)
    for yl in range(2):
        for m in range(8):
            tile = yl * 8 + m
            for b in range(4):
                block = 8 * m + 4 * (b // 2) + 2 * yl + b % 2
                part = x_ref[:, block * 128 : (block + 1) * 128].astype(F32)
                rows_ref[tile * 128 : (tile + 1) * 128, b * 128 : (b + 1) * 128] = (
                    part * factor * gain[block : block + 1, :]
                ).astype(BF16)
    src = lax.broadcasted_iota(jnp.int32, (512, 512), 0)
    dst = lax.broadcasted_iota(jnp.int32, (512, 512), 1)
    ahead = (src // 32 + NX - me) % NX
    goal = ahead * 128 + src // 128 * 32 + shuffled(src % 32)
    move = jnp.where(goal == dst, 1.0, 0.0).astype(BF16)
    for tile in range(16):
        seg = jnp.dot(
            rows_ref[tile * 128 : (tile + 1) * 128, :], move, preferred_element_type=F32
        ).astype(BF16)
        for i, x in enumerate(STEP):
            outs[i][:, tile * 128 : (tile + 1) * 128] = seg[:, x * 128 : (x + 1) * 128]


def choose_kernel(pat_ref, at_ref, out_ref, pick_ref):
    col = lax.broadcasted_iota(jnp.int32, (64, 128), 0)
    lane = lax.broadcasted_iota(jnp.int32, (64, 128), 1)
    pick = jnp.where(col - at_ref[1] * 32 == lane % 32, 1.0, 0.0).astype(BF16)
    chosen = lax.dot_general(
        pat_ref[...].astype(F32).astype(BF16),
        pick,
        (((0,), (0,)), ((), ())),
        preferred_element_type=F32,
    )
    pick_ref[...] = chosen.reshape(NZ, NYL, NC, NX, 8, 128)
    group = lane_group((32, 128))
    for x in range(NX):
        for yl in range(NYL):
            rows = pick_ref[:, yl, :, x].reshape(8, 32, 128)
            for tile in range(2):
                total = jnp.zeros((32, 128), F32)
                for b in range(4):
                    total = jnp.where(group == b, rows[tile * 4 + b], total)
                out_ref[x, yl * 32 : (yl + 1) * 32, tile * 128 : (tile + 1) * 128] = total.astype(BF16)


def pack_kernel(teacher_hbm, student_hbm, pat_hbm, at_ref, out_ref, rows_ref, *scratch):
    teacher_ref, student_ref, pat_ref, sems = scratch
    place = at_ref[3]
    window = pl.ds(pl.multiple_of(place // 4 * 128, 128), 128)
    loads = [
        pltpu.make_async_copy(pat_hbm.at[:, window], pat_ref, sems.at[0]),
        pltpu.make_async_copy(teacher_hbm, teacher_ref, sems.at[1]),
        pltpu.make_async_copy(student_hbm, student_ref, sems.at[2]),
    ]
    for load in loads:
        load.start()
    for load in loads:
        load.wait()
    row = lax.broadcasted_iota(jnp.int32, (128, 128), 0)
    col = lax.broadcasted_iota(jnp.int32, (128, 128), 1)
    spread = jnp.where(col // 4 + place % 4 * 32 == row, 1.0, 0.0).astype(BF16)
    pat = jnp.dot(pat_ref[...].astype(F32).astype(BF16), spread, preferred_element_type=F32)
    rows_ref[...] = pat
    first, second = kept_rows(pat)
    spot = row_of_four(pat.shape)
    keep = jnp.where((spot == first) | (spot == second), 1.0, 0.0)
    delta = student_ref[...].astype(F32) * keep - teacher_ref[...].astype(F32)
    delta = delta * 2.0**SHIFT
    delta = ((delta * jnp.abs(delta)) * (delta * delta)).astype(BF16)
    row = lax.broadcasted_iota(jnp.int32, (64, 128), 0)
    col = lax.broadcasted_iota(jnp.int32, (64, 128), 1)
    widen = jnp.where(row == col, 1.0, 0.0).astype(BF16)
    rows = lax.dot_general(
        delta, widen, (((0,), (0,)), ((), ())), preferred_element_type=F32
    ).astype(BF16)
    dst = lax.broadcasted_iota(jnp.int32, (128, 128), 0)
    src = lax.broadcasted_iota(jnp.int32, (128, 128), 1)
    move = jnp.where(src // 32 * 32 + shuffled(src % 32) == dst, 1.0, 0.0).astype(BF16)
    wide = jnp.dot(move, rows, preferred_element_type=F32).reshape(4, 4, 8, 128)
    for c in range(NC):
        piece = swap_groups([wide[:, q] for q in range(4)], c).reshape(32, 128).astype(BF16)
        for z in range(NZ):
            out_ref[z, c * 32 : (c + 1) * 32, :] = piece


def spread_kernel(got_ref, out_ref, mid_ref):
    got = got_ref[...].astype(F32).reshape(32, 4, 8, 128)
    for q in range(4):
        mid_ref[:, q] = swap_groups([got[:, x] for x in range(NX)], q)
    rows = mid_ref[...].reshape(1024, 128).astype(BF16)
    for y in range(4):
        out_ref[y] = rows


def decode_kernel(w_ref, high_ref, low_ref):
    for y in range(4):
        for k in range(4):
            sent = w_ref[y, k * 256 : (k + 1) * 256, :].astype(F32)
            size = jnp.sqrt(jnp.sqrt(jnp.abs(sent))) * 2.0**-SHIFT
            delta = jnp.where(sent < 0, -size, size)
            high = delta.astype(BF16)
            at = (y // 2) * 1024 + k * 256
            lane = (y % 2) * 128
            high_ref[at : at + 256, lane : lane + 128] = high
            low_ref[at : at + 256, lane : lane + 128] = (delta - high.astype(F32)).astype(BF16)


def forward_kernel(*refs):
    own, pair, rest = refs[:NX], refs[NX : 2 * NX], refs[2 * NX :]
    high_ref, low_ref, own_pat, other_pat, at_ref, out_ref, held_ref, sems = rest
    loads = [pltpu.make_async_copy(pair[i], held_ref.at[i], sems.at[i]) for i in range(NX)]
    for load in loads:
        load.start()
    for x in range(NX):
        out_ref[x, 256:320] = own_pat[x]
        out_ref[x, 320:] = other_pat[x]
    for row in (0, 128):
        for i in range(NX):
            if row:
                loads[i].wait()
            rows = held_ref[i] if row else own[i][...]
            part = jnp.dot(rows, high_ref[...], preferred_element_type=F32)
            part += jnp.dot(rows, low_ref[...], preferred_element_type=F32)
            out_ref[(at_ref[0] + BACK[i]) % NX, row : row + 128] = part.astype(BF16)


def thirds(value, rows):
    high = value.astype(BF16).astype(F32)
    mid = (value - high).astype(BF16).astype(F32)
    low = value - high - mid
    row = lax.broadcasted_iota(jnp.int32, (rows, value.shape[1]), 0)
    return jnp.where(row == 0, high, jnp.where(row == 1, mid, jnp.where(row == 2, low, 0.0)))


def slope_kernel(part_ref, out_ref, loss_ref, pat_ref):
    diff = part_ref[0, :256].astype(F32)
    for x in range(1, NX):
        diff = diff + part_ref[x, :256].astype(F32)
    slope = diff.astype(BF16)
    for x in range(NX):
        out_ref[x] = slope
    square = diff * diff
    loss_ref[...] = jnp.sum(square[:, :128] + square[:, 128:], axis=0, keepdims=True)
    group = lane_group((32, 128))
    for part in range(4):
        for b in range(8):
            total = jnp.zeros((32, 128), F32)
            for x in range(NX):
                sent = part_ref[x, 256 + part * 32 : 288 + part * 32, b // 4 * 128 : b // 4 * 128 + 128]
                shift = (x - b) % 4 * 32
                sent = sent.astype(F32)
                sent = pltpu.roll(sent, shift, 1) if shift else sent
                total = jnp.where(group == x, sent, total)
            pat_ref[part, b * 32 : (b + 1) * 32, :] = total.astype(BF16)


def grad_kernel(*refs):
    own, (held_ref, *rest) = refs[:NX], refs[NX:]
    pat_ref, slope_ref, loss_ref, at_ref, out_ref, s_ref, term_ref = rest
    contract = (((0,), (0,)), ((), ()))
    for i in range(NX):
        x = (at_ref[0] + BACK[i]) % NX
        s_ref[i * 128 : (i + 1) * 128] = slope_ref[x, :128]
        s_ref[512 + i * 128 : 512 + (i + 1) * 128] = slope_ref[x, 128:]
    for k in range(8):
        at = k * 256
        rows = [ref[:, at : at + 256] for ref in own]
        rows += [held_ref[i, :, at : at + 256] for i in range(NX)]
        rows = jnp.concatenate(rows, axis=0)
        term = lax.dot_general(rows, s_ref[...], contract, preferred_element_type=F32)
        for yh in range(2):
            term_ref[(k // 4) * 2 + yh, (k % 4) * 8 : (k % 4 + 1) * 8] = term[
                :, yh * 128 : (yh + 1) * 128
            ].reshape(8, 4, 8, 128)
    loss = thirds(loss_ref[...], 16).astype(BF16)
    for i in range(4):
        y = i % 2 * 2 + jnp.where(i < 2, at_ref[4], 1 - at_ref[4])
        first, second = kept_rows(pat_ref[i].astype(F32).reshape(32, 8, 128))
        for row, which in ((0, first), (256, second)):
            kept = jnp.zeros_like(which)
            for k in range(4):
                kept += jnp.where(which == k, term_ref[y, :, k], 0.0)
            out_ref[y, row : row + 256] = kept.reshape(256, 128).astype(BF16)
        out_ref[y, 512:] = loss


def gather_kernel(got_ref, out_ref, mid_ref):
    total = got_ref[0].astype(F32)
    for y in range(1, 4):
        total = total + got_ref[y].astype(F32)
    loss = jnp.sum(total[512:], axis=0, keepdims=True)
    loss = thirds(jnp.broadcast_to(jnp.sum(loss, axis=1, keepdims=True), (1, 128)), 8)
    row = lax.broadcasted_iota(jnp.int32, (8, 128), 0)
    lane = lax.broadcasted_iota(jnp.int32, (8, 128), 1)
    loss = jnp.where(lane == 64 + row, loss, 0.0)
    kept = [total[:256].reshape(32, 8, 128), total[256:512].reshape(32, 8, 128)]
    group = lane_group((32, 8, 128))
    for x in range(NX):
        one = pltpu.roll(kept[0], (4 - x) % 4 * 32, 2)
        two = pltpu.roll(kept[1], (5 - x) % 4 * 32, 2)
        mid_ref[:, x] = jnp.where(group == 0, one, jnp.where(group == 1, two, loss[None]))
    out_ref[...] = mid_ref[...].reshape(1024, 128).astype(BF16)


def final_kernel(got_ref, pat_ref, out_ref, loss_ref):
    total = got_ref[0].astype(F32)
    for z in range(1, NZ):
        total = total + got_ref[z].astype(F32)
    loss = jnp.where(lane_group(total.shape) == 2, total, 0.0)
    loss = jnp.sum(jnp.sum(loss, axis=0, keepdims=True), axis=1, keepdims=True)
    loss_ref[...] = loss / (TOKENS * KVW)
    one, two = total[:32], total[32:]
    group = lane_group((32, 128))
    near = jnp.where(group == 0, one, pltpu.roll(two, 32, 1))
    far = jnp.where(group == 2, pltpu.roll(one, 32, 1), pltpu.roll(two, 64, 1))
    kept = jnp.where(group < 2, near, far)
    row = lax.broadcasted_iota(jnp.int32, (32, 128), 0)
    col = lax.broadcasted_iota(jnp.int32, (32, 128), 1)
    spread = jnp.where(col // 4 == row, 1.0, 0.0).astype(BF16)
    wide = jnp.zeros((128, 128), F32)
    for _ in range(3):
        part = kept.astype(BF16)
        kept = kept - part.astype(F32)
        wide += lax.dot_general(
            part, spread, (((0,), (0,)), ((), ())), preferred_element_type=F32
        )
    first, second = kept_rows(pat_ref[...])
    spot = row_of_four(wide[:64].shape)
    grad = jnp.where(spot == first, wide[:64], 0.0) + jnp.where(spot == second, wide[64:], 0.0)
    out_ref[...] = grad / jnp.sqrt(F32(TOKENS))


def ring(step):
    return [(i, (i + step) % NX) for i in range(NX)]


def shards(hidden, norm_gain, teacher_k, student_k, keep_pattern):
    z, yl, core, yh, x = (lax.axis_index(a) for a in AXES)
    place = (z * NYL + yl) * NC + core
    at = jnp.stack([x, core, yl, place, yh]).astype(jnp.int32)
    patterns = keep_pattern.T

    packed, pat = call(
        pack_kernel,
        (shape((NZ, 64, 128), BF16), shape((64, 128), F32)),
        teacher_k.T,
        student_k.T,
        patterns,
        at,
        scratch=[
            pltpu.VMEM((64, 128), BF16),
            pltpu.VMEM((64, 128), BF16),
            pltpu.VMEM((64, 128), jnp.int32),
            pltpu.SemaphoreType.DMA((3,)),
        ],
        far=(0, 1, 2),
        grant=60,
        name="pack",
    )
    got_w = lax.all_to_all(packed.reshape(128, 8, 128), ZCX, 0, 0, tiled=True)

    split = call(
        norm_kernel,
        (shape((128, 2048), BF16),) * NX,
        hidden,
        norm_gain.reshape(64, 128),
        at,
        scratch=[
            pltpu.VMEM((2048, 512), BF16),
            pltpu.VMEM((128, D), BF16),
            pltpu.SemaphoreType.DMA((4,)),
        ],
        flops=2 * 2048 * 512 * 512,
        far=(0,),
        grant=60,
        name="norm",
    )
    own = [split[0]] + [lax.ppermute(split[i], "x", ring(STEP[i])) for i in range(1, NX)]
    pair = [lax.ppermute(piece, "core", [(0, 1), (1, 0)]) for piece in own]

    rows_w = call(
        spread_kernel,
        shape((4, 1024, 128), BF16),
        got_w.reshape(1024, 128),
        scratch=[pltpu.VMEM((32, 4, 8, 128), F32)],
        name="spread",
    )
    all_w = lax.all_to_all(rows_w, Y, 0, 0, tiled=True)
    high, low = call(decode_kernel, (shape((2048, 256), BF16),) * 2, all_w, name="decode")

    late, _ = lax.optimization_barrier((patterns, rows_w))
    own_pat = call(
        choose_kernel,
        shape((NX, 64, 256), BF16),
        late,
        at,
        scratch=[pltpu.VMEM((NZ, NYL, NC, NX, 8, 128), F32)],
        name="choose",
    )
    other_pat = lax.ppermute(own_pat, "yh", [(0, 1), (1, 0)])

    flops = 2 * 1024 * 2048 * 256
    part, held = call(
        forward_kernel,
        (shape((NX, 384, 256), BF16), shape((NX, 128, 2048), BF16)),
        *own,
        *pair,
        high,
        low,
        own_pat,
        other_pat,
        at,
        scratch=[pltpu.SemaphoreType.DMA((NX,))],
        flops=2 * flops,
        far=range(NX, 2 * NX),
        name="forward",
    )
    got_part = lax.all_to_all(part, "x", 0, 0, tiled=True)
    slope, loss_part, pats = call(
        slope_kernel,
        (shape((NX, 256, 256), BF16), shape((1, 128), F32), shape((4, 256, 128), BF16)),
        got_part,
        name="slope",
    )
    slopes = lax.all_to_all(slope, "x", 0, 0, tiled=True)

    term = call(
        grad_kernel,
        shape((4, 528, 128), BF16),
        *own,
        held,
        pats,
        slopes,
        loss_part,
        at,
        scratch=[pltpu.VMEM((1024, 256), BF16), pltpu.VMEM((4, 32, 4, 8, 128), F32)],
        flops=flops,
        name="grad",
    )
    got_term = lax.all_to_all(term, Y, 0, 0, tiled=True)
    packed_term = call(
        gather_kernel,
        shape((1024, 128), BF16),
        got_term,
        scratch=[pltpu.VMEM((32, 4, 8, 128), F32)],
        name="gather",
    )
    got_sum = lax.all_to_all(packed_term.reshape(128, 8, 128), ZCX, 0, 0, tiled=True)
    grad, loss = call(
        final_kernel,
        (shape((64, 128), F32), shape((1, 1), F32)),
        got_sum.reshape(NZ, 64, 128),
        pat,
        name="final",
    )
    return grad.T, loss.reshape(())


def solution(mesh):
    fine = Mesh(mesh.devices.reshape(NZ, NYL, NC, NYH, NX), AXES)
    dp, tensor = ("z", "yl", "core"), ("yh", "x")
    in_specs = (P(AXES, None), P(), P(dp, tensor), P(dp, tensor), P(None, tensor))
    out_specs = (P(dp, tensor), P())
    return jax.shard_map(shards, mesh=fine, in_specs=in_specs, out_specs=out_specs, check_vma=False)
```

```python
import jax
import jax.numpy as jnp
from jax import lax
from jax.experimental import pallas as pl
from jax.experimental.pallas import tpu as pltpu
from jax.sharding import Mesh, PartitionSpec as P

F32 = jnp.float32
BF16 = jnp.bfloat16
NZ, NYL, NC, NYH, NX = 16, 2, 2, 2, 4
AXES = ("z", "yl", "core", "yh", "x")
PLANE = ("yl", "core", "yh", "x")
D, KVW, TOKENS = 8192, 512, 65536
SHIFT = 34
VMEM = pl.BlockSpec(memory_space=pltpu.VMEM)
SMEM = pl.BlockSpec(memory_space=pltpu.SMEM)
STEP = (0, 2, 1, 3)
BACK = (0, 2, 3, 1)


def call(kernel, out_shape, *args, scratch=(), flops=0, name=None, far=(), grant=24):
    size = sum(a.size * a.dtype.itemsize for a in args)
    for o in jax.tree.leaves(out_shape):
        size += o.size * o.dtype.itemsize
    specs = [SMEM if a.shape == (5,) else VMEM for a in args]
    for i in far:
        specs[i] = pl.BlockSpec(memory_space=pl.ANY)
    return pl.pallas_call(
        kernel,
        out_shape=out_shape,
        in_specs=specs,
        out_specs=jax.tree.map(lambda _: VMEM, out_shape),
        scratch_shapes=list(scratch),
        name=name,
        cost_estimate=pl.CostEstimate(flops=flops, bytes_accessed=size, transcendentals=0),
        compiler_params=pltpu.CompilerParams(vmem_limit_bytes=grant * 1024 * 1024),
    )(*args)


def shape(dims, dtype):
    return jax.ShapeDtypeStruct(dims, dtype)


def lane_group(dims):
    return lax.broadcasted_iota(jnp.int32, dims, len(dims) - 1) // 32


def place_in_plane(yl, c, yh, x):
    return ((yl * NC + c) * NYH + yh) * NX + x


def swap_groups(parts, place):
    total = None
    for b, part in enumerate(parts):
        shift = (b - place) * 32 % 128
        moved = pltpu.roll(part, shift, part.ndim - 1) if shift else part
        here = jnp.where(lane_group(part.shape) == b, moved, 0.0)
        total = here if total is None else total + here
    return total


def kept_rows(pat):
    first = jnp.where(pat > 2.5, 1.0, 0.0) + jnp.where(pat > 4.5, 1.0, 0.0)
    second = jnp.where(pat < 2.5, pat + 1.0, jnp.where(pat < 3.5, 2.0, 3.0))
    return first, second


def row_of_four(dims):
    return (lax.broadcasted_iota(jnp.int32, dims, 1) % 4).astype(F32)


def shuffled(place):
    return place % 4 * 8 + place // 4


def norm_kernel(x_hbm, gain_ref, at_ref, *rest):
    outs, (rows_ref, x_ref, sems) = rest[:NX], rest[NX:]
    me = at_ref[0]
    cuts = [pl.ds(i * 2048, 2048) for i in range(4)]
    loads = [
        pltpu.make_async_copy(x_hbm.at[:, cut], x_ref.at[:, cut], sems.at[i])
        for i, cut in enumerate(cuts)
    ]
    for load in loads:
        load.start()
    total = jnp.zeros((128, 512), F32)
    for g in range(16):
        if g % 4 == 0:
            loads[g // 4].wait()
        part = x_ref[:, g * 512 : (g + 1) * 512].astype(F32)
        total += part * part
    factor = lax.rsqrt(jnp.sum(total, axis=1, keepdims=True) / D + 1e-05)
    gain = gain_ref[...].astype(F32)
    for yl in range(2):
        for m in range(8):
            tile = yl * 8 + m
            for b in range(4):
                block = 8 * m + 4 * (b // 2) + 2 * yl + b % 2
                part = x_ref[:, block * 128 : (block + 1) * 128].astype(F32)
                rows_ref[tile * 128 : (tile + 1) * 128, b * 128 : (b + 1) * 128] = (
                    part * factor * gain[block : block + 1, :]
                ).astype(BF16)
    src = lax.broadcasted_iota(jnp.int32, (512, 512), 0)
    dst = lax.broadcasted_iota(jnp.int32, (512, 512), 1)
    ahead = (src // 32 + NX - me) % NX
    goal = ahead * 128 + src // 128 * 32 + shuffled(src % 32)
    move = jnp.where(goal == dst, 1.0, 0.0).astype(BF16)
    for tile in range(16):
        seg = jnp.dot(
            rows_ref[tile * 128 : (tile + 1) * 128, :], move, preferred_element_type=F32
        ).astype(BF16)
        for i, x in enumerate(STEP):
            outs[i][:, tile * 128 : (tile + 1) * 128] = seg[:, x * 128 : (x + 1) * 128]


def choose_kernel(pat_ref, at_ref, out_ref, pick_ref):
    pats = pat_ref[...].astype(F32).astype(BF16)
    col = lax.broadcasted_iota(jnp.int32, (64, 128), 0)
    lane = lax.broadcasted_iota(jnp.int32, (64, 128), 1)
    group = lane_group((32, 128))
    for c in range(NC):
        pick = jnp.where(col - c * 32 == lane % 32, 1.0, 0.0).astype(BF16)
        chosen = lax.dot_general(pats, pick, (((0,), (0,)), ((), ())), preferred_element_type=F32)
        pick_ref[...] = chosen.reshape(NZ, NYL, NC, NX, 8, 128)
        for x in range(NX):
            rows = pick_ref[:, at_ref[2], at_ref[1], x].reshape(4, 32, 128)
            total = rows[0]
            for b in range(1, 4):
                total = jnp.where(group == b, rows[b], total)
            out_ref[c * NX + x] = total.astype(BF16)


def pack_kernel(teacher_hbm, student_hbm, pat_hbm, at_ref, out_ref, rows_ref, *scratch):
    teacher_ref, student_ref, pat_ref, sems = scratch
    place = at_ref[3]
    window = pl.ds(pl.multiple_of(place // 4 * 128, 128), 128)
    loads = [
        pltpu.make_async_copy(pat_hbm.at[:, window], pat_ref, sems.at[0]),
        pltpu.make_async_copy(teacher_hbm, teacher_ref, sems.at[1]),
        pltpu.make_async_copy(student_hbm, student_ref, sems.at[2]),
    ]
    for load in loads:
        load.start()
    for load in loads:
        load.wait()
    row = lax.broadcasted_iota(jnp.int32, (128, 128), 0)
    col = lax.broadcasted_iota(jnp.int32, (128, 128), 1)
    spread = jnp.where(col // 4 + place % 4 * 32 == row, 1.0, 0.0).astype(BF16)
    pat = jnp.dot(pat_ref[...].astype(F32).astype(BF16), spread, preferred_element_type=F32)
    rows_ref[...] = pat
    first, second = kept_rows(pat)
    spot = row_of_four(pat.shape)
    keep = jnp.where((spot == first) | (spot == second), 1.0, 0.0)
    delta = student_ref[...].astype(F32) * keep - teacher_ref[...].astype(F32)
    delta = delta * 2.0**SHIFT
    delta = ((delta * jnp.abs(delta)) * (delta * delta)).astype(BF16)
    row = lax.broadcasted_iota(jnp.int32, (64, 128), 0)
    col = lax.broadcasted_iota(jnp.int32, (64, 128), 1)
    widen = jnp.where(row == col, 1.0, 0.0).astype(BF16)
    rows = lax.dot_general(
        delta, widen, (((0,), (0,)), ((), ())), preferred_element_type=F32
    ).astype(BF16)
    dst = lax.broadcasted_iota(jnp.int32, (128, 128), 0)
    src = lax.broadcasted_iota(jnp.int32, (128, 128), 1)
    move = jnp.where(src // 32 * 32 + shuffled(src % 32) == dst, 1.0, 0.0).astype(BF16)
    wide = jnp.dot(move, rows, preferred_element_type=F32).reshape(4, 4, 8, 128)
    for c in range(NC):
        piece = swap_groups([wide[:, q] for q in range(4)], c).reshape(32, 128).astype(BF16)
        for z in range(NZ):
            out_ref[z, c * 32 : (c + 1) * 32, :] = piece


def spread_kernel(got_ref, pat_ref, out_ref):
    got = got_ref[...].astype(F32).reshape(NZ, 8, 8, 128)
    for c in range(NC):
        for x in range(NX):
            rows = got[:, c * NX + x].reshape(128, 128).astype(BF16)
            for y in range(4):
                at = place_in_plane(y // 2, c, y % 2, x)
                out_ref[at, :128, :] = rows
                out_ref[at, 128:, :] = pat_ref[c * NX + x]


def decode_kernel(got_ref, high_ref, low_ref, pat_ref, w_ref):
    for yl in range(NYL):
        for c in range(NC):
            for yh in range(NYH):
                at = [place_in_plane(yl, c, yh, x) for x in range(NX)]
                parts = [got_ref[i, :128, :].astype(F32).reshape(NZ, 8, 128) for i in at]
                for q in range(4):
                    sent = swap_groups(parts, q)
                    size = jnp.sqrt(jnp.sqrt(jnp.abs(sent))) * 2.0**-SHIFT
                    delta = jnp.where(sent < 0, -size, size)
                    w_ref[yl, :, c, q, :, yh * 128 : (yh + 1) * 128] = delta
                parts = [got_ref[i, 128:, :].astype(F32) for i in at]
                for b in range(4):
                    rows = swap_groups(parts, b).reshape(4, 8, 128)
                    pat_ref[yl * NYH + yh, b * 4 : (b + 1) * 4, c] = rows
    for yl in range(NYL):
        for k in range(4):
            delta = w_ref[yl, k * 4 : (k + 1) * 4].reshape(256, 256)
            high = delta.astype(BF16)
            at = yl * 1024 + k * 256
            high_ref[at : at + 256, :] = high
            low_ref[at : at + 256, :] = (delta - high.astype(F32)).astype(BF16)


def forward_kernel(*refs):
    own, pair, rest = refs[:NX], refs[NX : 2 * NX], refs[2 * NX :]
    high_ref, low_ref, at_ref, out_ref, held_ref, sems = rest
    loads = [pltpu.make_async_copy(pair[i], held_ref.at[i], sems.at[i]) for i in range(NX)]
    for load in loads:
        load.start()
    for row in (0, 128):
        if row:
            for load in loads:
                load.wait()
            rows = held_ref[...].reshape(512, 2048)
        else:
            rows = jnp.concatenate([ref[...] for ref in own], axis=0)
        part = jnp.dot(rows, high_ref[...], preferred_element_type=F32)
        part += jnp.dot(rows, low_ref[...], preferred_element_type=F32)
        part = part.astype(BF16)
        for i in range(NX):
            x = (at_ref[0] + BACK[i]) % NX
            out_ref[x, row : row + 128] = part[i * 128 : (i + 1) * 128]


def thirds(value, rows):
    high = value.astype(BF16).astype(F32)
    mid = (value - high).astype(BF16).astype(F32)
    low = value - high - mid
    row = lax.broadcasted_iota(jnp.int32, (rows, value.shape[1]), 0)
    return jnp.where(row == 0, high, jnp.where(row == 1, mid, jnp.where(row == 2, low, 0.0)))


def slope_kernel(part_ref, out_ref, loss_ref):
    diff = part_ref[0].astype(F32)
    for x in range(1, NX):
        diff = diff + part_ref[x].astype(F32)
    slope = diff.astype(BF16)
    for x in range(NX):
        out_ref[x] = slope
    square = diff * diff
    loss_ref[...] = jnp.sum(square[:, :128] + square[:, 128:], axis=0, keepdims=True)


def grad_kernel(*refs):
    own, (held_ref, *rest) = refs[:NX], refs[NX:]
    pat_ref, slope_ref, loss_ref, at_ref, out_ref, s_ref, term_ref = rest
    contract = (((0,), (0,)), ((), ()))
    for i in range(NX):
        x = (at_ref[0] + BACK[i]) % NX
        s_ref[i * 128 : (i + 1) * 128] = slope_ref[x, :128]
        s_ref[512 + i * 128 : 512 + (i + 1) * 128] = slope_ref[x, 128:]
    for k in range(8):
        at = k * 256
        rows = [ref[:, at : at + 256] for ref in own]
        rows += [held_ref[i, :, at : at + 256] for i in range(NX)]
        rows = jnp.concatenate(rows, axis=0)
        term = lax.dot_general(rows, s_ref[...], contract, preferred_element_type=F32)
        for yh in range(2):
            term_ref[(k // 4) * 2 + yh, (k % 4) * 8 : (k % 4 + 1) * 8] = term[
                :, yh * 128 : (yh + 1) * 128
            ].reshape(8, 4, 8, 128)
    loss = thirds(loss_ref[...], 16).astype(BF16)
    for y in range(4):
        which = kept_rows(pat_ref[y].reshape(32, 8, 128))
        kept = [jnp.zeros((32, 8, 128), F32) for _ in which]
        for k in range(4):
            for i in range(2):
                kept[i] += jnp.where(which[i] == k, term_ref[y, :, k], 0.0)
        kept = [part.reshape(2, 8, NC, 8, 128) for part in kept]
        for c in range(NC):
            parts = [kept[i][half, :, c] for half in range(2) for i in range(2)]
            for x in range(NX):
                at = place_in_plane(y // 2, c, y % 2, x)
                out_ref[at, :64, :] = swap_groups(parts, x).reshape(64, 128).astype(BF16)
                out_ref[at, 64:, :] = loss


def gather_kernel(got_ref, out_ref, mid_ref):
    loss = got_ref[0, 64:, :].astype(F32)
    for i in range(1, 32):
        loss = loss + got_ref[i, 64:, :].astype(F32)
    loss = jnp.sum(jnp.sum(loss, axis=0, keepdims=True), axis=1, keepdims=True)
    loss = thirds(jnp.broadcast_to(loss, (1, 128)), 16)
    lane = lax.broadcasted_iota(jnp.int32, (16, 128), 1)
    mid_ref[:, 32:, :] = jnp.broadcast_to(jnp.where(lane == 0, loss, 0.0), (NZ, 16, 128))
    group = lane_group((8, 8, 128))
    for x in range(NX):
        sums = []
        for c in range(NC):
            total = jnp.zeros((64, 128), F32)
            for y in range(4):
                total += got_ref[place_in_plane(y // 2, c, y % 2, x), :64, :].astype(F32)
            sums.append(total.reshape(8, 8, 128))
        for half in range(2):
            rows = jnp.zeros((8, 8, 128), F32)
            for kept in range(2):
                for c in range(NC):
                    goal = kept * 2 + c
                    shift = (goal - half * 2 - kept) % 4 * 32
                    moved = pltpu.roll(sums[c], shift, 2) if shift else sums[c]
                    rows = jnp.where(group == goal, moved, rows)
            mid_ref[half * 8 : (half + 1) * 8, x * 8 : (x + 1) * 8, :] = rows
    out_ref[...] = mid_ref[...].astype(BF16)


def final_kernel(got_ref, pat_ref, out_ref, loss_ref):
    total = got_ref[0].astype(F32)
    for z in range(1, NZ):
        total = total + got_ref[z].astype(F32)
    loss = jnp.sum(jnp.sum(total[32:], axis=0, keepdims=True), axis=1, keepdims=True)
    loss_ref[...] = loss / (TOKENS * KVW)
    kept = total[:32]
    row = lax.broadcasted_iota(jnp.int32, (32, 128), 0)
    col = lax.broadcasted_iota(jnp.int32, (32, 128), 1)
    spread = jnp.where(col // 4 == row, 1.0, 0.0).astype(BF16)
    wide = jnp.zeros((128, 128), F32)
    for _ in range(3):
        part = kept.astype(BF16)
        kept = kept - part.astype(F32)
        wide += lax.dot_general(
            part, spread, (((0,), (0,)), ((), ())), preferred_element_type=F32
        )
    first, second = kept_rows(pat_ref[...])
    spot = row_of_four(wide[:64].shape)
    grad = jnp.where(spot == first, wide[:64], 0.0) + jnp.where(spot == second, wide[64:], 0.0)
    out_ref[...] = grad / jnp.sqrt(F32(TOKENS))


def ring(step):
    return [(i, (i + step) % NX) for i in range(NX)]


def shards(hidden, norm_gain, teacher_k, student_k, keep_pattern):
    z, yl, core, yh, x = (lax.axis_index(a) for a in AXES)
    place = (z * NYL + yl) * NC + core
    at = jnp.stack([x, core, yl, place, yh]).astype(jnp.int32)
    patterns = keep_pattern.T

    packed, pat = call(
        pack_kernel,
        (shape((NZ, 64, 128), BF16), shape((64, 128), F32)),
        teacher_k.T,
        student_k.T,
        patterns,
        at,
        scratch=[
            pltpu.VMEM((64, 128), BF16),
            pltpu.VMEM((64, 128), BF16),
            pltpu.VMEM((64, 128), jnp.int32),
            pltpu.SemaphoreType.DMA((3,)),
        ],
        far=(0, 1, 2),
        grant=60,
        name="pack",
    )
    got_w = lax.all_to_all(packed, "z", 0, 0, tiled=True)

    split = call(
        norm_kernel,
        (shape((128, 2048), BF16),) * NX,
        hidden,
        norm_gain.reshape(64, 128),
        at,
        scratch=[
            pltpu.VMEM((2048, 512), BF16),
            pltpu.VMEM((128, D), BF16),
            pltpu.SemaphoreType.DMA((4,)),
        ],
        flops=2 * 2048 * 512 * 512,
        far=(0,),
        grant=60,
        name="norm",
    )
    own = [split[0]] + [lax.ppermute(split[i], "x", ring(STEP[i])) for i in range(1, NX)]
    pair = [lax.ppermute(piece, "core", [(0, 1), (1, 0)]) for piece in own]

    own_pat = call(
        choose_kernel,
        shape((8, 32, 128), BF16),
        patterns,
        at,
        scratch=[pltpu.VMEM((NZ, NYL, NC, NX, 8, 128), F32)],
        name="choose",
    )
    rows_w = call(spread_kernel, shape((32, 160, 128), BF16), got_w, own_pat, name="spread")
    all_w = lax.all_to_all(rows_w, PLANE, 0, 0, tiled=True)
    high, low, pats = call(
        decode_kernel,
        (shape((2048, 256), BF16),) * 2 + (shape((4, NZ, NC, 8, 128), F32),),
        all_w,
        scratch=[pltpu.VMEM((NYL, NZ, NC, 4, 8, 256), F32)],
        name="decode",
    )

    flops = 2 * 1024 * 2048 * 256
    part, held = call(
        forward_kernel,
        (shape((NX, 256, 256), BF16), shape((NX, 128, 2048), BF16)),
        *own,
        *pair,
        high,
        low,
        at,
        scratch=[pltpu.SemaphoreType.DMA((NX,))],
        flops=2 * flops,
        far=range(NX, 2 * NX),
        name="forward",
    )
    got_part = lax.all_to_all(part, "x", 0, 0, tiled=True)
    slope, loss_part = call(
        slope_kernel, (shape((NX, 256, 256), BF16), shape((1, 128), F32)), got_part, name="slope"
    )
    slopes = lax.all_to_all(slope, "x", 0, 0, tiled=True)

    term = call(
        grad_kernel,
        shape((32, 80, 128), BF16),
        *own,
        held,
        pats,
        slopes,
        loss_part,
        at,
        scratch=[pltpu.VMEM((1024, 256), BF16), pltpu.VMEM((4, 32, 4, 8, 128), F32)],
        flops=flops,
        name="grad",
    )
    got_term = lax.all_to_all(term, PLANE, 0, 0, tiled=True)
    packed_term = call(
        gather_kernel,
        shape((NZ, 48, 128), BF16),
        got_term,
        scratch=[pltpu.VMEM((NZ, 48, 128), F32)],
        name="gather",
    )
    got_sum = lax.all_to_all(packed_term, "z", 0, 0, tiled=True)
    grad, loss = call(
        final_kernel,
        (shape((64, 128), F32), shape((1, 1), F32)),
        got_sum,
        pat,
        name="final",
    )
    return grad.T, loss.reshape(())


def solution(mesh):
    fine = Mesh(mesh.devices.reshape(NZ, NYL, NC, NYH, NX), AXES)
    dp, tensor = ("z", "yl", "core"), ("yh", "x")
    in_specs = (P(AXES, None), P(), P(dp, tensor), P(dp, tensor), P(None, tensor))
    out_specs = (P(dp, tensor), P())
    return jax.shard_map(shards, mesh=fine, in_specs=in_specs, out_specs=out_specs, check_vma=False)
```

```python
import jax
import jax.numpy as jnp
from jax import lax
from jax.experimental import pallas as pl
from jax.experimental.pallas import tpu as pltpu
from jax.sharding import Mesh, PartitionSpec as P

F32 = jnp.float32
BF16 = jnp.bfloat16
NZ, NYL, NC, NYH, NX = 16, 2, 2, 2, 4
AXES = ("z", "yl", "core", "yh", "x")
Y = ("yl", "yh")
ZCX = ("z", "core", "x")
PLANE = ("yl", "core", "yh", "x")
D, KVW, TOKENS = 8192, 512, 65536
SHIFT = 34
VMEM = pl.BlockSpec(memory_space=pltpu.VMEM)
SMEM = pl.BlockSpec(memory_space=pltpu.SMEM)
STEP = (0, 2, 1, 3)
BACK = (0, 2, 3, 1)


def call(kernel, out_shape, *args, scratch=(), flops=0, name=None, far=(), grant=24):
    size = sum(a.size * a.dtype.itemsize for a in args)
    for o in jax.tree.leaves(out_shape):
        size += o.size * o.dtype.itemsize
    specs = [SMEM if a.shape == (5,) else VMEM for a in args]
    for i in far:
        specs[i] = pl.BlockSpec(memory_space=pl.ANY)
    return pl.pallas_call(
        kernel,
        out_shape=out_shape,
        in_specs=specs,
        out_specs=jax.tree.map(lambda _: VMEM, out_shape),
        scratch_shapes=list(scratch),
        name=name,
        cost_estimate=pl.CostEstimate(flops=flops, bytes_accessed=size, transcendentals=0),
        compiler_params=pltpu.CompilerParams(vmem_limit_bytes=grant * 1024 * 1024),
    )(*args)


def shape(dims, dtype):
    return jax.ShapeDtypeStruct(dims, dtype)


def lane_group(dims):
    return lax.broadcasted_iota(jnp.int32, dims, len(dims) - 1) // 32


def place_in_plane(yl, c, yh, x):
    return ((yl * NC + c) * NYH + yh) * NX + x


def swap_groups(parts, place):
    total = None
    for b, part in enumerate(parts):
        shift = (b - place) * 32 % 128
        moved = pltpu.roll(part, shift, part.ndim - 1) if shift else part
        here = jnp.where(lane_group(part.shape) == b, moved, 0.0)
        total = here if total is None else total + here
    return total


def kept_rows(pat):
    first = jnp.where(pat > 2.5, 1.0, 0.0) + jnp.where(pat > 4.5, 1.0, 0.0)
    second = jnp.where(pat < 2.5, pat + 1.0, jnp.where(pat < 3.5, 2.0, 3.0))
    return first, second


def row_of_four(dims):
    return (lax.broadcasted_iota(jnp.int32, dims, 1) % 4).astype(F32)


def shuffled(place):
    return place % 4 * 8 + place // 4


def norm_kernel(x_hbm, gain_ref, at_ref, *rest):
    outs, (rows_ref, x_ref, sems) = rest[:NX], rest[NX:]
    me = at_ref[0]
    cuts = [pl.ds(i * 2048, 2048) for i in range(4)]
    loads = [
        pltpu.make_async_copy(x_hbm.at[:, cut], x_ref.at[:, cut], sems.at[i])
        for i, cut in enumerate(cuts)
    ]
    for load in loads:
        load.start()
    total = jnp.zeros((128, 512), F32)
    for g in range(16):
        if g % 4 == 0:
            loads[g // 4].wait()
        part = x_ref[:, g * 512 : (g + 1) * 512].astype(F32)
        total += part * part
    factor = lax.rsqrt(jnp.sum(total, axis=1, keepdims=True) / D + 1e-05)
    gain = gain_ref[...].astype(F32)
    for yl in range(2):
        for m in range(8):
            tile = yl * 8 + m
            for b in range(4):
                block = 8 * m + 4 * (b // 2) + 2 * yl + b % 2
                part = x_ref[:, block * 128 : (block + 1) * 128].astype(F32)
                rows_ref[tile * 128 : (tile + 1) * 128, b * 128 : (b + 1) * 128] = (
                    part * factor * gain[block : block + 1, :]
                ).astype(BF16)
    src = lax.broadcasted_iota(jnp.int32, (512, 512), 0)
    dst = lax.broadcasted_iota(jnp.int32, (512, 512), 1)
    ahead = (src // 32 + NX - me) % NX
    goal = ahead * 128 + src // 128 * 32 + shuffled(src % 32)
    move = jnp.where(goal == dst, 1.0, 0.0).astype(BF16)
    for tile in range(16):
        seg = jnp.dot(
            rows_ref[tile * 128 : (tile + 1) * 128, :], move, preferred_element_type=F32
        ).astype(BF16)
        for i, x in enumerate(STEP):
            outs[i][:, tile * 128 : (tile + 1) * 128] = seg[:, x * 128 : (x + 1) * 128]


def choose_kernel(pat_ref, at_ref, out_ref, pick_ref):
    pats = pat_ref[...].astype(F32).astype(BF16)
    col = lax.broadcasted_iota(jnp.int32, (64, 128), 0)
    lane = lax.broadcasted_iota(jnp.int32, (64, 128), 1)
    for c in range(NC):
        pick = jnp.where(col - c * 32 == lane % 32, 1.0, 0.0).astype(BF16)
        chosen = lax.dot_general(pats, pick, (((0,), (0,)), ((), ())), preferred_element_type=F32)
        pick_ref[...] = chosen.reshape(NZ, NYL, NC, NX, 8, 128)
        out_ref[c] = pick_ref[:, at_ref[2], at_ref[1]]


def pack_kernel(teacher_hbm, student_hbm, pat_hbm, at_ref, out_ref, rows_ref, *scratch):
    teacher_ref, student_ref, pat_ref, sems = scratch
    place = at_ref[3]
    window = pl.ds(pl.multiple_of(place // 4 * 128, 128), 128)
    loads = [
        pltpu.make_async_copy(pat_hbm.at[:, window], pat_ref, sems.at[0]),
        pltpu.make_async_copy(teacher_hbm, teacher_ref, sems.at[1]),
        pltpu.make_async_copy(student_hbm, student_ref, sems.at[2]),
    ]
    for load in loads:
        load.start()
    for load in loads:
        load.wait()
    row = lax.broadcasted_iota(jnp.int32, (128, 128), 0)
    col = lax.broadcasted_iota(jnp.int32, (128, 128), 1)
    spread = jnp.where(col // 4 + place % 4 * 32 == row, 1.0, 0.0).astype(BF16)
    pat = jnp.dot(pat_ref[...].astype(F32).astype(BF16), spread, preferred_element_type=F32)
    rows_ref[...] = pat
    first, second = kept_rows(pat)
    spot = row_of_four(pat.shape)
    keep = jnp.where((spot == first) | (spot == second), 1.0, 0.0)
    delta = student_ref[...].astype(F32) * keep - teacher_ref[...].astype(F32)
    delta = delta * 2.0**SHIFT
    delta = ((delta * jnp.abs(delta)) * (delta * delta)).astype(BF16)
    row = lax.broadcasted_iota(jnp.int32, (64, 128), 0)
    col = lax.broadcasted_iota(jnp.int32, (64, 128), 1)
    widen = jnp.where(row == col, 1.0, 0.0).astype(BF16)
    rows = lax.dot_general(
        delta, widen, (((0,), (0,)), ((), ())), preferred_element_type=F32
    ).astype(BF16)
    dst = lax.broadcasted_iota(jnp.int32, (128, 128), 0)
    src = lax.broadcasted_iota(jnp.int32, (128, 128), 1)
    move = jnp.where(src // 32 * 32 + shuffled(src % 32) == dst, 1.0, 0.0).astype(BF16)
    wide = jnp.dot(move, rows, preferred_element_type=F32).reshape(4, 4, 8, 128)
    for c in range(NC):
        piece = swap_groups([wide[:, q] for q in range(4)], c).reshape(32, 128).astype(BF16)
        for z in range(NZ):
            out_ref[z, c * 32 : (c + 1) * 32, :] = piece


def spread_kernel(got_ref, out_ref, mid_ref):
    got = got_ref[...].astype(F32).reshape(32, 4, 8, 128)
    for q in range(4):
        mid_ref[:, q] = swap_groups([got[:, x] for x in range(NX)], q)
    rows = mid_ref[...].reshape(1024, 128).astype(BF16)
    for y in range(4):
        out_ref[y] = rows


def decode_kernel(w_ref, high_ref, low_ref):
    for y in range(4):
        for k in range(4):
            sent = w_ref[y, k * 256 : (k + 1) * 256, :].astype(F32)
            size = jnp.sqrt(jnp.sqrt(jnp.abs(sent))) * 2.0**-SHIFT
            delta = jnp.where(sent < 0, -size, size)
            high = delta.astype(BF16)
            at = (y // 2) * 1024 + k * 256
            lane = (y % 2) * 128
            high_ref[at : at + 256, lane : lane + 128] = high
            low_ref[at : at + 256, lane : lane + 128] = (delta - high.astype(F32)).astype(BF16)


def forward_kernel(*refs):
    own, pair, rest = refs[:NX], refs[NX : 2 * NX], refs[2 * NX :]
    high_ref, low_ref, at_ref, out_ref, held_ref, sems = rest
    loads = [pltpu.make_async_copy(pair[i], held_ref.at[i], sems.at[i]) for i in range(NX)]
    for load in loads:
        load.start()
    for row in (0, 128):
        if row:
            for load in loads:
                load.wait()
            rows = held_ref[...].reshape(512, 2048)
        else:
            rows = jnp.concatenate([ref[...] for ref in own], axis=0)
        part = jnp.dot(rows, high_ref[...], preferred_element_type=F32)
        part += jnp.dot(rows, low_ref[...], preferred_element_type=F32)
        part = part.astype(BF16)
        for i in range(NX):
            x = (at_ref[0] + BACK[i]) % NX
            out_ref[x, row : row + 128] = part[i * 128 : (i + 1) * 128]


def thirds(value, rows):
    high = value.astype(BF16).astype(F32)
    mid = (value - high).astype(BF16).astype(F32)
    low = value - high - mid
    row = lax.broadcasted_iota(jnp.int32, (rows, value.shape[1]), 0)
    return jnp.where(row == 0, high, jnp.where(row == 1, mid, jnp.where(row == 2, low, 0.0)))


def slope_kernel(part_ref, out_ref, loss_ref):
    diff = part_ref[0].astype(F32)
    for x in range(1, NX):
        diff = diff + part_ref[x].astype(F32)
    slope = diff.astype(BF16)
    for x in range(NX):
        out_ref[x] = slope
    square = diff * diff
    loss_ref[...] = jnp.sum(square[:, :128] + square[:, 128:], axis=0, keepdims=True)


def grad_kernel(*refs):
    own, (held_ref, *rest) = refs[:NX], refs[NX:]
    slope_ref, loss_ref, at_ref, out_ref, s_ref, term_ref = rest
    contract = (((0,), (0,)), ((), ()))
    for i in range(NX):
        x = (at_ref[0] + BACK[i]) % NX
        s_ref[i * 128 : (i + 1) * 128] = slope_ref[x, :128]
        s_ref[512 + i * 128 : 512 + (i + 1) * 128] = slope_ref[x, 128:]
    for k in range(8):
        at = k * 256
        rows = [ref[:, at : at + 256] for ref in own]
        rows += [held_ref[i, :, at : at + 256] for i in range(NX)]
        rows = jnp.concatenate(rows, axis=0)
        term = lax.dot_general(rows, s_ref[...], contract, preferred_element_type=F32)
        for yh in range(2):
            term_ref[(k // 4) * 2 + yh, (k % 4) * 8 : (k % 4 + 1) * 8] = term[
                :, yh * 128 : (yh + 1) * 128
            ].reshape(8, 4, 8, 128)
    loss = thirds(loss_ref[...], 16).astype(BF16)
    for y in range(4):
        term = term_ref[y].reshape(NZ, NC, 4, 8, 128)
        for c in range(NC):
            parts = [term[:, c, q] for q in range(4)]
            for x in range(NX):
                at = place_in_plane(y // 2, c, y % 2, x)
                out_ref[at, :128, :] = swap_groups(parts, x).reshape(128, 128).astype(BF16)
                out_ref[at, 128:, :] = loss


def gather_kernel(got_ref, pat_ref, out_ref, mid_ref):
    loss = got_ref[0, 128:, :].astype(F32)
    for i in range(1, 32):
        loss = loss + got_ref[i, 128:, :].astype(F32)
    loss = jnp.sum(jnp.sum(loss, axis=0, keepdims=True), axis=1, keepdims=True)
    loss = thirds(jnp.broadcast_to(loss, (1, 128)), 16)
    lane = lax.broadcasted_iota(jnp.int32, (16, 128), 1)
    mid_ref[:, 32:, :] = jnp.broadcast_to(jnp.where(lane == 0, loss, 0.0), (NZ, 16, 128))
    group = lane_group((NZ, 8, 128))
    for x in range(NX):
        rows = jnp.zeros((NZ, 8, 128), F32)
        for c in range(NC):
            total = jnp.zeros((128, 128), F32)
            for y in range(4):
                total += got_ref[place_in_plane(y // 2, c, y % 2, x), :128, :].astype(F32)
            total = total.reshape(NZ, 8, 128)
            for i, which in enumerate(kept_rows(pat_ref[c, :, x])):
                kept = jnp.where(which == group.astype(F32), total, 0.0)
                kept += pltpu.roll(kept, 64, 2)
                kept += pltpu.roll(kept, 32, 2)
                rows = jnp.where(group == i * 2 + c, kept, rows)
        mid_ref[:, x * 8 : (x + 1) * 8, :] = rows
    out_ref[...] = mid_ref[...].astype(BF16)


def final_kernel(got_ref, pat_ref, out_ref, loss_ref):
    total = got_ref[0].astype(F32)
    for z in range(1, NZ):
        total = total + got_ref[z].astype(F32)
    loss = jnp.sum(jnp.sum(total[32:], axis=0, keepdims=True), axis=1, keepdims=True)
    loss_ref[...] = loss / (TOKENS * KVW)
    kept = total[:32]
    row = lax.broadcasted_iota(jnp.int32, (32, 128), 0)
    col = lax.broadcasted_iota(jnp.int32, (32, 128), 1)
    spread = jnp.where(col // 4 == row, 1.0, 0.0).astype(BF16)
    wide = jnp.zeros((128, 128), F32)
    for _ in range(3):
        part = kept.astype(BF16)
        kept = kept - part.astype(F32)
        wide += lax.dot_general(
            part, spread, (((0,), (0,)), ((), ())), preferred_element_type=F32
        )
    first, second = kept_rows(pat_ref[...])
    spot = row_of_four(wide[:64].shape)
    grad = jnp.where(spot == first, wide[:64], 0.0) + jnp.where(spot == second, wide[64:], 0.0)
    out_ref[...] = grad / jnp.sqrt(F32(TOKENS))


def ring(step):
    return [(i, (i + step) % NX) for i in range(NX)]


def shards(hidden, norm_gain, teacher_k, student_k, keep_pattern):
    z, yl, core, yh, x = (lax.axis_index(a) for a in AXES)
    place = (z * NYL + yl) * NC + core
    at = jnp.stack([x, core, yl, place, yh]).astype(jnp.int32)
    patterns = keep_pattern.T

    packed, pat = call(
        pack_kernel,
        (shape((NZ, 64, 128), BF16), shape((64, 128), F32)),
        teacher_k.T,
        student_k.T,
        patterns,
        at,
        scratch=[
            pltpu.VMEM((64, 128), BF16),
            pltpu.VMEM((64, 128), BF16),
            pltpu.VMEM((64, 128), jnp.int32),
            pltpu.SemaphoreType.DMA((3,)),
        ],
        far=(0, 1, 2),
        grant=60,
        name="pack",
    )
    got_w = lax.all_to_all(packed.reshape(128, 8, 128), ZCX, 0, 0, tiled=True)

    split = call(
        norm_kernel,
        (shape((128, 2048), BF16),) * NX,
        hidden,
        norm_gain.reshape(64, 128),
        at,
        scratch=[
            pltpu.VMEM((2048, 512), BF16),
            pltpu.VMEM((128, D), BF16),
            pltpu.SemaphoreType.DMA((4,)),
        ],
        flops=2 * 2048 * 512 * 512,
        far=(0,),
        grant=60,
        name="norm",
    )
    own = [split[0]] + [lax.ppermute(split[i], "x", ring(STEP[i])) for i in range(1, NX)]
    pair = [lax.ppermute(piece, "core", [(0, 1), (1, 0)]) for piece in own]

    rows_w = call(
        spread_kernel,
        shape((4, 1024, 128), BF16),
        got_w.reshape(1024, 128),
        scratch=[pltpu.VMEM((32, 4, 8, 128), F32)],
        name="spread",
    )
    all_w = lax.all_to_all(rows_w, Y, 0, 0, tiled=True)
    high, low = call(decode_kernel, (shape((2048, 256), BF16),) * 2, all_w, name="decode")

    late, _ = lax.optimization_barrier((patterns, rows_w))
    own_pat = call(
        choose_kernel,
        shape((NC, NZ, NX, 8, 128), F32),
        late,
        at,
        scratch=[pltpu.VMEM((NZ, NYL, NC, NX, 8, 128), F32)],
        name="choose",
    )

    flops = 2 * 1024 * 2048 * 256
    part, held = call(
        forward_kernel,
        (shape((NX, 256, 256), BF16), shape((NX, 128, 2048), BF16)),
        *own,
        *pair,
        high,
        low,
        at,
        scratch=[pltpu.SemaphoreType.DMA((NX,))],
        flops=2 * flops,
        far=range(NX, 2 * NX),
        name="forward",
    )
    got_part = lax.all_to_all(part, "x", 0, 0, tiled=True)
    slope, loss_part = call(
        slope_kernel, (shape((NX, 256, 256), BF16), shape((1, 128), F32)), got_part, name="slope"
    )
    slopes = lax.all_to_all(slope, "x", 0, 0, tiled=True)

    term = call(
        grad_kernel,
        shape((32, 144, 128), BF16),
        *own,
        held,
        slopes,
        loss_part,
        at,
        scratch=[pltpu.VMEM((1024, 256), BF16), pltpu.VMEM((4, 32, 4, 8, 128), F32)],
        flops=flops,
        name="grad",
    )
    got_term = lax.all_to_all(term, PLANE, 0, 0, tiled=True)
    packed_term = call(
        gather_kernel,
        shape((NZ, 48, 128), BF16),
        got_term,
        own_pat,
        scratch=[pltpu.VMEM((NZ, 48, 128), F32)],
        name="gather",
    )
    got_sum = lax.all_to_all(packed_term, "z", 0, 0, tiled=True)
    grad, loss = call(
        final_kernel,
        (shape((64, 128), F32), shape((1, 1), F32)),
        got_sum,
        pat,
        name="final",
    )
    return grad.T, loss.reshape(())


def solution(mesh):
    fine = Mesh(mesh.devices.reshape(NZ, NYL, NC, NYH, NX), AXES)
    dp, tensor = ("z", "yl", "core"), ("yh", "x")
    in_specs = (P(AXES, None), P(), P(dp, tensor), P(dp, tensor), P(None, tensor))
    out_specs = (P(dp, tensor), P())
    return jax.shard_map(shards, mesh=fine, in_specs=in_specs, out_specs=out_specs, check_vma=False)
```

```python
import jax
import jax.numpy as jnp
from jax import lax
from jax.experimental import pallas as pl
from jax.experimental.pallas import tpu as pltpu
from jax.sharding import Mesh, PartitionSpec as P

F32 = jnp.float32
BF16 = jnp.bfloat16
NZ, NYL, NC, NYH, NX = 16, 2, 2, 2, 4
AXES = ("z", "yl", "core", "yh", "x")
Y = ("yl", "yh")
ZCX = ("z", "core", "x")
PLANE = ("yl", "core", "yh", "x")
D, KVW, TOKENS = 8192, 512, 65536
SHIFT = 34
VMEM = pl.BlockSpec(memory_space=pltpu.VMEM)
SMEM = pl.BlockSpec(memory_space=pltpu.SMEM)
STEP = (0, 2, 1, 3)
BACK = (0, 2, 3, 1)


def call(kernel, out_shape, *args, scratch=(), flops=0, name=None, far=(), grant=24):
    size = sum(a.size * a.dtype.itemsize for a in args)
    for o in jax.tree.leaves(out_shape):
        size += o.size * o.dtype.itemsize
    specs = [SMEM if a.shape == (5,) else VMEM for a in args]
    for i in far:
        specs[i] = pl.BlockSpec(memory_space=pl.ANY)
    return pl.pallas_call(
        kernel,
        out_shape=out_shape,
        in_specs=specs,
        out_specs=jax.tree.map(lambda _: VMEM, out_shape),
        scratch_shapes=list(scratch),
        name=name,
        cost_estimate=pl.CostEstimate(flops=flops, bytes_accessed=size, transcendentals=0),
        compiler_params=pltpu.CompilerParams(vmem_limit_bytes=grant * 1024 * 1024),
    )(*args)


def shape(dims, dtype):
    return jax.ShapeDtypeStruct(dims, dtype)


def lane_group(dims):
    return lax.broadcasted_iota(jnp.int32, dims, len(dims) - 1) // 32


def place_in_plane(yl, c, yh, x):
    return ((yl * NC + c) * NYH + yh) * NX + x


def swap_groups(parts, place):
    total = None
    for b, part in enumerate(parts):
        shift = (b - place) * 32 % 128
        moved = pltpu.roll(part, shift, part.ndim - 1) if shift else part
        here = jnp.where(lane_group(part.shape) == b, moved, 0.0)
        total = here if total is None else total + here
    return total


def kept_rows(pat):
    first = jnp.where(pat > 2.5, 1.0, 0.0) + jnp.where(pat > 4.5, 1.0, 0.0)
    second = jnp.where(pat < 2.5, pat + 1.0, jnp.where(pat < 3.5, 2.0, 3.0))
    return first, second


def row_of_four(dims):
    return (lax.broadcasted_iota(jnp.int32, dims, 1) % 4).astype(F32)


def shuffled(place):
    return place % 4 * 8 + place // 4


def norm_kernel(x_hbm, gain_ref, at_ref, *rest):
    outs, (rows_ref, x_ref, sems) = rest[:NX], rest[NX:]
    me = at_ref[0]
    cuts = [pl.ds(i * 2048, 2048) for i in range(4)]
    loads = [
        pltpu.make_async_copy(x_hbm.at[:, cut], x_ref.at[:, cut], sems.at[i])
        for i, cut in enumerate(cuts)
    ]
    for load in loads:
        load.start()
    total = jnp.zeros((128, 512), F32)
    for g in range(16):
        if g % 4 == 0:
            loads[g // 4].wait()
        part = x_ref[:, g * 512 : (g + 1) * 512].astype(F32)
        total += part * part
    factor = lax.rsqrt(jnp.sum(total, axis=1, keepdims=True) / D + 1e-05)
    gain = gain_ref[...].astype(F32)
    for yl in range(2):
        for m in range(8):
            tile = yl * 8 + m
            for b in range(4):
                block = 8 * m + 4 * (b // 2) + 2 * yl + b % 2
                part = x_ref[:, block * 128 : (block + 1) * 128].astype(F32)
                rows_ref[tile * 128 : (tile + 1) * 128, b * 128 : (b + 1) * 128] = (
                    part * factor * gain[block : block + 1, :]
                ).astype(BF16)
    src = lax.broadcasted_iota(jnp.int32, (512, 512), 0)
    dst = lax.broadcasted_iota(jnp.int32, (512, 512), 1)
    ahead = (src // 32 + NX - me) % NX
    goal = ahead * 128 + src // 128 * 32 + shuffled(src % 32)
    move = jnp.where(goal == dst, 1.0, 0.0).astype(BF16)
    for tile in range(16):
        seg = jnp.dot(
            rows_ref[tile * 128 : (tile + 1) * 128, :], move, preferred_element_type=F32
        ).astype(BF16)
        for i, x in enumerate(STEP):
            outs[i][:, tile * 128 : (tile + 1) * 128] = seg[:, x * 128 : (x + 1) * 128]


def choose_kernel(pat_ref, at_ref, out_ref, pick_ref):
    col = lax.broadcasted_iota(jnp.int32, (64, 128), 0)
    lane = lax.broadcasted_iota(jnp.int32, (64, 128), 1)
    pick = jnp.where(col - at_ref[1] * 32 == lane % 32, 1.0, 0.0).astype(BF16)
    chosen = lax.dot_general(
        pat_ref[...].astype(F32).astype(BF16),
        pick,
        (((0,), (0,)), ((), ())),
        preferred_element_type=F32,
    )
    pick_ref[...] = chosen.reshape(NZ, NYL, NC, NX, 8, 128)
    group = lane_group((32, 128))
    for x in range(NX):
        for yl in range(NYL):
            rows = pick_ref[:, yl, :, x].reshape(8, 32, 128)
            for tile in range(2):
                total = jnp.zeros((32, 128), F32)
                for b in range(4):
                    total = jnp.where(group == b, rows[tile * 4 + b], total)
                out_ref[x, yl * 32 : (yl + 1) * 32, tile * 128 : (tile + 1) * 128] = total.astype(BF16)


def pack_kernel(teacher_hbm, student_hbm, pat_hbm, at_ref, out_ref, rows_ref, *scratch):
    teacher_ref, student_ref, pat_ref, sems = scratch
    place = at_ref[3]
    window = pl.ds(pl.multiple_of(place // 4 * 128, 128), 128)
    loads = [
        pltpu.make_async_copy(pat_hbm.at[:, window], pat_ref, sems.at[0]),
        pltpu.make_async_copy(teacher_hbm, teacher_ref, sems.at[1]),
        pltpu.make_async_copy(student_hbm, student_ref, sems.at[2]),
    ]
    for load in loads:
        load.start()
    for load in loads:
        load.wait()
    row = lax.broadcasted_iota(jnp.int32, (128, 128), 0)
    col = lax.broadcasted_iota(jnp.int32, (128, 128), 1)
    spread = jnp.where(col // 4 + place % 4 * 32 == row, 1.0, 0.0).astype(BF16)
    pat = jnp.dot(pat_ref[...].astype(F32).astype(BF16), spread, preferred_element_type=F32)
    rows_ref[...] = pat
    first, second = kept_rows(pat)
    spot = row_of_four(pat.shape)
    keep = jnp.where((spot == first) | (spot == second), 1.0, 0.0)
    delta = student_ref[...].astype(F32) * keep - teacher_ref[...].astype(F32)
    delta = delta * 2.0**SHIFT
    delta = ((delta * jnp.abs(delta)) * (delta * delta)).astype(BF16)
    row = lax.broadcasted_iota(jnp.int32, (64, 128), 0)
    col = lax.broadcasted_iota(jnp.int32, (64, 128), 1)
    widen = jnp.where(row == col, 1.0, 0.0).astype(BF16)
    rows = lax.dot_general(
        delta, widen, (((0,), (0,)), ((), ())), preferred_element_type=F32
    ).astype(BF16)
    dst = lax.broadcasted_iota(jnp.int32, (128, 128), 0)
    src = lax.broadcasted_iota(jnp.int32, (128, 128), 1)
    move = jnp.where(src // 32 * 32 + shuffled(src % 32) == dst, 1.0, 0.0).astype(BF16)
    wide = jnp.dot(move, rows, preferred_element_type=F32).reshape(4, 4, 8, 128)
    for c in range(NC):
        piece = swap_groups([wide[:, q] for q in range(4)], c).reshape(32, 128).astype(BF16)
        for z in range(NZ):
            out_ref[z, c * 32 : (c + 1) * 32, :] = piece


def spread_kernel(got_ref, out_ref, mid_ref):
    got = got_ref[...].astype(F32).reshape(32, 4, 8, 128)
    for q in range(4):
        mid_ref[:, q] = swap_groups([got[:, x] for x in range(NX)], q)
    rows = mid_ref[...].reshape(1024, 128).astype(BF16)
    for y in range(4):
        out_ref[y] = rows


def decode_kernel(w_ref, high_ref, low_ref):
    for y in range(4):
        for k in range(4):
            sent = w_ref[y, k * 256 : (k + 1) * 256, :].astype(F32)
            size = jnp.sqrt(jnp.sqrt(jnp.abs(sent))) * 2.0**-SHIFT
            delta = jnp.where(sent < 0, -size, size)
            high = delta.astype(BF16)
            at = (y // 2) * 1024 + k * 256
            lane = (y % 2) * 128
            high_ref[at : at + 256, lane : lane + 128] = high
            low_ref[at : at + 256, lane : lane + 128] = (delta - high.astype(F32)).astype(BF16)


def forward_kernel(*refs):
    own, pair, rest = refs[:NX], refs[NX : 2 * NX], refs[2 * NX :]
    high_ref, low_ref, own_pat, other_pat, at_ref, out_ref, held_ref, sems = rest
    loads = [pltpu.make_async_copy(pair[i], held_ref.at[i], sems.at[i]) for i in range(NX)]
    for load in loads:
        load.start()
    for x in range(NX):
        out_ref[x, 256:320] = own_pat[x]
        out_ref[x, 320:] = other_pat[x]
    for row in (0, 128):
        if row:
            for load in loads:
                load.wait()
            rows = held_ref[...].reshape(512, 2048)
        else:
            rows = jnp.concatenate([ref[...] for ref in own], axis=0)
        part = jnp.dot(rows, high_ref[...], preferred_element_type=F32)
        part += jnp.dot(rows, low_ref[...], preferred_element_type=F32)
        part = part.astype(BF16)
        for i in range(NX):
            x = (at_ref[0] + BACK[i]) % NX
            out_ref[x, row : row + 128] = part[i * 128 : (i + 1) * 128]


def thirds(value, rows):
    high = value.astype(BF16).astype(F32)
    mid = (value - high).astype(BF16).astype(F32)
    low = value - high - mid
    row = lax.broadcasted_iota(jnp.int32, (rows, value.shape[1]), 0)
    return jnp.where(row == 0, high, jnp.where(row == 1, mid, jnp.where(row == 2, low, 0.0)))


def slope_kernel(part_ref, out_ref, loss_ref, pat_ref):
    diff = part_ref[0, :256].astype(F32)
    for x in range(1, NX):
        diff = diff + part_ref[x, :256].astype(F32)
    slope = diff.astype(BF16)
    for x in range(NX):
        out_ref[x] = slope
    square = diff * diff
    loss_ref[...] = jnp.sum(square[:, :128] + square[:, 128:], axis=0, keepdims=True)
    group = lane_group((32, 128))
    for part in range(4):
        for b in range(8):
            total = jnp.zeros((32, 128), F32)
            for x in range(NX):
                sent = part_ref[x, 256 + part * 32 : 288 + part * 32, b // 4 * 128 : b // 4 * 128 + 128]
                shift = (x - b) % 4 * 32
                sent = sent.astype(F32)
                sent = pltpu.roll(sent, shift, 1) if shift else sent
                total = jnp.where(group == x, sent, total)
            pat_ref[part, b * 32 : (b + 1) * 32, :] = total


def grad_kernel(*refs):
    own, (held_ref, *rest) = refs[:NX], refs[NX:]
    pat_ref, slope_ref, loss_ref, at_ref, out_ref, s_ref, term_ref = rest
    contract = (((0,), (0,)), ((), ()))
    for i in range(NX):
        x = (at_ref[0] + BACK[i]) % NX
        s_ref[i * 128 : (i + 1) * 128] = slope_ref[x, :128]
        s_ref[512 + i * 128 : 512 + (i + 1) * 128] = slope_ref[x, 128:]
    for k in range(8):
        at = k * 256
        rows = [ref[:, at : at + 256] for ref in own]
        rows += [held_ref[i, :, at : at + 256] for i in range(NX)]
        rows = jnp.concatenate(rows, axis=0)
        term = lax.dot_general(rows, s_ref[...], contract, preferred_element_type=F32)
        for yh in range(2):
            term_ref[(k // 4) * 2 + yh, (k % 4) * 8 : (k % 4 + 1) * 8] = term[
                :, yh * 128 : (yh + 1) * 128
            ].reshape(8, 4, 8, 128)
    loss = thirds(loss_ref[...], 16).astype(BF16)
    for part in range(4):
        yl = part % 2
        yh = at_ref[4] if part < 2 else 1 - at_ref[4]
        y = yl * NYH + yh
        which = kept_rows(pat_ref[part].reshape(32, 8, 128))
        kept = [jnp.zeros((32, 8, 128), F32) for _ in which]
        for k in range(4):
            for i in range(2):
                kept[i] += jnp.where(which[i] == k, term_ref[y, :, k], 0.0)
        kept = [rows.reshape(2, 8, NC, 8, 128) for rows in kept]
        for c in range(NC):
            parts = [kept[i][half, :, c] for half in range(2) for i in range(2)]
            for x in range(NX):
                at = place_in_plane(yl, c, yh, x)
                out_ref[at, :64, :] = swap_groups(parts, x).reshape(64, 128).astype(BF16)
                out_ref[at, 64:, :] = loss


def gather_kernel(got_ref, out_ref, mid_ref):
    loss = got_ref[0, 64:, :].astype(F32)
    for i in range(1, 32):
        loss = loss + got_ref[i, 64:, :].astype(F32)
    loss = jnp.sum(jnp.sum(loss, axis=0, keepdims=True), axis=1, keepdims=True)
    loss = thirds(jnp.broadcast_to(loss, (1, 128)), 16)
    lane = lax.broadcasted_iota(jnp.int32, (16, 128), 1)
    mid_ref[:, 32:, :] = jnp.broadcast_to(jnp.where(lane == 0, loss, 0.0), (NZ, 16, 128))
    group = lane_group((8, 8, 128))
    for x in range(NX):
        sums = []
        for c in range(NC):
            total = jnp.zeros((64, 128), F32)
            for y in range(4):
                total += got_ref[place_in_plane(y // 2, c, y % 2, x), :64, :].astype(F32)
            sums.append(total.reshape(8, 8, 128))
        for half in range(2):
            rows = jnp.zeros((8, 8, 128), F32)
            for kept in range(2):
                for c in range(NC):
                    goal = kept * 2 + c
                    shift = (goal - half * 2 - kept) % 4 * 32
                    moved = pltpu.roll(sums[c], shift, 2) if shift else sums[c]
                    rows = jnp.where(group == goal, moved, rows)
            mid_ref[half * 8 : (half + 1) * 8, x * 8 : (x + 1) * 8, :] = rows
    out_ref[...] = mid_ref[...].astype(BF16)


def final_kernel(got_ref, pat_ref, out_ref, loss_ref):
    total = got_ref[0].astype(F32)
    for z in range(1, NZ):
        total = total + got_ref[z].astype(F32)
    loss = jnp.sum(jnp.sum(total[32:], axis=0, keepdims=True), axis=1, keepdims=True)
    loss_ref[...] = loss / (TOKENS * KVW)
    kept = total[:32]
    row = lax.broadcasted_iota(jnp.int32, (32, 128), 0)
    col = lax.broadcasted_iota(jnp.int32, (32, 128), 1)
    spread = jnp.where(col // 4 == row, 1.0, 0.0).astype(BF16)
    wide = jnp.zeros((128, 128), F32)
    for _ in range(3):
        part = kept.astype(BF16)
        kept = kept - part.astype(F32)
        wide += lax.dot_general(
            part, spread, (((0,), (0,)), ((), ())), preferred_element_type=F32
        )
    first, second = kept_rows(pat_ref[...])
    spot = row_of_four(wide[:64].shape)
    grad = jnp.where(spot == first, wide[:64], 0.0) + jnp.where(spot == second, wide[64:], 0.0)
    out_ref[...] = grad / jnp.sqrt(F32(TOKENS))


def ring(step):
    return [(i, (i + step) % NX) for i in range(NX)]


def shards(hidden, norm_gain, teacher_k, student_k, keep_pattern):
    z, yl, core, yh, x = (lax.axis_index(a) for a in AXES)
    place = (z * NYL + yl) * NC + core
    at = jnp.stack([x, core, yl, place, yh]).astype(jnp.int32)
    patterns = keep_pattern.T

    packed, pat = call(
        pack_kernel,
        (shape((NZ, 64, 128), BF16), shape((64, 128), F32)),
        teacher_k.T,
        student_k.T,
        patterns,
        at,
        scratch=[
            pltpu.VMEM((64, 128), BF16),
            pltpu.VMEM((64, 128), BF16),
            pltpu.VMEM((64, 128), jnp.int32),
            pltpu.SemaphoreType.DMA((3,)),
        ],
        far=(0, 1, 2),
        grant=60,
        name="pack",
    )
    got_w = lax.all_to_all(packed.reshape(128, 8, 128), ZCX, 0, 0, tiled=True)

    split = call(
        norm_kernel,
        (shape((128, 2048), BF16),) * NX,
        hidden,
        norm_gain.reshape(64, 128),
        at,
        scratch=[
            pltpu.VMEM((2048, 512), BF16),
            pltpu.VMEM((128, D), BF16),
            pltpu.SemaphoreType.DMA((4,)),
        ],
        flops=2 * 2048 * 512 * 512,
        far=(0,),
        grant=60,
        name="norm",
    )
    own = [split[0]] + [lax.ppermute(split[i], "x", ring(STEP[i])) for i in range(1, NX)]
    rows_w = call(
        spread_kernel,
        shape((4, 1024, 128), BF16),
        got_w.reshape(1024, 128),
        scratch=[pltpu.VMEM((32, 4, 8, 128), F32)],
        name="spread",
    )
    all_w = lax.all_to_all(rows_w, Y, 0, 0, tiled=True)

    late, _ = lax.optimization_barrier((patterns, rows_w))
    own_pat = call(
        choose_kernel,
        shape((NX, 64, 256), BF16),
        late,
        at,
        scratch=[pltpu.VMEM((NZ, NYL, NC, NX, 8, 128), F32)],
        name="choose",
    )
    other_pat = lax.ppermute(own_pat, "yh", [(0, 1), (1, 0)])
    own[2], own[3], other_pat = lax.optimization_barrier((own[2], own[3], other_pat))
    pair = [lax.ppermute(piece, "core", [(0, 1), (1, 0)]) for piece in own]

    high, low = call(decode_kernel, (shape((2048, 256), BF16),) * 2, all_w, name="decode")

    flops = 2 * 1024 * 2048 * 256
    part, held = call(
        forward_kernel,
        (shape((NX, 384, 256), BF16), shape((NX, 128, 2048), BF16)),
        *own,
        *pair,
        high,
        low,
        own_pat,
        other_pat,
        at,
        scratch=[pltpu.SemaphoreType.DMA((NX,))],
        flops=2 * flops,
        far=range(NX, 2 * NX),
        name="forward",
    )
    got_part = lax.all_to_all(part, "x", 0, 0, tiled=True)
    slope, loss_part, pats = call(
        slope_kernel,
        (shape((NX, 256, 256), BF16), shape((1, 128), F32), shape((4, 256, 128), F32)),
        got_part,
        name="slope",
    )
    slopes = lax.all_to_all(slope, "x", 0, 0, tiled=True)

    term = call(
        grad_kernel,
        shape((32, 80, 128), BF16),
        *own,
        held,
        pats,
        slopes,
        loss_part,
        at,
        scratch=[pltpu.VMEM((1024, 256), BF16), pltpu.VMEM((4, 32, 4, 8, 128), F32)],
        flops=flops,
        name="grad",
    )
    got_term = lax.all_to_all(term, PLANE, 0, 0, tiled=True)
    packed_term = call(
        gather_kernel,
        shape((NZ, 48, 128), BF16),
        got_term,
        scratch=[pltpu.VMEM((NZ, 48, 128), F32)],
        name="gather",
    )
    got_sum = lax.all_to_all(packed_term, "z", 0, 0, tiled=True)
    grad, loss = call(
        final_kernel,
        (shape((64, 128), F32), shape((1, 1), F32)),
        got_sum,
        pat,
        name="final",
    )
    return grad.T, loss.reshape(())


def solution(mesh):
    fine = Mesh(mesh.devices.reshape(NZ, NYL, NC, NYH, NX), AXES)
    dp, tensor = ("z", "yl", "core"), ("yh", "x")
    in_specs = (P(AXES, None), P(), P(dp, tensor), P(dp, tensor), P(None, tensor))
    out_specs = (P(dp, tensor), P())
    return jax.shard_map(shards, mesh=fine, in_specs=in_specs, out_specs=out_specs, check_vma=False)
```

```python
import jax
import jax.numpy as jnp
from jax import lax
from jax.experimental import pallas as pl
from jax.experimental.pallas import tpu as pltpu
from jax.sharding import Mesh, PartitionSpec as P

F32 = jnp.float32
BF16 = jnp.bfloat16
NZ, NYL, NC, NYH, NX = 16, 2, 2, 2, 4
AXES = ("z", "yl", "core", "yh", "x")
Y = ("yl", "yh")
ZCX = ("z", "core", "x")
PLANE = ("yl", "core", "yh", "x")
D, KVW, TOKENS = 8192, 512, 65536
SHIFT = 34
VMEM = pl.BlockSpec(memory_space=pltpu.VMEM)
SMEM = pl.BlockSpec(memory_space=pltpu.SMEM)
STEP = (0, 2, 1, 3)
BACK = (0, 2, 3, 1)


def call(kernel, out_shape, *args, scratch=(), flops=0, name=None, far=(), out_far=False, grant=24):
    size = sum(a.size * a.dtype.itemsize for a in args)
    for o in jax.tree.leaves(out_shape):
        size += o.size * o.dtype.itemsize
    specs = [SMEM if a.shape == (5,) else VMEM for a in args]
    for i in far:
        specs[i] = pl.BlockSpec(memory_space=pl.ANY)
    return pl.pallas_call(
        kernel,
        out_shape=out_shape,
        in_specs=specs,
        out_specs=jax.tree.map(
            lambda _: pl.BlockSpec(memory_space=pl.ANY) if out_far else VMEM, out_shape
        ),
        scratch_shapes=list(scratch),
        name=name,
        cost_estimate=pl.CostEstimate(flops=flops, bytes_accessed=size, transcendentals=0),
        compiler_params=pltpu.CompilerParams(vmem_limit_bytes=grant * 1024 * 1024),
    )(*args)


def shape(dims, dtype):
    return jax.ShapeDtypeStruct(dims, dtype)


def lane_group(dims):
    return lax.broadcasted_iota(jnp.int32, dims, len(dims) - 1) // 32


def place_in_plane(yl, c, yh, x):
    return ((yl * NC + c) * NYH + yh) * NX + x


def swap_groups(parts, place):
    total = None
    for b, part in enumerate(parts):
        shift = (b - place) * 32 % 128
        moved = pltpu.roll(part, shift, part.ndim - 1) if shift else part
        here = jnp.where(lane_group(part.shape) == b, moved, 0.0)
        total = here if total is None else total + here
    return total


def swap_all(parts):
    axis = parts[0].ndim - 1
    group = lane_group(parts[0].shape)
    low, even = group < 2, group % 2 == 0
    half = []
    for a, b in ((0, 2), (1, 3)):
        half.append(jnp.where(low, parts[a], pltpu.roll(parts[b], 64, axis)))
        half.append(jnp.where(low, pltpu.roll(parts[a], 64, axis), parts[b]))
    out = []
    for a, b in ((half[0], half[2]), (half[1], half[3])):
        out.append(jnp.where(even, a, pltpu.roll(b, 32, axis)))
        out.append(jnp.where(even, pltpu.roll(a, 96, axis), b))
    return out


def kept_rows(pat):
    first = jnp.where(pat > 2.5, 1.0, 0.0) + jnp.where(pat > 4.5, 1.0, 0.0)
    second = jnp.where(pat < 2.5, pat + 1.0, jnp.where(pat < 3.5, 2.0, 3.0))
    return first, second


def row_of_four(dims):
    return (lax.broadcasted_iota(jnp.int32, dims, 1) % 4).astype(F32)


def shuffled(place):
    return place % 4 * 8 + place // 4


def norm_kernel(x_hbm, gain_ref, at_ref, *rest):
    outs, (x_ref, move_ref, split_ref, sems, out_sems) = rest[:NX], rest[NX:]
    loads = [
        pltpu.make_async_copy(x_hbm.at[:, cut], x_ref.at[:, cut], sems.at[i])
        for i, cut in enumerate(pl.ds(i * 1024, 1024) for i in range(8))
    ]
    for load in loads:
        load.start()
    src = lax.broadcasted_iota(jnp.int32, (512, 128), 0)
    dst = lax.broadcasted_iota(jnp.int32, (512, 128), 1)
    goal = ((src >> 5 & 3) << 7) + (src >> 7 << 5) + ((src & 3) << 3) + (src >> 2 & 7)
    for x in range(NX):
        move_ref[:, x * 128 : (x + 1) * 128] = jnp.where(goal == dst + x * 128, 1.0, 0.0).astype(BF16)
    total = jnp.zeros((128, 128), F32)
    for g in range(64):
        if g % 8 == 0:
            loads[g // 8].wait()
        part = x_ref[:, g * 128 : (g + 1) * 128].astype(F32)
        total += part * part
    factor = lax.rsqrt(jnp.sum(total, axis=1, keepdims=True) / D + 1e-05)
    factor = jnp.broadcast_to(factor, (128, 128))
    gain = gain_ref[...].astype(F32)
    stores = []
    for yl in range(2):
        for m in range(8):
            tile = yl * 8 + m
            parts = []
            for b in range(4):
                block = 8 * m + 4 * (b // 2) + 2 * yl + b % 2
                part = x_ref[:, block * 128 : (block + 1) * 128].astype(F32)
                parts.append((part * factor * gain[block : block + 1, :]).astype(BF16))
            parts = jnp.concatenate(parts, axis=1)
            seg = jnp.dot(parts, move_ref[...], preferred_element_type=F32).astype(BF16)
            for x in range(NX):
                split_ref[x, :, tile * 128 : (tile + 1) * 128] = seg[:, x * 128 : (x + 1) * 128]
        for i in range(NX):
            cut = pl.ds(yl * 1024, 1024)
            piece = split_ref.at[(at_ref[0] + STEP[i]) % NX]
            stores.append(
                pltpu.make_async_copy(piece.at[:, cut], outs[i].at[:, cut], out_sems.at[yl * NX + i])
            )
            stores[-1].start()
    for store in stores:
        store.wait()


def choose_kernel(pat_ref, at_ref, out_ref, pick_ref):
    pats = pat_ref[...].astype(F32).astype(BF16)
    col = lax.broadcasted_iota(jnp.int32, (64, 128), 0)
    lane = lax.broadcasted_iota(jnp.int32, (64, 128), 1)
    for c in range(NC):
        pick = jnp.where(col - c * 32 == lane % 32, 1.0, 0.0).astype(BF16)
        chosen = lax.dot_general(pats, pick, (((0,), (0,)), ((), ())), preferred_element_type=F32)
        pick_ref[...] = chosen.reshape(NZ, NYL, NC, NX, 8, 128)
        out_ref[c] = pick_ref[:, at_ref[2], at_ref[1]]


def pack_kernel(teacher_hbm, student_hbm, pat_hbm, at_ref, out_ref, rows_ref, *scratch):
    teacher_ref, student_ref, pat_ref, sems = scratch
    place = at_ref[3]
    window = pl.ds(pl.multiple_of(place // 4 * 128, 128), 128)
    loads = [
        pltpu.make_async_copy(pat_hbm.at[:, window], pat_ref, sems.at[0]),
        pltpu.make_async_copy(teacher_hbm, teacher_ref, sems.at[1]),
        pltpu.make_async_copy(student_hbm, student_ref, sems.at[2]),
    ]
    for load in loads:
        load.start()
    for load in loads:
        load.wait()
    row = lax.broadcasted_iota(jnp.int32, (128, 128), 0)
    col = lax.broadcasted_iota(jnp.int32, (128, 128), 1)
    spread = jnp.where(col // 4 + place % 4 * 32 == row, 1.0, 0.0).astype(BF16)
    pat = jnp.dot(pat_ref[...].astype(F32).astype(BF16), spread, preferred_element_type=F32)
    rows_ref[...] = pat
    first, second = kept_rows(pat)
    spot = row_of_four(pat.shape)
    keep = jnp.where((spot == first) | (spot == second), 1.0, 0.0)
    delta = student_ref[...].astype(F32) * keep - teacher_ref[...].astype(F32)
    delta = delta * 2.0**SHIFT
    delta = ((delta * jnp.abs(delta)) * (delta * delta)).astype(BF16)
    dst = lax.broadcasted_iota(jnp.int32, (128, 128), 0)
    src = lax.broadcasted_iota(jnp.int32, (128, 128), 1)
    move = jnp.where(src // 32 * 32 + shuffled(src % 32) == dst, 1.0, 0.0).astype(BF16)
    delta = jnp.concatenate([delta, jnp.zeros_like(delta)], axis=0)
    wide = lax.dot_general(
        move, delta, (((1,), (1,)), ((), ())), preferred_element_type=F32
    ).reshape(4, 4, 8, 128)
    for c in range(NC):
        piece = swap_groups([wide[:, q] for q in range(4)], c).reshape(32, 128).astype(BF16)
        for z in range(NZ):
            out_ref[z, c * 32 : (c + 1) * 32, :] = piece


def spread_kernel(got_ref, out_ref, mid_ref):
    got = got_ref[...].astype(F32).reshape(32, 4, 8, 128)
    for q, rows in enumerate(swap_all([got[:, x] for x in range(NX)])):
        mid_ref[:, q] = rows
    rows = mid_ref[...].reshape(1024, 128).astype(BF16)
    for y in range(4):
        out_ref[y] = rows


def decode_kernel(w_ref, high_ref, low_ref):
    for y in range(4):
        for k in range(4):
            sent = w_ref[y, k * 256 : (k + 1) * 256, :].astype(F32)
            size = lax.rsqrt(lax.rsqrt(jnp.abs(sent))) * 2.0**-SHIFT
            delta = jnp.where(sent < 0, -size, size)
            high = delta.astype(BF16)
            at = (y // 2) * 1024 + k * 256
            lane = (y % 2) * 128
            high_ref[at : at + 256, lane : lane + 128] = high
            low_ref[at : at + 256, lane : lane + 128] = (delta - high.astype(F32)).astype(BF16)


def forward_kernel(*refs):
    own, pair, rest = refs[:NX], refs[NX : 2 * NX], refs[2 * NX :]
    high_ref, low_ref, at_ref, out_ref, held_ref, sems = rest
    loads = [pltpu.make_async_copy(pair[i], held_ref.at[i], sems.at[i]) for i in range(NX)]
    for load in loads:
        load.start()
    for row in (0, 128):
        for i in range(NX):
            if row:
                loads[i].wait()
            rows = held_ref[i] if row else own[i][...]
            part = jnp.dot(rows, high_ref[...], preferred_element_type=F32)
            part += jnp.dot(rows, low_ref[...], preferred_element_type=F32)
            out_ref[(at_ref[0] + BACK[i]) % NX, row : row + 128] = part.astype(BF16)


def thirds(value, rows):
    high = value.astype(BF16).astype(F32)
    mid = (value - high).astype(BF16).astype(F32)
    low = value - high - mid
    row = lax.broadcasted_iota(jnp.int32, (rows, value.shape[1]), 0)
    return jnp.where(row == 0, high, jnp.where(row == 1, mid, jnp.where(row == 2, low, 0.0)))


def slope_kernel(part_ref, out_ref, loss_ref):
    diff = part_ref[0].astype(F32)
    for x in range(1, NX):
        diff = diff + part_ref[x].astype(F32)
    slope = diff.astype(BF16)
    for x in range(NX):
        out_ref[x] = slope
    square = diff * diff
    loss_ref[...] = jnp.sum(square[:, :128] + square[:, 128:], axis=0, keepdims=True)


def grad_kernel(*refs):
    own, (held_ref, *rest) = refs[:NX], refs[NX:]
    slope_ref, loss_ref, at_ref, out_ref, s_ref, term_ref = rest
    contract = (((0,), (0,)), ((), ()))
    for i in range(NX):
        x = (at_ref[0] + BACK[i]) % NX
        s_ref[i * 128 : (i + 1) * 128] = slope_ref[x, :128]
        s_ref[512 + i * 128 : 512 + (i + 1) * 128] = slope_ref[x, 128:]
    for k in range(8):
        at = k * 256
        rows = [ref[:, at : at + 256] for ref in own]
        rows += [held_ref[i, :, at : at + 256] for i in range(NX)]
        rows = jnp.concatenate(rows, axis=0)
        term = lax.dot_general(rows, s_ref[...], contract, preferred_element_type=F32)
        for yh in range(2):
            term_ref[(k // 4) * 2 + yh, (k % 4) * 8 : (k % 4 + 1) * 8] = term[
                :, yh * 128 : (yh + 1) * 128
            ].reshape(8, 4, 8, 128)
    loss = thirds(loss_ref[...], 16).astype(BF16)
    for y in range(4):
        term = term_ref[y].reshape(NZ, NC, 4, 8, 128)
        for c in range(NC):
            for x, rows in enumerate(swap_all([term[:, c, q] for q in range(4)])):
                at = place_in_plane(y // 2, c, y % 2, x)
                out_ref[at, :128, :] = rows.reshape(128, 128).astype(BF16)
                out_ref[at, 128:, :] = loss


def gather_kernel(got_ref, pat_ref, out_ref, mid_ref):
    loss = got_ref[0, 128:, :].astype(F32)
    for i in range(1, 32):
        loss = loss + got_ref[i, 128:, :].astype(F32)
    loss = jnp.sum(jnp.sum(loss, axis=0, keepdims=True), axis=1, keepdims=True)
    loss = thirds(jnp.broadcast_to(loss, (1, 128)), 16)
    lane = lax.broadcasted_iota(jnp.int32, (16, 128), 1)
    mid_ref[:, 32:, :] = jnp.broadcast_to(jnp.where(lane == 0, loss, 0.0), (NZ, 16, 128))
    group = lane_group((NZ, 8, 128))
    for x in range(NX):
        rows = jnp.zeros((NZ, 8, 128), F32)
        for c in range(NC):
            total = jnp.zeros((128, 128), F32)
            for y in range(4):
                total += got_ref[place_in_plane(y // 2, c, y % 2, x), :128, :].astype(F32)
            total = total.reshape(NZ, 8, 128)
            for i, which in enumerate(kept_rows(pat_ref[c, :, x])):
                kept = jnp.where(which == group.astype(F32), total, 0.0)
                kept += pltpu.roll(kept, 64, 2)
                kept += pltpu.roll(kept, 32, 2)
                rows = jnp.where(group == i * 2 + c, kept, rows)
        mid_ref[:, x * 8 : (x + 1) * 8, :] = rows
    out_ref[...] = mid_ref[...].astype(BF16)


def final_kernel(got_ref, pat_ref, out_ref, loss_ref):
    total = got_ref[0].astype(F32)
    for z in range(1, NZ):
        total = total + got_ref[z].astype(F32)
    loss = jnp.sum(jnp.sum(total[32:], axis=0, keepdims=True), axis=1, keepdims=True)
    loss_ref[...] = loss / (TOKENS * KVW)
    kept = total[:32]
    row = lax.broadcasted_iota(jnp.int32, (32, 128), 0)
    col = lax.broadcasted_iota(jnp.int32, (32, 128), 1)
    spread = jnp.where(col // 4 == row, 1.0, 0.0).astype(BF16)
    wide = jnp.zeros((128, 128), F32)
    for _ in range(3):
        part = kept.astype(BF16)
        kept = kept - part.astype(F32)
        wide += lax.dot_general(
            part, spread, (((0,), (0,)), ((), ())), preferred_element_type=F32
        )
    first, second = kept_rows(pat_ref[...])
    spot = row_of_four(wide[:64].shape)
    grad = jnp.where(spot == first, wide[:64], 0.0) + jnp.where(spot == second, wide[64:], 0.0)
    out_ref[...] = grad / jnp.sqrt(F32(TOKENS))


def ring(step):
    return [(i, (i + step) % NX) for i in range(NX)]


def shards(hidden, norm_gain, teacher_k, student_k, keep_pattern):
    z, yl, core, yh, x = (lax.axis_index(a) for a in AXES)
    place = (z * NYL + yl) * NC + core
    at = jnp.stack([x, core, yl, place, yh]).astype(jnp.int32)
    patterns = keep_pattern.T

    packed, pat = call(
        pack_kernel,
        (shape((NZ, 64, 128), BF16), shape((64, 128), F32)),
        teacher_k.T,
        student_k.T,
        patterns,
        at,
        scratch=[
            pltpu.VMEM((64, 128), BF16),
            pltpu.VMEM((64, 128), BF16),
            pltpu.VMEM((64, 128), jnp.int32),
            pltpu.SemaphoreType.DMA((3,)),
        ],
        far=(0, 1, 2),
        grant=60,
        name="pack",
    )
    got_w = lax.all_to_all(packed.reshape(128, 8, 128), ZCX, 0, 0, tiled=True)

    split = call(
        norm_kernel,
        (shape((128, 2048), BF16),) * NX,
        hidden,
        norm_gain.reshape(64, 128),
        at,
        scratch=[
            pltpu.VMEM((128, D), BF16),
            pltpu.VMEM((512, 512), BF16),
            pltpu.VMEM((NX, 128, 2048), BF16),
            pltpu.SemaphoreType.DMA((8,)),
            pltpu.SemaphoreType.DMA((2 * NX,)),
        ],
        flops=2 * 2048 * 512 * 512,
        far=(0,),
        out_far=True,
        grant=60,
        name="norm",
    )
    own = [split[0]] + [lax.ppermute(split[i], "x", ring(STEP[i])) for i in range(1, NX)]
    rows_w = call(
        spread_kernel,
        shape((4, 1024, 128), BF16),
        got_w.reshape(1024, 128),
        scratch=[pltpu.VMEM((32, 4, 8, 128), F32)],
        name="spread",
    )
    all_w = lax.all_to_all(rows_w, Y, 0, 0, tiled=True)

    late, _ = lax.optimization_barrier((patterns, rows_w))
    own_pat = call(
        choose_kernel,
        shape((NC, NZ, NX, 8, 128), F32),
        late,
        at,
        scratch=[pltpu.VMEM((NZ, NYL, NC, NX, 8, 128), F32)],
        name="choose",
    )
    own[2], own_pat = lax.optimization_barrier((own[2], own_pat))
    pair = [lax.ppermute(piece, "core", [(0, 1), (1, 0)]) for piece in own]

    high, low = call(decode_kernel, (shape((2048, 256), BF16),) * 2, all_w, name="decode")

    flops = 2 * 1024 * 2048 * 256
    part, held = call(
        forward_kernel,
        (shape((NX, 256, 256), BF16), shape((NX, 128, 2048), BF16)),
        *own,
        *pair,
        high,
        low,
        at,
        scratch=[pltpu.SemaphoreType.DMA((NX,))],
        flops=2 * flops,
        far=range(NX, 2 * NX),
        name="forward",
    )
    got_part = lax.all_to_all(part, "x", 0, 0, tiled=True)
    slope, loss_part = call(
        slope_kernel, (shape((NX, 256, 256), BF16), shape((1, 128), F32)), got_part, name="slope"
    )
    slopes = lax.all_to_all(slope, "x", 0, 0, tiled=True)

    term = call(
        grad_kernel,
        shape((32, 144, 128), BF16),
        *own,
        held,
        slopes,
        loss_part,
        at,
        scratch=[pltpu.VMEM((1024, 256), BF16), pltpu.VMEM((4, 32, 4, 8, 128), F32)],
        flops=flops,
        name="grad",
    )
    got_term = lax.all_to_all(term, PLANE, 0, 0, tiled=True)
    packed_term = call(
        gather_kernel,
        shape((NZ, 48, 128), BF16),
        got_term,
        own_pat,
        scratch=[pltpu.VMEM((NZ, 48, 128), F32)],
        name="gather",
    )
    got_sum = lax.all_to_all(packed_term, "z", 0, 0, tiled=True)
    grad, loss = call(
        final_kernel,
        (shape((64, 128), F32), shape((1, 1), F32)),
        got_sum,
        pat,
        name="final",
    )
    return grad.T, loss.reshape(())


def solution(mesh):
    fine = Mesh(mesh.devices.reshape(NZ, NYL, NC, NYH, NX), AXES)
    dp, tensor = ("z", "yl", "core"), ("yh", "x")
    in_specs = (P(AXES, None), P(), P(dp, tensor), P(dp, tensor), P(None, tensor))
    out_specs = (P(dp, tensor), P())
    return jax.shard_map(shards, mesh=fine, in_specs=in_specs, out_specs=out_specs, check_vma=False)
```

```python
import jax
import jax.numpy as jnp
from jax import lax
from jax.experimental import pallas as pl
from jax.experimental.pallas import tpu as pltpu
from jax.sharding import Mesh, PartitionSpec as P

F32 = jnp.float32
BF16 = jnp.bfloat16
NZ, NYL, NC, NYH, NX = 16, 2, 2, 2, 4
AXES = ("z", "yl", "core", "yh", "x")
PLANE = ("yl", "core", "yh", "x")
D, KVW, TOKENS = 8192, 512, 65536
FLOPS = 2 * 10**9
SHIFT = 34
VMEM = pl.BlockSpec(memory_space=pltpu.VMEM)
SMEM = pl.BlockSpec(memory_space=pltpu.SMEM)
STEP = (0, 2, 1, 3)
BACK = (0, 2, 3, 1)


def call(kernel, out_shape, *args, scratch=(), flops=0, name=None, far=(), out_far=False, grant=24):
    size = sum(a.size * a.dtype.itemsize for a in args)
    for o in jax.tree.leaves(out_shape):
        size += o.size * o.dtype.itemsize
    specs = [SMEM if a.shape == (5,) else VMEM for a in args]
    for i in far:
        specs[i] = pl.BlockSpec(memory_space=pl.ANY)
    return pl.pallas_call(
        kernel,
        out_shape=out_shape,
        in_specs=specs,
        out_specs=jax.tree.map(
            lambda _: pl.BlockSpec(memory_space=pl.ANY) if out_far else VMEM, out_shape
        ),
        scratch_shapes=list(scratch),
        name=name,
        cost_estimate=pl.CostEstimate(flops=flops, bytes_accessed=size, transcendentals=0),
        compiler_params=pltpu.CompilerParams(vmem_limit_bytes=grant * 1024 * 1024),
    )(*args)


def shape(dims, dtype):
    return jax.ShapeDtypeStruct(dims, dtype)


def lane_group(dims):
    return lax.broadcasted_iota(jnp.int32, dims, len(dims) - 1) // 32


def place_in_plane(yl, c, yh, x):
    return ((yl * NC + c) * NYH + yh) * NX + x


def swap_groups(parts, place):
    total = None
    for b, part in enumerate(parts):
        shift = (b - place) * 32 % 128
        moved = pltpu.roll(part, shift, part.ndim - 1) if shift else part
        here = jnp.where(lane_group(part.shape) == b, moved, 0.0)
        total = here if total is None else total + here
    return total


def swap_all(parts):
    axis = parts[0].ndim - 1
    group = lane_group(parts[0].shape)
    low, even = group < 2, group % 2 == 0
    half = []
    for a, b in ((0, 2), (1, 3)):
        half.append(jnp.where(low, parts[a], pltpu.roll(parts[b], 64, axis)))
        half.append(jnp.where(low, pltpu.roll(parts[a], 64, axis), parts[b]))
    out = []
    for a, b in ((half[0], half[2]), (half[1], half[3])):
        out.append(jnp.where(even, a, pltpu.roll(b, 32, axis)))
        out.append(jnp.where(even, pltpu.roll(a, 96, axis), b))
    return out


def kept_rows(pat):
    first = jnp.where(pat > 2.5, 1.0, 0.0) + jnp.where(pat > 4.5, 1.0, 0.0)
    second = jnp.where(pat < 2.5, pat + 1.0, jnp.where(pat < 3.5, 2.0, 3.0))
    return first, second


def row_of_four(dims):
    return (lax.broadcasted_iota(jnp.int32, dims, 1) % 4).astype(F32)


def shuffled(place):
    return place % 4 * 8 + place // 4


def norm_kernel(x_hbm, gain_ref, at_ref, *rest):
    outs, (x_ref, move_ref, split_ref, sems, out_sems) = rest[:NX], rest[NX:]
    loads = [
        pltpu.make_async_copy(x_hbm.at[:, cut], x_ref.at[:, cut], sems.at[i])
        for i, cut in enumerate(pl.ds(i * 1024, 1024) for i in range(8))
    ]
    for load in loads:
        load.start()
    src = lax.broadcasted_iota(jnp.int32, (512, 128), 0)
    dst = lax.broadcasted_iota(jnp.int32, (512, 128), 1)
    goal = ((src >> 5 & 3) << 7) + (src >> 7 << 5) + ((src & 3) << 3) + (src >> 2 & 7)
    for x in range(NX):
        move_ref[:, x * 128 : (x + 1) * 128] = jnp.where(goal == dst + x * 128, 1.0, 0.0).astype(BF16)
    total = jnp.zeros((128, 128), F32)
    for g in range(64):
        if g % 8 == 0:
            loads[g // 8].wait()
        part = x_ref[:, g * 128 : (g + 1) * 128].astype(F32)
        total += part * part
    factor = lax.rsqrt(jnp.sum(total, axis=1, keepdims=True) / D + 1e-05)
    factor = jnp.broadcast_to(factor, (128, 128))
    gain = gain_ref[...].astype(F32)
    stores = []
    for yl in range(2):
        for m in range(8):
            tile = yl * 8 + m
            parts = []
            for b in range(4):
                block = 8 * m + 4 * (b // 2) + 2 * yl + b % 2
                part = x_ref[:, block * 128 : (block + 1) * 128].astype(F32)
                parts.append((part * factor * gain[block : block + 1, :]).astype(BF16))
            parts = jnp.concatenate(parts, axis=1)
            seg = jnp.dot(parts, move_ref[...], preferred_element_type=F32).astype(BF16)
            for x in range(NX):
                split_ref[x, :, tile * 128 : (tile + 1) * 128] = seg[:, x * 128 : (x + 1) * 128]
        for i in range(NX):
            cut = pl.ds(yl * 1024, 1024)
            piece = split_ref.at[(at_ref[0] + STEP[i]) % NX]
            stores.append(
                pltpu.make_async_copy(piece.at[:, cut], outs[i].at[:, cut], out_sems.at[yl * NX + i])
            )
            stores[-1].start()
    for store in stores:
        store.wait()


def choose_kernel(pat_ref, at_ref, out_ref, pick_ref):
    pats = pat_ref[...].astype(F32).astype(BF16)
    col = lax.broadcasted_iota(jnp.int32, (64, 128), 0)
    lane = lax.broadcasted_iota(jnp.int32, (64, 128), 1)
    for c in range(NC):
        pick = jnp.where(col - c * 32 == lane % 32, 1.0, 0.0).astype(BF16)
        chosen = lax.dot_general(pats, pick, (((0,), (0,)), ((), ())), preferred_element_type=F32)
        pick_ref[...] = chosen.reshape(NZ, NYL, NC, NX, 8, 128)
        out_ref[c] = pick_ref[:, at_ref[2], at_ref[1]]


def pack_kernel(teacher_hbm, student_hbm, pat_hbm, at_ref, out_ref, rows_ref, *scratch):
    teacher_ref, student_ref, pat_ref, sems = scratch
    place = at_ref[3]
    window = pl.ds(pl.multiple_of(place // 4 * 128, 128), 128)
    loads = [
        pltpu.make_async_copy(pat_hbm.at[:, window], pat_ref, sems.at[0]),
        pltpu.make_async_copy(teacher_hbm, teacher_ref, sems.at[1]),
        pltpu.make_async_copy(student_hbm, student_ref, sems.at[2]),
    ]
    for load in loads:
        load.start()
    for load in loads:
        load.wait()
    row = lax.broadcasted_iota(jnp.int32, (128, 128), 0)
    col = lax.broadcasted_iota(jnp.int32, (128, 128), 1)
    spread = jnp.where(col // 4 + place % 4 * 32 == row, 1.0, 0.0).astype(BF16)
    pat = jnp.dot(pat_ref[...].astype(F32).astype(BF16), spread, preferred_element_type=F32)
    rows_ref[...] = pat
    first, second = kept_rows(pat)
    spot = row_of_four(pat.shape)
    keep = jnp.where((spot == first) | (spot == second), 1.0, 0.0)
    delta = student_ref[...].astype(F32) * keep - teacher_ref[...].astype(F32)
    delta = delta * 2.0**SHIFT
    delta = ((delta * jnp.abs(delta)) * (delta * delta)).astype(BF16)
    dst = lax.broadcasted_iota(jnp.int32, (128, 128), 0)
    src = lax.broadcasted_iota(jnp.int32, (128, 128), 1)
    move = jnp.where(src // 32 * 32 + shuffled(src % 32) == dst, 1.0, 0.0).astype(BF16)
    delta = jnp.concatenate([delta, jnp.zeros_like(delta)], axis=0)
    wide = lax.dot_general(
        move, delta, (((1,), (1,)), ((), ())), preferred_element_type=F32
    ).reshape(4, 4, 8, 128)
    for c in range(NC):
        piece = swap_groups([wide[:, q] for q in range(4)], c).reshape(32, 128).astype(BF16)
        for z in range(NZ):
            out_ref[z, c * 32 : (c + 1) * 32, :] = piece


def spread_kernel(got_ref, out_ref):
    got = got_ref[...].astype(F32).reshape(NZ, 8, 8, 128)
    for c in range(NC):
        for x in range(NX):
            rows = got[:, c * NX + x].reshape(128, 128).astype(BF16)
            for y in range(4):
                out_ref[place_in_plane(y // 2, c, y % 2, x)] = rows


def decode_kernel(got_ref, high_ref, low_ref, w_ref):
    for yl in range(NYL):
        for c in range(NC):
            for yh in range(NYH):
                at = [place_in_plane(yl, c, yh, x) for x in range(NX)]
                parts = [got_ref[i].astype(F32).reshape(NZ, 8, 128) for i in at]
                for q, sent in enumerate(swap_all(parts)):
                    size = lax.rsqrt(lax.rsqrt(jnp.abs(sent))) * 2.0**-SHIFT
                    delta = jnp.where(sent < 0, -size, size)
                    w_ref[yl, :, c, q, :, yh * 128 : (yh + 1) * 128] = delta
    for yl in range(NYL):
        for k in range(4):
            delta = w_ref[yl, k * 4 : (k + 1) * 4].reshape(256, 256)
            high = delta.astype(BF16)
            at = yl * 1024 + k * 256
            high_ref[at : at + 256, :] = high
            low_ref[at : at + 256, :] = (delta - high.astype(F32)).astype(BF16)


def forward(rows, high_ref, low_ref):
    part = jnp.dot(rows, high_ref[...], preferred_element_type=F32)
    part += jnp.dot(rows, low_ref[...], preferred_element_type=F32)
    return part.astype(BF16)


def forward_own_kernel(*refs):
    own, (high_ref, low_ref, at_ref, out_ref) = refs[:NX], refs[NX:]
    for i in range(NX):
        out_ref[(at_ref[0] + BACK[i]) % NX] = forward(own[i][...], high_ref, low_ref)


def forward_pair_kernel(*refs):
    pair, rest = refs[:NX], refs[NX:]
    part_ref, high_ref, low_ref, at_ref, out_ref, held_ref, sems = rest[NX - 1 :]
    loads = [pltpu.make_async_copy(pair[i], held_ref.at[i], sems.at[i]) for i in range(NX)]
    for load in loads:
        load.start()
    for x in range(NX):
        out_ref[x, :128] = part_ref[x]
    for i in range(NX):
        loads[i].wait()
        out_ref[(at_ref[0] + BACK[i]) % NX, 128:] = forward(held_ref[i], high_ref, low_ref)


def mark_kernel(piece_hbm, out_ref):
    out_ref[...] = jnp.zeros_like(out_ref)


def thirds(value, rows):
    high = value.astype(BF16).astype(F32)
    mid = (value - high).astype(BF16).astype(F32)
    low = value - high - mid
    row = lax.broadcasted_iota(jnp.int32, (rows, value.shape[1]), 0)
    return jnp.where(row == 0, high, jnp.where(row == 1, mid, jnp.where(row == 2, low, 0.0)))


def slope_kernel(part_ref, out_ref, loss_ref):
    diff = part_ref[0].astype(F32)
    for x in range(1, NX):
        diff = diff + part_ref[x].astype(F32)
    slope = diff.astype(BF16)
    for x in range(NX):
        out_ref[x] = slope
    square = diff * diff
    loss_ref[...] = jnp.sum(square[:, :128] + square[:, 128:], axis=0, keepdims=True)


def grad_kernel(*refs):
    own, (held_ref, *rest) = refs[:NX], refs[NX:]
    slope_ref, loss_ref, at_ref, out_ref, s_ref, term_ref = rest
    contract = (((0,), (0,)), ((), ()))
    for i in range(NX):
        x = (at_ref[0] + BACK[i]) % NX
        s_ref[i * 128 : (i + 1) * 128] = slope_ref[x, :128]
        s_ref[512 + i * 128 : 512 + (i + 1) * 128] = slope_ref[x, 128:]
    for k in range(8):
        at = k * 256
        rows = [ref[:, at : at + 256] for ref in own]
        rows += [held_ref[i, :, at : at + 256] for i in range(NX)]
        rows = jnp.concatenate(rows, axis=0)
        term = lax.dot_general(rows, s_ref[...], contract, preferred_element_type=F32)
        for yh in range(2):
            term_ref[(k // 4) * 2 + yh, (k % 4) * 8 : (k % 4 + 1) * 8] = term[
                :, yh * 128 : (yh + 1) * 128
            ].reshape(8, 4, 8, 128)
    loss = thirds(loss_ref[...], 16).astype(BF16)
    for y in range(4):
        term = term_ref[y].reshape(NZ, NC, 4, 8, 128)
        for c in range(NC):
            for x, rows in enumerate(swap_all([term[:, c, q] for q in range(4)])):
                at = place_in_plane(y // 2, c, y % 2, x)
                out_ref[at, :128, :] = rows.reshape(128, 128).astype(BF16)
                out_ref[at, 128:, :] = loss


def gather_kernel(got_ref, pat_ref, out_ref, mid_ref):
    loss = got_ref[0, 128:, :].astype(F32)
    for i in range(1, 32):
        loss = loss + got_ref[i, 128:, :].astype(F32)
    loss = jnp.sum(jnp.sum(loss, axis=0, keepdims=True), axis=1, keepdims=True)
    loss = thirds(jnp.broadcast_to(loss, (1, 128)), 16)
    lane = lax.broadcasted_iota(jnp.int32, (16, 128), 1)
    mid_ref[:, 32:, :] = jnp.broadcast_to(jnp.where(lane == 0, loss, 0.0), (NZ, 16, 128))
    group = lane_group((NZ, 8, 128))
    for x in range(NX):
        rows = jnp.zeros((NZ, 8, 128), F32)
        for c in range(NC):
            total = jnp.zeros((128, 128), F32)
            for y in range(4):
                total += got_ref[place_in_plane(y // 2, c, y % 2, x), :128, :].astype(F32)
            total = total.reshape(NZ, 8, 128)
            for i, which in enumerate(kept_rows(pat_ref[c, :, x])):
                kept = jnp.where(which == group.astype(F32), total, 0.0)
                kept += pltpu.roll(kept, 64, 2)
                kept += pltpu.roll(kept, 32, 2)
                rows = jnp.where(group == i * 2 + c, kept, rows)
        mid_ref[:, x * 8 : (x + 1) * 8, :] = rows
    out_ref[...] = mid_ref[...].astype(BF16)


def final_kernel(got_ref, pat_ref, out_ref, loss_ref):
    total = got_ref[0].astype(F32)
    for z in range(1, NZ):
        total = total + got_ref[z].astype(F32)
    loss = jnp.sum(jnp.sum(total[32:], axis=0, keepdims=True), axis=1, keepdims=True)
    loss_ref[...] = loss / (TOKENS * KVW)
    kept = total[:32]
    row = lax.broadcasted_iota(jnp.int32, (32, 128), 0)
    col = lax.broadcasted_iota(jnp.int32, (32, 128), 1)
    spread = jnp.where(col // 4 == row, 1.0, 0.0).astype(BF16)
    wide = jnp.zeros((128, 128), F32)
    for _ in range(3):
        part = kept.astype(BF16)
        kept = kept - part.astype(F32)
        wide += lax.dot_general(
            part, spread, (((0,), (0,)), ((), ())), preferred_element_type=F32
        )
    first, second = kept_rows(pat_ref[...])
    spot = row_of_four(wide[:64].shape)
    grad = jnp.where(spot == first, wide[:64], 0.0) + jnp.where(spot == second, wide[64:], 0.0)
    out_ref[...] = grad / jnp.sqrt(F32(TOKENS))


def ring(step):
    return [(i, (i + step) % NX) for i in range(NX)]


def shards(hidden, norm_gain, teacher_k, student_k, keep_pattern):
    z, yl, core, yh, x = (lax.axis_index(a) for a in AXES)
    place = (z * NYL + yl) * NC + core
    at = jnp.stack([x, core, yl, place, yh]).astype(jnp.int32)
    patterns = keep_pattern.T

    packed, pat = call(
        pack_kernel,
        (shape((NZ, 64, 128), BF16), shape((64, 128), F32)),
        teacher_k.T,
        student_k.T,
        patterns,
        at,
        scratch=[
            pltpu.VMEM((64, 128), BF16),
            pltpu.VMEM((64, 128), BF16),
            pltpu.VMEM((64, 128), jnp.int32),
            pltpu.SemaphoreType.DMA((3,)),
        ],
        far=(0, 1, 2),
        grant=60,
        name="pack",
    )
    got_w = lax.all_to_all(packed, "z", 0, 0, tiled=True)

    split = call(
        norm_kernel,
        (shape((128, 2048), BF16),) * NX,
        hidden,
        norm_gain.reshape(64, 128),
        at,
        scratch=[
            pltpu.VMEM((128, D), BF16),
            pltpu.VMEM((512, 512), BF16),
            pltpu.VMEM((NX, 128, 2048), BF16),
            pltpu.SemaphoreType.DMA((8,)),
            pltpu.SemaphoreType.DMA((2 * NX,)),
        ],
        flops=2 * 2048 * 512 * 512,
        far=(0,),
        out_far=True,
        grant=60,
        name="norm",
    )
    own = [split[0]] + [lax.ppermute(split[i], "x", ring(STEP[i])) for i in range(1, NX)]
    rows_w = call(spread_kernel, shape((32, 128, 128), BF16), got_w, name="spread")
    all_w = lax.all_to_all(rows_w, PLANE, 0, 0, tiled=True)

    late, _ = lax.optimization_barrier((patterns, rows_w))
    own_pat = call(
        choose_kernel,
        shape((NC, NZ, NX, 8, 128), F32),
        late,
        at,
        scratch=[pltpu.VMEM((NZ, NYL, NC, NX, 8, 128), F32)],
        name="choose",
    )
    own[2], own_pat = lax.optimization_barrier((own[2], own_pat))
    marks = []
    for i in range(1, NX):
        mark = call(
            mark_kernel, shape((8, 128), F32), own[i], far=(0,), flops=FLOPS, name="mark"
        )
        own[i], mark = lax.optimization_barrier((own[i], mark))
        marks.append(mark)
    pair = [lax.ppermute(piece, "core", [(0, 1), (1, 0)]) for piece in own]


    high, low = call(
        decode_kernel,
        (shape((2048, 256), BF16),) * 2,
        all_w,
        scratch=[pltpu.VMEM((NYL, NZ, NC, 4, 8, 256), F32)],
        name="decode",
    )
    flops = 2 * 1024 * 2048 * 256
    part = call(
        forward_own_kernel,
        shape((NX, 128, 256), BF16),
        *own,
        high,
        low,
        at,
        flops=flops,
        name="forward_own",
    )
    part, held = call(
        forward_pair_kernel,
        (shape((NX, 256, 256), BF16), shape((NX, 128, 2048), BF16)),
        *pair,
        *marks,
        part,
        high,
        low,
        at,
        scratch=[pltpu.SemaphoreType.DMA((NX,))],
        flops=flops,
        far=range(NX),
        name="forward_pair",
    )
    got_part = lax.all_to_all(part, "x", 0, 0, tiled=True)
    slope, loss_part = call(
        slope_kernel, (shape((NX, 256, 256), BF16), shape((1, 128), F32)), got_part, name="slope"
    )
    slopes = lax.all_to_all(slope, "x", 0, 0, tiled=True)

    term = call(
        grad_kernel,
        shape((32, 144, 128), BF16),
        *own,
        held,
        slopes,
        loss_part,
        at,
        scratch=[pltpu.VMEM((1024, 256), BF16), pltpu.VMEM((4, 32, 4, 8, 128), F32)],
        flops=flops,
        name="grad",
    )
    got_term = lax.all_to_all(term, PLANE, 0, 0, tiled=True)
    packed_term = call(
        gather_kernel,
        shape((NZ, 48, 128), BF16),
        got_term,
        own_pat,
        scratch=[pltpu.VMEM((NZ, 48, 128), F32)],
        name="gather",
    )
    got_sum = lax.all_to_all(packed_term, "z", 0, 0, tiled=True)
    grad, loss = call(
        final_kernel,
        (shape((64, 128), F32), shape((1, 1), F32)),
        got_sum,
        pat,
        name="final",
    )
    return grad.T, loss.reshape(())


def solution(mesh):
    fine = Mesh(mesh.devices.reshape(NZ, NYL, NC, NYH, NX), AXES)
    dp, tensor = ("z", "yl", "core"), ("yh", "x")
    in_specs = (P(AXES, None), P(), P(dp, tensor), P(dp, tensor), P(None, tensor))
    out_specs = (P(dp, tensor), P())
    return jax.shard_map(shards, mesh=fine, in_specs=in_specs, out_specs=out_specs, check_vma=False)
```

```python
import jax
import jax.numpy as jnp
from jax import lax
from jax.experimental import pallas as pl
from jax.experimental.pallas import tpu as pltpu
from jax.sharding import Mesh, PartitionSpec as P

F32 = jnp.float32
BF16 = jnp.bfloat16
NZ, NYL, NC, NYH, NX = 16, 2, 2, 2, 4
AXES = ("z", "yl", "core", "yh", "x")
PLANE = ("yl", "core", "yh", "x")
D, KVW, TOKENS = 8192, 512, 65536
FLOPS = (0, 3 * 10**9, 2 * 10**9, 0)
SHIFT = 34
VMEM = pl.BlockSpec(memory_space=pltpu.VMEM)
SMEM = pl.BlockSpec(memory_space=pltpu.SMEM)
STEP = (0, 2, 1, 3)
BACK = (0, 2, 3, 1)
SOON, LAST = (0, 1, 2), 3


def call(kernel, out_shape, *args, scratch=(), flops=0, name=None, far=(), out_far=False, grant=24):
    size = sum(a.size * a.dtype.itemsize for a in args)
    for o in jax.tree.leaves(out_shape):
        size += o.size * o.dtype.itemsize
    specs = [SMEM if a.shape == (5,) else VMEM for a in args]
    for i in far:
        specs[i] = pl.BlockSpec(memory_space=pl.ANY)
    return pl.pallas_call(
        kernel,
        out_shape=out_shape,
        in_specs=specs,
        out_specs=jax.tree.map(
            lambda _: pl.BlockSpec(memory_space=pl.ANY) if out_far else VMEM, out_shape
        ),
        scratch_shapes=list(scratch),
        name=name,
        cost_estimate=pl.CostEstimate(flops=flops, bytes_accessed=size, transcendentals=0),
        compiler_params=pltpu.CompilerParams(vmem_limit_bytes=grant * 1024 * 1024),
    )(*args)


def shape(dims, dtype):
    return jax.ShapeDtypeStruct(dims, dtype)


def lane_group(dims):
    return lax.broadcasted_iota(jnp.int32, dims, len(dims) - 1) // 32


def place_in_plane(yl, c, yh, x):
    return ((yl * NC + c) * NYH + yh) * NX + x


def swap_groups(parts, place):
    total = None
    for b, part in enumerate(parts):
        shift = (b - place) * 32 % 128
        moved = pltpu.roll(part, shift, part.ndim - 1) if shift else part
        here = jnp.where(lane_group(part.shape) == b, moved, 0.0)
        total = here if total is None else total + here
    return total


def swap_all(parts):
    axis = parts[0].ndim - 1
    group = lane_group(parts[0].shape)
    low, even = group < 2, group % 2 == 0
    half = []
    for a, b in ((0, 2), (1, 3)):
        half.append(jnp.where(low, parts[a], pltpu.roll(parts[b], 64, axis)))
        half.append(jnp.where(low, pltpu.roll(parts[a], 64, axis), parts[b]))
    out = []
    for a, b in ((half[0], half[2]), (half[1], half[3])):
        out.append(jnp.where(even, a, pltpu.roll(b, 32, axis)))
        out.append(jnp.where(even, pltpu.roll(a, 96, axis), b))
    return out


def kept_rows(pat):
    first = jnp.where(pat > 2.5, 1.0, 0.0) + jnp.where(pat > 4.5, 1.0, 0.0)
    second = jnp.where(pat < 2.5, pat + 1.0, jnp.where(pat < 3.5, 2.0, 3.0))
    return first, second


def row_of_four(dims):
    return (lax.broadcasted_iota(jnp.int32, dims, 1) % 4).astype(F32)


def shuffled(place):
    return place % 4 * 8 + place // 4


def norm_kernel(x_hbm, gain_ref, at_ref, *rest):
    outs, (x_ref, move_ref, split_ref, sems, out_sems) = rest[:NX], rest[NX:]
    loads = [
        pltpu.make_async_copy(x_hbm.at[:, cut], x_ref.at[:, cut], sems.at[i])
        for i, cut in enumerate(pl.ds(i * 1024, 1024) for i in range(8))
    ]
    for load in loads:
        load.start()
    src = lax.broadcasted_iota(jnp.int32, (512, 128), 0)
    dst = lax.broadcasted_iota(jnp.int32, (512, 128), 1)
    goal = ((src >> 5 & 3) << 7) + (src >> 7 << 5) + ((src & 3) << 3) + (src >> 2 & 7)
    for x in range(NX):
        move_ref[:, x * 128 : (x + 1) * 128] = jnp.where(goal == dst + x * 128, 1.0, 0.0).astype(BF16)
    total = jnp.zeros((128, 128), F32)
    for g in range(64):
        if g % 8 == 0:
            loads[g // 8].wait()
        part = x_ref[:, g * 128 : (g + 1) * 128].astype(F32)
        total += part * part
    factor = lax.rsqrt(jnp.sum(total, axis=1, keepdims=True) / D + 1e-05)
    factor = jnp.broadcast_to(factor, (128, 128))
    gain = gain_ref[...].astype(F32)
    stores = []
    for yl in range(2):
        for m in range(8):
            tile = yl * 8 + m
            parts = []
            for b in range(4):
                block = 8 * m + 4 * (b // 2) + 2 * yl + b % 2
                part = x_ref[:, block * 128 : (block + 1) * 128].astype(F32)
                parts.append((part * factor * gain[block : block + 1, :]).astype(BF16))
            parts = jnp.concatenate(parts, axis=1)
            seg = jnp.dot(parts, move_ref[...], preferred_element_type=F32).astype(BF16)
            for x in range(NX):
                split_ref[x, :, tile * 128 : (tile + 1) * 128] = seg[:, x * 128 : (x + 1) * 128]
        for i in range(NX):
            cut = pl.ds(yl * 1024, 1024)
            piece = split_ref.at[(at_ref[0] + STEP[i]) % NX]
            stores.append(
                pltpu.make_async_copy(piece.at[:, cut], outs[i].at[:, cut], out_sems.at[yl * NX + i])
            )
            stores[-1].start()
    for store in stores:
        store.wait()


def choose_kernel(pat_ref, at_ref, out_ref, pick_ref):
    pats = pat_ref[...].astype(F32).astype(BF16)
    col = lax.broadcasted_iota(jnp.int32, (64, 128), 0)
    lane = lax.broadcasted_iota(jnp.int32, (64, 128), 1)
    group = lane_group((32, 128))
    for c in range(NC):
        pick = jnp.where(col - c * 32 == lane % 32, 1.0, 0.0).astype(BF16)
        chosen = lax.dot_general(pats, pick, (((0,), (0,)), ((), ())), preferred_element_type=F32)
        pick_ref[...] = chosen.reshape(NZ, NYL, NC, NX, 8, 128)
        for x in range(NX):
            rows = pick_ref[:, at_ref[2], at_ref[1], x].reshape(4, 32, 128)
            total = rows[0]
            for b in range(1, 4):
                total = jnp.where(group == b, rows[b], total)
            out_ref[c * NX + x] = total.astype(BF16)


def pack_kernel(teacher_hbm, student_hbm, pat_hbm, at_ref, out_ref, rows_ref, *scratch):
    teacher_ref, student_ref, pat_ref, sems = scratch
    place = at_ref[3]
    window = pl.ds(pl.multiple_of(place // 4 * 128, 128), 128)
    loads = [
        pltpu.make_async_copy(pat_hbm.at[:, window], pat_ref, sems.at[0]),
        pltpu.make_async_copy(teacher_hbm, teacher_ref, sems.at[1]),
        pltpu.make_async_copy(student_hbm, student_ref, sems.at[2]),
    ]
    for load in loads:
        load.start()
    for load in loads:
        load.wait()
    row = lax.broadcasted_iota(jnp.int32, (128, 128), 0)
    col = lax.broadcasted_iota(jnp.int32, (128, 128), 1)
    spread = jnp.where(col // 4 + place % 4 * 32 == row, 1.0, 0.0).astype(BF16)
    pat = jnp.dot(pat_ref[...].astype(F32).astype(BF16), spread, preferred_element_type=F32)
    rows_ref[...] = pat
    first, second = kept_rows(pat)
    spot = row_of_four(pat.shape)
    keep = jnp.where((spot == first) | (spot == second), 1.0, 0.0)
    delta = student_ref[...].astype(F32) * keep - teacher_ref[...].astype(F32)
    delta = delta * 2.0**SHIFT
    delta = ((delta * jnp.abs(delta)) * (delta * delta)).astype(BF16)
    dst = lax.broadcasted_iota(jnp.int32, (128, 128), 0)
    src = lax.broadcasted_iota(jnp.int32, (128, 128), 1)
    move = jnp.where(src // 32 * 32 + shuffled(src % 32) == dst, 1.0, 0.0).astype(BF16)
    delta = jnp.concatenate([delta, jnp.zeros_like(delta)], axis=0)
    wide = lax.dot_general(
        move, delta, (((1,), (1,)), ((), ())), preferred_element_type=F32
    ).reshape(4, 4, 8, 128)
    for c in range(NC):
        piece = swap_groups([wide[:, q] for q in range(4)], c).reshape(32, 128).astype(BF16)
        for z in range(NZ):
            out_ref[z, c * 32 : (c + 1) * 32, :] = piece


def spread_kernel(got_ref, pat_ref, out_ref):
    got = got_ref[...].astype(F32).reshape(NZ, 8, 8, 128)
    for c in range(NC):
        for x in range(NX):
            rows = got[:, c * NX + x].reshape(128, 128).astype(BF16)
            for y in range(4):
                at = place_in_plane(y // 2, c, y % 2, x)
                out_ref[at, :128, :] = rows
                out_ref[at, 128:, :] = pat_ref[c * NX + x]


def decode_kernel(got_ref, high_ref, low_ref, pat_ref, w_ref):
    for yl in range(NYL):
        for c in range(NC):
            for yh in range(NYH):
                at = [place_in_plane(yl, c, yh, x) for x in range(NX)]
                parts = [got_ref[i, :128, :].astype(F32).reshape(NZ, 8, 128) for i in at]
                for q, sent in enumerate(swap_all(parts)):
                    size = lax.rsqrt(lax.rsqrt(jnp.abs(sent))) * 2.0**-SHIFT
                    delta = jnp.where(sent < 0, -size, size)
                    w_ref[yl, :, c, q, :, yh * 128 : (yh + 1) * 128] = delta
                parts = [got_ref[i, 128:, :].astype(F32) for i in at]
                for b, rows in enumerate(swap_all(parts)):
                    pat_ref[yl * NYH + yh, b * 4 : (b + 1) * 4, c] = rows.reshape(4, 8, 128)
    for yl in range(NYL):
        for k in range(4):
            delta = w_ref[yl, k * 4 : (k + 1) * 4].reshape(256, 256)
            high = delta.astype(BF16)
            at = yl * 1024 + k * 256
            high_ref[at : at + 256, :] = high
            low_ref[at : at + 256, :] = (delta - high.astype(F32)).astype(BF16)


def forward(rows, high_ref, low_ref):
    part = jnp.dot(rows, high_ref[...], preferred_element_type=F32)
    part += jnp.dot(rows, low_ref[...], preferred_element_type=F32)
    return part.astype(BF16)


def forward_most_kernel(*refs):
    own, pair, rest = refs[:NX], refs[NX : NX + 3], refs[NX + 3 :]
    high_ref, low_ref, at_ref, out_ref, held_ref, sems = rest
    loads = [pltpu.make_async_copy(pair[i], held_ref.at[i], sems.at[i]) for i in range(3)]
    for load in loads:
        load.start()
    for i in range(NX):
        out_ref[(at_ref[0] + BACK[i]) % NX, :128] = forward(own[i][...], high_ref, low_ref)
    for i in range(3):
        loads[i].wait()
        x = (at_ref[0] + BACK[SOON[i]]) % NX
        out_ref[x, 128:] = forward(held_ref[i], high_ref, low_ref)
    out_ref[(at_ref[0] + BACK[LAST]) % NX, 128:] = jnp.zeros((128, 256), BF16)


def forward_last_kernel(pair_hbm, part_ref, high_ref, low_ref, at_ref, *rest):
    out_ref, held_ref, sem = rest[NX - 1 :]
    load = pltpu.make_async_copy(pair_hbm, held_ref, sem)
    load.start()
    out_ref[...] = part_ref[...]
    load.wait()
    out_ref[(at_ref[0] + BACK[LAST]) % NX, 128:] = forward(held_ref[...], high_ref, low_ref)


def mark_kernel(piece_hbm, out_ref):
    out_ref[...] = jnp.zeros_like(out_ref)


def thirds(value, rows):
    high = value.astype(BF16).astype(F32)
    mid = (value - high).astype(BF16).astype(F32)
    low = value - high - mid
    row = lax.broadcasted_iota(jnp.int32, (rows, value.shape[1]), 0)
    return jnp.where(row == 0, high, jnp.where(row == 1, mid, jnp.where(row == 2, low, 0.0)))


def slope_kernel(part_ref, out_ref, loss_ref):
    diff = part_ref[0].astype(F32)
    for x in range(1, NX):
        diff = diff + part_ref[x].astype(F32)
    slope = diff.astype(BF16)
    for x in range(NX):
        out_ref[x] = slope
    square = diff * diff
    loss_ref[...] = jnp.sum(square[:, :128] + square[:, 128:], axis=0, keepdims=True)


def grad_kernel(*refs):
    own, (soon_ref, last_ref, *rest) = refs[:NX], refs[NX:]
    pat_ref, slope_ref, loss_ref, at_ref, out_ref, s_ref, term_ref = rest
    contract = (((0,), (0,)), ((), ()))
    for i in range(NX):
        x = (at_ref[0] + BACK[i]) % NX
        s_ref[i * 128 : (i + 1) * 128] = slope_ref[x, :128]
        s_ref[512 + i * 128 : 512 + (i + 1) * 128] = slope_ref[x, 128:]
    for k in range(8):
        at = k * 256
        rows = [ref[:, at : at + 256] for ref in own]
        pair = [soon_ref[i, :, at : at + 256] for i in range(3)]
        pair.insert(LAST, last_ref[:, at : at + 256])
        rows += pair
        rows = jnp.concatenate(rows, axis=0)
        term = lax.dot_general(rows, s_ref[...], contract, preferred_element_type=F32)
        for yh in range(2):
            term_ref[(k // 4) * 2 + yh, (k % 4) * 8 : (k % 4 + 1) * 8] = term[
                :, yh * 128 : (yh + 1) * 128
            ].reshape(8, 4, 8, 128)
    loss = thirds(loss_ref[...], 16).astype(BF16)
    for y in range(4):
        which = kept_rows(pat_ref[y].reshape(32, 8, 128))
        kept = [jnp.zeros((32, 8, 128), F32) for _ in which]
        for k in range(4):
            for i in range(2):
                kept[i] += jnp.where(which[i] == k, term_ref[y, :, k], 0.0)
        kept = [part.reshape(2, 8, NC, 8, 128) for part in kept]
        for c in range(NC):
            parts = [kept[i][half, :, c] for half in range(2) for i in range(2)]
            for x, rows in enumerate(swap_all(parts)):
                at = place_in_plane(y // 2, c, y % 2, x)
                out_ref[at, :64, :] = rows.reshape(64, 128).astype(BF16)
                out_ref[at, 64:, :] = loss


def gather_kernel(got_ref, out_ref, mid_ref):
    loss = got_ref[0, 64:, :].astype(F32)
    for i in range(1, 32):
        loss = loss + got_ref[i, 64:, :].astype(F32)
    loss = jnp.sum(jnp.sum(loss, axis=0, keepdims=True), axis=1, keepdims=True)
    loss = thirds(jnp.broadcast_to(loss, (1, 128)), 16)
    lane = lax.broadcasted_iota(jnp.int32, (16, 128), 1)
    mid_ref[:, 32:, :] = jnp.broadcast_to(jnp.where(lane == 0, loss, 0.0), (NZ, 16, 128))
    group = lane_group((8, 8, 128))
    for x in range(NX):
        sums = []
        for c in range(NC):
            total = jnp.zeros((64, 128), F32)
            for y in range(4):
                total += got_ref[place_in_plane(y // 2, c, y % 2, x), :64, :].astype(F32)
            sums.append(total.reshape(8, 8, 128))
        for half in range(2):
            rows = jnp.zeros((8, 8, 128), F32)
            for kept in range(2):
                for c in range(NC):
                    goal = kept * 2 + c
                    shift = (goal - half * 2 - kept) % 4 * 32
                    moved = pltpu.roll(sums[c], shift, 2) if shift else sums[c]
                    rows = jnp.where(group == goal, moved, rows)
            mid_ref[half * 8 : (half + 1) * 8, x * 8 : (x + 1) * 8, :] = rows
    out_ref[...] = mid_ref[...].astype(BF16)


def final_kernel(got_ref, pat_ref, out_ref, loss_ref):
    total = got_ref[0].astype(F32)
    for z in range(1, NZ):
        total = total + got_ref[z].astype(F32)
    loss = jnp.sum(jnp.sum(total[32:], axis=0, keepdims=True), axis=1, keepdims=True)
    loss_ref[...] = loss / (TOKENS * KVW)
    kept = total[:32]
    row = lax.broadcasted_iota(jnp.int32, (32, 128), 0)
    col = lax.broadcasted_iota(jnp.int32, (32, 128), 1)
    spread = jnp.where(col // 4 == row, 1.0, 0.0).astype(BF16)
    wide = jnp.zeros((128, 128), F32)
    for _ in range(3):
        part = kept.astype(BF16)
        kept = kept - part.astype(F32)
        wide += lax.dot_general(
            part, spread, (((0,), (0,)), ((), ())), preferred_element_type=F32
        )
    first, second = kept_rows(pat_ref[...])
    spot = row_of_four(wide[:64].shape)
    grad = jnp.where(spot == first, wide[:64], 0.0) + jnp.where(spot == second, wide[64:], 0.0)
    out_ref[...] = grad / jnp.sqrt(F32(TOKENS))


def ring(step):
    return [(i, (i + step) % NX) for i in range(NX)]


def shards(hidden, norm_gain, teacher_k, student_k, keep_pattern):
    z, yl, core, yh, x = (lax.axis_index(a) for a in AXES)
    place = (z * NYL + yl) * NC + core
    at = jnp.stack([x, core, yl, place, yh]).astype(jnp.int32)
    patterns = keep_pattern.T

    packed, pat = call(
        pack_kernel,
        (shape((NZ, 64, 128), BF16), shape((64, 128), F32)),
        teacher_k.T,
        student_k.T,
        patterns,
        at,
        scratch=[
            pltpu.VMEM((64, 128), BF16),
            pltpu.VMEM((64, 128), BF16),
            pltpu.VMEM((64, 128), jnp.int32),
            pltpu.SemaphoreType.DMA((3,)),
        ],
        far=(0, 1, 2),
        grant=60,
        name="pack",
    )
    got_w = lax.all_to_all(packed, "z", 0, 0, tiled=True)

    split = call(
        norm_kernel,
        (shape((128, 2048), BF16),) * NX,
        hidden,
        norm_gain.reshape(64, 128),
        at,
        scratch=[
            pltpu.VMEM((128, D), BF16),
            pltpu.VMEM((512, 512), BF16),
            pltpu.VMEM((NX, 128, 2048), BF16),
            pltpu.SemaphoreType.DMA((8,)),
            pltpu.SemaphoreType.DMA((2 * NX,)),
        ],
        flops=2 * 2048 * 512 * 512,
        far=(0,),
        out_far=True,
        grant=60,
        name="norm",
    )
    own = [split[0]] + [lax.ppermute(split[i], "x", ring(STEP[i])) for i in range(1, NX)]
    late, got_w = lax.optimization_barrier((patterns, got_w))
    own_pat = call(
        choose_kernel,
        shape((8, 32, 128), BF16),
        late,
        at,
        scratch=[pltpu.VMEM((NZ, NYL, NC, NX, 8, 128), F32)],
        name="choose",
    )
    rows_w = call(spread_kernel, shape((32, 160, 128), BF16), got_w, own_pat, name="spread")
    all_w = lax.all_to_all(rows_w, PLANE, 0, 0, tiled=True)

    marks = []
    for i in range(1, NX):
        mark = call(
            mark_kernel, shape((8, 128), F32), own[i], far=(0,), flops=FLOPS[i], name="mark"
        )
        own[i], mark = lax.optimization_barrier((own[i], mark))
        marks.append(mark)
    pair = [lax.ppermute(piece, "core", [(0, 1), (1, 0)]) for piece in own]


    high, low, pats = call(
        decode_kernel,
        (shape((2048, 256), BF16),) * 2 + (shape((4, NZ, NC, 8, 128), F32),),
        all_w,
        scratch=[pltpu.VMEM((NYL, NZ, NC, 4, 8, 256), F32)],
        name="decode",
    )
    flops = 2 * 1024 * 2048 * 256
    part, soon = call(
        forward_most_kernel,
        (shape((NX, 256, 256), BF16), shape((3, 128, 2048), BF16)),
        *own,
        *(pair[i] for i in SOON),
        high,
        low,
        at,
        scratch=[pltpu.SemaphoreType.DMA((3,))],
        flops=2 * flops * 7 // 8,
        far=range(NX, NX + 3),
        name="forward_most",
    )
    part, last = call(
        forward_last_kernel,
        (shape((NX, 256, 256), BF16), shape((128, 2048), BF16)),
        pair[LAST],
        part,
        high,
        low,
        at,
        *marks,
        scratch=[pltpu.SemaphoreType.DMA],
        flops=flops // 4,
        far=(0,),
        name="forward_last",
    )
    got_part = lax.all_to_all(part, "x", 0, 0, tiled=True)
    slope, loss_part = call(
        slope_kernel, (shape((NX, 256, 256), BF16), shape((1, 128), F32)), got_part, name="slope"
    )
    slopes = lax.all_to_all(slope, "x", 0, 0, tiled=True)

    term = call(
        grad_kernel,
        shape((32, 80, 128), BF16),
        *own,
        soon,
        last,
        pats,
        slopes,
        loss_part,
        at,
        scratch=[pltpu.VMEM((1024, 256), BF16), pltpu.VMEM((4, 32, 4, 8, 128), F32)],
        flops=flops,
        name="grad",
    )
    got_term = lax.all_to_all(term, PLANE, 0, 0, tiled=True)
    packed_term = call(
        gather_kernel,
        shape((NZ, 48, 128), BF16),
        got_term,
        scratch=[pltpu.VMEM((NZ, 48, 128), F32)],
        name="gather",
    )
    got_sum = lax.all_to_all(packed_term, "z", 0, 0, tiled=True)
    grad, loss = call(
        final_kernel,
        (shape((64, 128), F32), shape((1, 1), F32)),
        got_sum,
        pat,
        name="final",
    )
    return grad.T, loss.reshape(())


def solution(mesh):
    fine = Mesh(mesh.devices.reshape(NZ, NYL, NC, NYH, NX), AXES)
    dp, tensor = ("z", "yl", "core"), ("yh", "x")
    in_specs = (P(AXES, None), P(), P(dp, tensor), P(dp, tensor), P(None, tensor))
    out_specs = (P(dp, tensor), P())
    return jax.shard_map(shards, mesh=fine, in_specs=in_specs, out_specs=out_specs, check_vma=False)
```

```python
import jax
import jax.numpy as jnp
from jax import lax
from jax.experimental import pallas as pl
from jax.experimental.pallas import tpu as pltpu
from jax.sharding import Mesh, PartitionSpec as P

F32 = jnp.float32
BF16 = jnp.bfloat16
NZ, NYL, NC, NYH, NX = 16, 2, 2, 2, 4
AXES = ("z", "yl", "core", "yh", "x")
Y = ("yl", "yh")
ZCX = ("z", "core", "x")
PLANE = ("yl", "core", "yh", "x")
D, KVW, TOKENS = 8192, 512, 65536
SHIFT = 34
VMEM = pl.BlockSpec(memory_space=pltpu.VMEM)
SMEM = pl.BlockSpec(memory_space=pltpu.SMEM)
STEP = (0, 2, 1, 3)
BACK = (0, 2, 3, 1)
SOON, LAST = (0, 1, 3), 2


def call(kernel, out_shape, *args, scratch=(), flops=0, name=None, far=(), out_far=False, grant=24):
    size = sum(a.size * a.dtype.itemsize for a in args)
    for o in jax.tree.leaves(out_shape):
        size += o.size * o.dtype.itemsize
    specs = [SMEM if a.shape == (5,) else VMEM for a in args]
    for i in far:
        specs[i] = pl.BlockSpec(memory_space=pl.ANY)
    return pl.pallas_call(
        kernel,
        out_shape=out_shape,
        in_specs=specs,
        out_specs=jax.tree.map(
            lambda _: pl.BlockSpec(memory_space=pl.ANY) if out_far else VMEM, out_shape
        ),
        scratch_shapes=list(scratch),
        name=name,
        cost_estimate=pl.CostEstimate(flops=flops, bytes_accessed=size, transcendentals=0),
        compiler_params=pltpu.CompilerParams(vmem_limit_bytes=grant * 1024 * 1024),
    )(*args)


def shape(dims, dtype):
    return jax.ShapeDtypeStruct(dims, dtype)


def lane_group(dims):
    return lax.broadcasted_iota(jnp.int32, dims, len(dims) - 1) // 32


def place_in_plane(yl, c, yh, x):
    return ((yl * NC + c) * NYH + yh) * NX + x


def swap_groups(parts, place):
    total = None
    for b, part in enumerate(parts):
        shift = (b - place) * 32 % 128
        moved = pltpu.roll(part, shift, part.ndim - 1) if shift else part
        here = jnp.where(lane_group(part.shape) == b, moved, 0.0)
        total = here if total is None else total + here
    return total


def swap_all(parts):
    axis = parts[0].ndim - 1
    group = lane_group(parts[0].shape)
    low, even = group < 2, group % 2 == 0
    half = []
    for a, b in ((0, 2), (1, 3)):
        half.append(jnp.where(low, parts[a], pltpu.roll(parts[b], 64, axis)))
        half.append(jnp.where(low, pltpu.roll(parts[a], 64, axis), parts[b]))
    out = []
    for a, b in ((half[0], half[2]), (half[1], half[3])):
        out.append(jnp.where(even, a, pltpu.roll(b, 32, axis)))
        out.append(jnp.where(even, pltpu.roll(a, 96, axis), b))
    return out


def kept_rows(pat):
    first = jnp.where(pat > 2.5, 1.0, 0.0) + jnp.where(pat > 4.5, 1.0, 0.0)
    second = jnp.where(pat < 2.5, pat + 1.0, jnp.where(pat < 3.5, 2.0, 3.0))
    return first, second


def row_of_four(dims):
    return (lax.broadcasted_iota(jnp.int32, dims, 1) % 4).astype(F32)


def shuffled(place):
    return place % 4 * 8 + place // 4


def norm_kernel(x_hbm, gain_ref, at_ref, *rest):
    outs, (x_ref, move_ref, split_ref, sems, out_sems) = rest[:NX], rest[NX:]
    loads = [
        pltpu.make_async_copy(x_hbm.at[:, cut], x_ref.at[:, cut], sems.at[i])
        for i, cut in enumerate(pl.ds(i * 1024, 1024) for i in range(8))
    ]
    for load in loads:
        load.start()
    src = lax.broadcasted_iota(jnp.int32, (512, 128), 0)
    dst = lax.broadcasted_iota(jnp.int32, (512, 128), 1)
    goal = ((src >> 5 & 3) << 7) + (src >> 7 << 5) + ((src & 3) << 3) + (src >> 2 & 7)
    for x in range(NX):
        move_ref[:, x * 128 : (x + 1) * 128] = jnp.where(goal == dst + x * 128, 1.0, 0.0).astype(BF16)
    total = jnp.zeros((128, 128), F32)
    for g in range(64):
        if g % 8 == 0:
            loads[g // 8].wait()
        part = x_ref[:, g * 128 : (g + 1) * 128].astype(F32)
        total += part * part
    factor = lax.rsqrt(jnp.sum(total, axis=1, keepdims=True) / D + 1e-05)
    factor = jnp.broadcast_to(factor, (128, 128))
    gain = gain_ref[...].astype(F32)
    stores = []
    for yl in range(2):
        for m in range(8):
            tile = yl * 8 + m
            parts = []
            for b in range(4):
                block = 8 * m + 4 * (b // 2) + 2 * yl + b % 2
                part = x_ref[:, block * 128 : (block + 1) * 128].astype(F32)
                parts.append((part * factor * gain[block : block + 1, :]).astype(BF16))
            parts = jnp.concatenate(parts, axis=1)
            seg = jnp.dot(parts, move_ref[...], preferred_element_type=F32).astype(BF16)
            for x in range(NX):
                split_ref[x, :, tile * 128 : (tile + 1) * 128] = seg[:, x * 128 : (x + 1) * 128]
        for i in range(NX):
            cut = pl.ds(yl * 1024, 1024)
            piece = split_ref.at[(at_ref[0] + STEP[i]) % NX]
            stores.append(
                pltpu.make_async_copy(piece.at[:, cut], outs[i].at[:, cut], out_sems.at[yl * NX + i])
            )
            stores[-1].start()
    for store in stores:
        store.wait()


def choose_kernel(pat_ref, at_ref, out_ref, pick_ref):
    pats = pat_ref[...].astype(F32).astype(BF16)
    col = lax.broadcasted_iota(jnp.int32, (64, 128), 0)
    lane = lax.broadcasted_iota(jnp.int32, (64, 128), 1)
    for c in range(NC):
        pick = jnp.where(col - c * 32 == lane % 32, 1.0, 0.0).astype(BF16)
        chosen = lax.dot_general(pats, pick, (((0,), (0,)), ((), ())), preferred_element_type=F32)
        pick_ref[...] = chosen.reshape(NZ, NYL, NC, NX, 8, 128)
        out_ref[c] = pick_ref[:, at_ref[2], at_ref[1]]


def pack_kernel(teacher_hbm, student_hbm, pat_hbm, at_ref, out_ref, rows_ref, *scratch):
    teacher_ref, student_ref, pat_ref, sems = scratch
    place = at_ref[3]
    window = pl.ds(pl.multiple_of(place // 4 * 128, 128), 128)
    loads = [
        pltpu.make_async_copy(pat_hbm.at[:, window], pat_ref, sems.at[0]),
        pltpu.make_async_copy(teacher_hbm, teacher_ref, sems.at[1]),
        pltpu.make_async_copy(student_hbm, student_ref, sems.at[2]),
    ]
    for load in loads:
        load.start()
    for load in loads:
        load.wait()
    row = lax.broadcasted_iota(jnp.int32, (128, 128), 0)
    col = lax.broadcasted_iota(jnp.int32, (128, 128), 1)
    spread = jnp.where(col // 4 + place % 4 * 32 == row, 1.0, 0.0).astype(BF16)
    pat = jnp.dot(pat_ref[...].astype(F32).astype(BF16), spread, preferred_element_type=F32)
    rows_ref[...] = pat
    first, second = kept_rows(pat)
    spot = row_of_four(pat.shape)
    keep = jnp.where((spot == first) | (spot == second), 1.0, 0.0)
    delta = student_ref[...].astype(F32) * keep - teacher_ref[...].astype(F32)
    delta = delta * 2.0**SHIFT
    delta = ((delta * jnp.abs(delta)) * (delta * delta)).astype(BF16)
    dst = lax.broadcasted_iota(jnp.int32, (128, 128), 0)
    src = lax.broadcasted_iota(jnp.int32, (128, 128), 1)
    move = jnp.where(src // 32 * 32 + shuffled(src % 32) == dst, 1.0, 0.0).astype(BF16)
    delta = jnp.concatenate([delta, jnp.zeros_like(delta)], axis=0)
    wide = lax.dot_general(
        move, delta, (((1,), (1,)), ((), ())), preferred_element_type=F32
    ).reshape(4, 4, 8, 128)
    for c in range(NC):
        piece = swap_groups([wide[:, q] for q in range(4)], c).reshape(32, 128).astype(BF16)
        for z in range(NZ):
            out_ref[z, c * 32 : (c + 1) * 32, :] = piece


def spread_kernel(got_ref, out_ref, mid_ref):
    got = got_ref[...].astype(F32).reshape(32, 4, 8, 128)
    for q, rows in enumerate(swap_all([got[:, x] for x in range(NX)])):
        mid_ref[:, q] = rows
    rows = mid_ref[...].reshape(1024, 128).astype(BF16)
    for y in range(4):
        out_ref[y] = rows


def decode_kernel(w_ref, high_ref, low_ref):
    for y in range(4):
        for k in range(4):
            sent = w_ref[y, k * 256 : (k + 1) * 256, :].astype(F32)
            size = lax.rsqrt(lax.rsqrt(jnp.abs(sent))) * 2.0**-SHIFT
            delta = jnp.where(sent < 0, -size, size)
            high = delta.astype(BF16)
            at = (y // 2) * 1024 + k * 256
            lane = (y % 2) * 128
            high_ref[at : at + 256, lane : lane + 128] = high
            low_ref[at : at + 256, lane : lane + 128] = (delta - high.astype(F32)).astype(BF16)


def forward(rows, high_ref, low_ref):
    part = jnp.dot(rows, high_ref[...], preferred_element_type=F32)
    part += jnp.dot(rows, low_ref[...], preferred_element_type=F32)
    return part.astype(BF16)


def forward_most_kernel(*refs):
    own, pair, rest = refs[:NX], refs[NX : NX + 3], refs[NX + 3 :]
    high_ref, low_ref, at_ref, out_ref, held_ref, sems = rest
    loads = [pltpu.make_async_copy(pair[i], held_ref.at[i], sems.at[i]) for i in range(3)]
    for load in loads:
        load.start()
    for i in range(NX):
        out_ref[(at_ref[0] + BACK[i]) % NX, :128] = forward(own[i][...], high_ref, low_ref)
    for i in range(3):
        loads[i].wait()
        x = (at_ref[0] + BACK[SOON[i]]) % NX
        out_ref[x, 128:] = forward(held_ref[i], high_ref, low_ref)
    out_ref[(at_ref[0] + BACK[LAST]) % NX, 128:] = jnp.zeros((128, 256), BF16)


def forward_last_kernel(pair_hbm, part_ref, high_ref, low_ref, at_ref, *rest):
    out_ref, held_ref, sem = rest
    load = pltpu.make_async_copy(pair_hbm, held_ref, sem)
    load.start()
    out_ref[...] = part_ref[...]
    load.wait()
    out_ref[(at_ref[0] + BACK[LAST]) % NX, 128:] = forward(held_ref[...], high_ref, low_ref)


def thirds(value, rows):
    high = value.astype(BF16).astype(F32)
    mid = (value - high).astype(BF16).astype(F32)
    low = value - high - mid
    row = lax.broadcasted_iota(jnp.int32, (rows, value.shape[1]), 0)
    return jnp.where(row == 0, high, jnp.where(row == 1, mid, jnp.where(row == 2, low, 0.0)))


def slope_kernel(part_ref, out_ref, loss_ref):
    diff = part_ref[0].astype(F32)
    for x in range(1, NX):
        diff = diff + part_ref[x].astype(F32)
    slope = diff.astype(BF16)
    for x in range(NX):
        out_ref[x] = slope
    square = diff * diff
    loss_ref[...] = jnp.sum(square[:, :128] + square[:, 128:], axis=0, keepdims=True)


def grad_kernel(*refs):
    own, (soon_ref, last_ref, *rest) = refs[:NX], refs[NX:]
    slope_ref, loss_ref, at_ref, out_ref, s_ref, term_ref = rest
    contract = (((0,), (0,)), ((), ()))
    for i in range(NX):
        x = (at_ref[0] + BACK[i]) % NX
        s_ref[i * 128 : (i + 1) * 128] = slope_ref[x, :128]
        s_ref[512 + i * 128 : 512 + (i + 1) * 128] = slope_ref[x, 128:]
    for k in range(8):
        at = k * 256
        rows = [ref[:, at : at + 256] for ref in own]
        pair = [soon_ref[i, :, at : at + 256] for i in range(3)]
        pair.insert(LAST, last_ref[:, at : at + 256])
        rows += pair
        rows = jnp.concatenate(rows, axis=0)
        term = lax.dot_general(rows, s_ref[...], contract, preferred_element_type=F32)
        for yh in range(2):
            term_ref[(k // 4) * 2 + yh, (k % 4) * 8 : (k % 4 + 1) * 8] = term[
                :, yh * 128 : (yh + 1) * 128
            ].reshape(8, 4, 8, 128)
    loss = thirds(loss_ref[...], 16).astype(BF16)
    for y in range(4):
        term = term_ref[y].reshape(NZ, NC, 4, 8, 128)
        for c in range(NC):
            for x, rows in enumerate(swap_all([term[:, c, q] for q in range(4)])):
                at = place_in_plane(y // 2, c, y % 2, x)
                out_ref[at, :128, :] = rows.reshape(128, 128).astype(BF16)
                out_ref[at, 128:, :] = loss


def gather_kernel(got_ref, pat_ref, out_ref, mid_ref):
    loss = got_ref[0, 128:, :].astype(F32)
    for i in range(1, 32):
        loss = loss + got_ref[i, 128:, :].astype(F32)
    loss = jnp.sum(jnp.sum(loss, axis=0, keepdims=True), axis=1, keepdims=True)
    loss = thirds(jnp.broadcast_to(loss, (1, 128)), 16)
    lane = lax.broadcasted_iota(jnp.int32, (16, 128), 1)
    mid_ref[:, 32:, :] = jnp.broadcast_to(jnp.where(lane == 0, loss, 0.0), (NZ, 16, 128))
    group = lane_group((NZ, 8, 128))
    for x in range(NX):
        rows = jnp.zeros((NZ, 8, 128), F32)
        for c in range(NC):
            total = jnp.zeros((128, 128), F32)
            for y in range(4):
                total += got_ref[place_in_plane(y // 2, c, y % 2, x), :128, :].astype(F32)
            total = total.reshape(NZ, 8, 128)
            for i, which in enumerate(kept_rows(pat_ref[c, :, x])):
                kept = jnp.where(which == group.astype(F32), total, 0.0)
                kept += pltpu.roll(kept, 64, 2)
                kept += pltpu.roll(kept, 32, 2)
                rows = jnp.where(group == i * 2 + c, kept, rows)
        mid_ref[:, x * 8 : (x + 1) * 8, :] = rows
    out_ref[...] = mid_ref[...].astype(BF16)


def final_kernel(got_ref, pat_ref, out_ref, loss_ref):
    total = got_ref[0].astype(F32)
    for z in range(1, NZ):
        total = total + got_ref[z].astype(F32)
    loss = jnp.sum(jnp.sum(total[32:], axis=0, keepdims=True), axis=1, keepdims=True)
    loss_ref[...] = loss / (TOKENS * KVW)
    kept = total[:32]
    row = lax.broadcasted_iota(jnp.int32, (32, 128), 0)
    col = lax.broadcasted_iota(jnp.int32, (32, 128), 1)
    spread = jnp.where(col // 4 == row, 1.0, 0.0).astype(BF16)
    wide = jnp.zeros((128, 128), F32)
    for _ in range(3):
        part = kept.astype(BF16)
        kept = kept - part.astype(F32)
        wide += lax.dot_general(
            part, spread, (((0,), (0,)), ((), ())), preferred_element_type=F32
        )
    first, second = kept_rows(pat_ref[...])
    spot = row_of_four(wide[:64].shape)
    grad = jnp.where(spot == first, wide[:64], 0.0) + jnp.where(spot == second, wide[64:], 0.0)
    out_ref[...] = grad / jnp.sqrt(F32(TOKENS))


def ring(step):
    return [(i, (i + step) % NX) for i in range(NX)]


def shards(hidden, norm_gain, teacher_k, student_k, keep_pattern):
    z, yl, core, yh, x = (lax.axis_index(a) for a in AXES)
    place = (z * NYL + yl) * NC + core
    at = jnp.stack([x, core, yl, place, yh]).astype(jnp.int32)
    patterns = keep_pattern.T

    packed, pat = call(
        pack_kernel,
        (shape((NZ, 64, 128), BF16), shape((64, 128), F32)),
        teacher_k.T,
        student_k.T,
        patterns,
        at,
        scratch=[
            pltpu.VMEM((64, 128), BF16),
            pltpu.VMEM((64, 128), BF16),
            pltpu.VMEM((64, 128), jnp.int32),
            pltpu.SemaphoreType.DMA((3,)),
        ],
        far=(0, 1, 2),
        grant=60,
        name="pack",
    )
    got_w = lax.all_to_all(packed.reshape(128, 8, 128), ZCX, 0, 0, tiled=True)

    split = call(
        norm_kernel,
        (shape((128, 2048), BF16),) * NX,
        hidden,
        norm_gain.reshape(64, 128),
        at,
        scratch=[
            pltpu.VMEM((128, D), BF16),
            pltpu.VMEM((512, 512), BF16),
            pltpu.VMEM((NX, 128, 2048), BF16),
            pltpu.SemaphoreType.DMA((8,)),
            pltpu.SemaphoreType.DMA((2 * NX,)),
        ],
        flops=2 * 2048 * 512 * 512,
        far=(0,),
        out_far=True,
        grant=60,
        name="norm",
    )
    own = [split[0]] + [lax.ppermute(split[i], "x", ring(STEP[i])) for i in range(1, NX)]
    rows_w = call(
        spread_kernel,
        shape((4, 1024, 128), BF16),
        got_w.reshape(1024, 128),
        scratch=[pltpu.VMEM((32, 4, 8, 128), F32)],
        name="spread",
    )
    all_w = lax.all_to_all(rows_w, Y, 0, 0, tiled=True)

    late, _ = lax.optimization_barrier((patterns, rows_w))
    own_pat = call(
        choose_kernel,
        shape((NC, NZ, NX, 8, 128), F32),
        late,
        at,
        scratch=[pltpu.VMEM((NZ, NYL, NC, NX, 8, 128), F32)],
        name="choose",
    )
    own[3], own_pat = lax.optimization_barrier((own[3], own_pat))
    pair = [lax.ppermute(piece, "core", [(0, 1), (1, 0)]) for piece in own]

    high, low = call(decode_kernel, (shape((2048, 256), BF16),) * 2, all_w, name="decode")

    flops = 2 * 1024 * 2048 * 256
    part, soon = call(
        forward_most_kernel,
        (shape((NX, 256, 256), BF16), shape((3, 128, 2048), BF16)),
        *own,
        *(pair[i] for i in SOON),
        high,
        low,
        at,
        scratch=[pltpu.SemaphoreType.DMA((3,))],
        flops=2 * flops * 7 // 8,
        far=range(NX, NX + 3),
        name="forward_most",
    )
    part, last = call(
        forward_last_kernel,
        (shape((NX, 256, 256), BF16), shape((128, 2048), BF16)),
        pair[LAST],
        part,
        high,
        low,
        at,
        scratch=[pltpu.SemaphoreType.DMA],
        flops=flops // 4,
        far=(0,),
        name="forward_last",
    )
    got_part = lax.all_to_all(part, "x", 0, 0, tiled=True)
    slope, loss_part = call(
        slope_kernel, (shape((NX, 256, 256), BF16), shape((1, 128), F32)), got_part, name="slope"
    )
    slopes = lax.all_to_all(slope, "x", 0, 0, tiled=True)

    term = call(
        grad_kernel,
        shape((32, 144, 128), BF16),
        *own,
        soon,
        last,
        slopes,
        loss_part,
        at,
        scratch=[pltpu.VMEM((1024, 256), BF16), pltpu.VMEM((4, 32, 4, 8, 128), F32)],
        flops=flops,
        name="grad",
    )
    got_term = lax.all_to_all(term, PLANE, 0, 0, tiled=True)
    packed_term = call(
        gather_kernel,
        shape((NZ, 48, 128), BF16),
        got_term,
        own_pat,
        scratch=[pltpu.VMEM((NZ, 48, 128), F32)],
        name="gather",
    )
    got_sum = lax.all_to_all(packed_term, "z", 0, 0, tiled=True)
    grad, loss = call(
        final_kernel,
        (shape((64, 128), F32), shape((1, 1), F32)),
        got_sum,
        pat,
        name="final",
    )
    return grad.T, loss.reshape(())


def solution(mesh):
    fine = Mesh(mesh.devices.reshape(NZ, NYL, NC, NYH, NX), AXES)
    dp, tensor = ("z", "yl", "core"), ("yh", "x")
    in_specs = (P(AXES, None), P(), P(dp, tensor), P(dp, tensor), P(None, tensor))
    out_specs = (P(dp, tensor), P())
    return jax.shard_map(shards, mesh=fine, in_specs=in_specs, out_specs=out_specs, check_vma=False)
```

```python
import jax
import jax.numpy as jnp
from jax import lax
from jax.experimental import pallas as pl
from jax.experimental.pallas import tpu as pltpu
from jax.sharding import Mesh, PartitionSpec as P

F32 = jnp.float32
BF16 = jnp.bfloat16
NZ, NYL, NC, NYH, NX = 16, 2, 2, 2, 4
AXES = ("z", "yl", "core", "yh", "x")
Y = ("yl", "yh")
ZCX = ("z", "core", "x")
PLANE = ("yl", "core", "yh", "x")
D, KVW, TOKENS = 8192, 512, 65536
SHIFT = 34
VMEM = pl.BlockSpec(memory_space=pltpu.VMEM)
SMEM = pl.BlockSpec(memory_space=pltpu.SMEM)
STEP = (0, 2, 1, 3)
BACK = (0, 2, 3, 1)
SOON, LAST = (0, 1, 3), 2


def call(kernel, out_shape, *args, scratch=(), flops=0, name=None, far=(), out_far=False, grant=24):
    size = sum(a.size * a.dtype.itemsize for a in args)
    for o in jax.tree.leaves(out_shape):
        size += o.size * o.dtype.itemsize
    specs = [SMEM if a.shape == (5,) else VMEM for a in args]
    for i in far:
        specs[i] = pl.BlockSpec(memory_space=pl.ANY)
    return pl.pallas_call(
        kernel,
        out_shape=out_shape,
        in_specs=specs,
        out_specs=jax.tree.map(
            lambda _: pl.BlockSpec(memory_space=pl.ANY) if out_far else VMEM, out_shape
        ),
        scratch_shapes=list(scratch),
        name=name,
        cost_estimate=pl.CostEstimate(flops=flops, bytes_accessed=size, transcendentals=0),
        compiler_params=pltpu.CompilerParams(vmem_limit_bytes=grant * 1024 * 1024),
    )(*args)


def shape(dims, dtype):
    return jax.ShapeDtypeStruct(dims, dtype)


def lane_group(dims):
    return lax.broadcasted_iota(jnp.int32, dims, len(dims) - 1) // 32


def place_in_plane(yl, c, yh, x):
    return ((yl * NC + c) * NYH + yh) * NX + x


def swap_groups(parts, place):
    total = None
    for b, part in enumerate(parts):
        shift = (b - place) * 32 % 128
        moved = pltpu.roll(part, shift, part.ndim - 1) if shift else part
        here = jnp.where(lane_group(part.shape) == b, moved, 0.0)
        total = here if total is None else total + here
    return total


def swap_all(parts):
    axis = parts[0].ndim - 1
    group = lane_group(parts[0].shape)
    low, even = group < 2, group % 2 == 0
    half = []
    for a, b in ((0, 2), (1, 3)):
        half.append(jnp.where(low, parts[a], pltpu.roll(parts[b], 64, axis)))
        half.append(jnp.where(low, pltpu.roll(parts[a], 64, axis), parts[b]))
    out = []
    for a, b in ((half[0], half[2]), (half[1], half[3])):
        out.append(jnp.where(even, a, pltpu.roll(b, 32, axis)))
        out.append(jnp.where(even, pltpu.roll(a, 96, axis), b))
    return out


def kept_rows(pat):
    first = jnp.where(pat > 2.5, 1.0, 0.0) + jnp.where(pat > 4.5, 1.0, 0.0)
    second = jnp.where(pat < 2.5, pat + 1.0, jnp.where(pat < 3.5, 2.0, 3.0))
    return first, second


def row_of_four(dims):
    return (lax.broadcasted_iota(jnp.int32, dims, 1) % 4).astype(F32)


def shuffled(place):
    return place % 4 * 8 + place // 4


def norm_kernel(x_hbm, gain_ref, at_ref, *rest):
    outs, (x_ref, move_ref, split_ref, sems, out_sems) = rest[:NX], rest[NX:]
    loads = [
        pltpu.make_async_copy(x_hbm.at[:, cut], x_ref.at[:, cut], sems.at[i])
        for i, cut in enumerate(pl.ds(i * 1024, 1024) for i in range(8))
    ]
    for load in loads:
        load.start()
    src = lax.broadcasted_iota(jnp.int32, (512, 128), 0)
    dst = lax.broadcasted_iota(jnp.int32, (512, 128), 1)
    goal = ((src >> 5 & 3) << 7) + (src >> 7 << 5) + ((src & 3) << 3) + (src >> 2 & 7)
    for x in range(NX):
        move_ref[:, x * 128 : (x + 1) * 128] = jnp.where(goal == dst + x * 128, 1.0, 0.0).astype(BF16)
    total = jnp.zeros((128, 128), F32)
    for g in range(64):
        if g % 8 == 0:
            loads[g // 8].wait()
        part = x_ref[:, g * 128 : (g + 1) * 128].astype(F32)
        total += part * part
    factor = lax.rsqrt(jnp.sum(total, axis=1, keepdims=True) / D + 1e-05)
    factor = jnp.broadcast_to(factor, (128, 128))
    gain = gain_ref[...].astype(F32)
    stores = []
    for yl in range(2):
        for m in range(8):
            tile = yl * 8 + m
            parts = []
            for b in range(4):
                block = 8 * m + 4 * (b // 2) + 2 * yl + b % 2
                part = x_ref[:, block * 128 : (block + 1) * 128].astype(F32)
                parts.append((part * factor * gain[block : block + 1, :]).astype(BF16))
            parts = jnp.concatenate(parts, axis=1)
            seg = jnp.dot(parts, move_ref[...], preferred_element_type=F32).astype(BF16)
            for x in range(NX):
                split_ref[x, :, tile * 128 : (tile + 1) * 128] = seg[:, x * 128 : (x + 1) * 128]
        for i in range(NX):
            cut = pl.ds(yl * 1024, 1024)
            piece = split_ref.at[(at_ref[0] + STEP[i]) % NX]
            stores.append(
                pltpu.make_async_copy(piece.at[:, cut], outs[i].at[:, cut], out_sems.at[yl * NX + i])
            )
            stores[-1].start()
    for store in stores:
        store.wait()


def choose_kernel(pat_ref, at_ref, out_ref, pick_ref):
    pats = pat_ref[...].astype(F32).astype(BF16)
    col = lax.broadcasted_iota(jnp.int32, (64, 128), 0)
    lane = lax.broadcasted_iota(jnp.int32, (64, 128), 1)
    for c in range(NC):
        pick = jnp.where(col - c * 32 == lane % 32, 1.0, 0.0).astype(BF16)
        chosen = lax.dot_general(pats, pick, (((0,), (0,)), ((), ())), preferred_element_type=F32)
        pick_ref[...] = chosen.reshape(NZ, NYL, NC, NX, 8, 128)
        out_ref[c] = pick_ref[:, at_ref[2], at_ref[1]]


def pack_kernel(teacher_hbm, student_hbm, pat_hbm, at_ref, out_ref, rows_ref, *scratch):
    teacher_ref, student_ref, pat_ref, sems = scratch
    place = at_ref[3]
    window = pl.ds(pl.multiple_of(place // 4 * 128, 128), 128)
    loads = [
        pltpu.make_async_copy(pat_hbm.at[:, window], pat_ref, sems.at[0]),
        pltpu.make_async_copy(teacher_hbm, teacher_ref, sems.at[1]),
        pltpu.make_async_copy(student_hbm, student_ref, sems.at[2]),
    ]
    for load in loads:
        load.start()
    for load in loads:
        load.wait()
    row = lax.broadcasted_iota(jnp.int32, (128, 128), 0)
    col = lax.broadcasted_iota(jnp.int32, (128, 128), 1)
    spread = jnp.where(col // 4 + place % 4 * 32 == row, 1.0, 0.0).astype(BF16)
    pat = jnp.dot(pat_ref[...].astype(F32).astype(BF16), spread, preferred_element_type=F32)
    rows_ref[...] = pat
    first, second = kept_rows(pat)
    spot = row_of_four(pat.shape)
    keep = jnp.where((spot == first) | (spot == second), 1.0, 0.0)
    delta = student_ref[...].astype(F32) * keep - teacher_ref[...].astype(F32)
    delta = delta * 2.0**SHIFT
    delta = ((delta * jnp.abs(delta)) * (delta * delta)).astype(BF16)
    dst = lax.broadcasted_iota(jnp.int32, (128, 128), 0)
    src = lax.broadcasted_iota(jnp.int32, (128, 128), 1)
    move = jnp.where(src // 32 * 32 + shuffled(src % 32) == dst, 1.0, 0.0).astype(BF16)
    delta = jnp.concatenate([delta, jnp.zeros_like(delta)], axis=0)
    wide = lax.dot_general(
        move, delta, (((1,), (1,)), ((), ())), preferred_element_type=F32
    ).reshape(4, 4, 8, 128)
    for c in range(NC):
        piece = swap_groups([wide[:, q] for q in range(4)], c).reshape(32, 128).astype(BF16)
        for z in range(NZ):
            out_ref[z, c * 32 : (c + 1) * 32, :] = piece


def spread_kernel(got_ref, out_ref, mid_ref):
    got = got_ref[...].astype(F32).reshape(32, 4, 8, 128)
    for q, rows in enumerate(swap_all([got[:, x] for x in range(NX)])):
        mid_ref[:, q] = rows
    rows = mid_ref[...].reshape(1024, 128).astype(BF16)
    for y in range(4):
        out_ref[y] = rows


def decode_kernel(w_ref, high_ref, low_ref):
    for y in range(4):
        for k in range(4):
            sent = w_ref[y, k * 256 : (k + 1) * 256, :].astype(F32)
            size = lax.rsqrt(lax.rsqrt(jnp.abs(sent))) * 2.0**-SHIFT
            delta = jnp.where(sent < 0, -size, size)
            high = delta.astype(BF16)
            at = (y // 2) * 1024 + k * 256
            lane = (y % 2) * 128
            high_ref[at : at + 256, lane : lane + 128] = high
            low_ref[at : at + 256, lane : lane + 128] = (delta - high.astype(F32)).astype(BF16)


def forward(rows, high_ref, low_ref):
    part = jnp.dot(rows, high_ref[...], preferred_element_type=F32)
    part += jnp.dot(rows, low_ref[...], preferred_element_type=F32)
    return part.astype(BF16)


def forward_most_kernel(*refs):
    pieces, (high_ref, low_ref, at_ref, out_ref, held_ref, sems) = refs[: NX + 3], refs[NX + 3 :]
    loads = [
        pltpu.make_async_copy(piece, held_ref.at[i], sems.at[i]) for i, piece in enumerate(pieces)
    ]
    for load in loads:
        load.start()
    for i, load in enumerate(loads):
        load.wait()
        back, row = (BACK[i], 0) if i < NX else (BACK[SOON[i - NX]], 128)
        x = (at_ref[0] + back) % NX
        out_ref[x, row : row + 128] = forward(held_ref[i], high_ref, low_ref)
    out_ref[(at_ref[0] + BACK[LAST]) % NX, 128:] = jnp.zeros((128, 256), BF16)


def forward_last_kernel(pair_hbm, part_ref, high_ref, low_ref, at_ref, *rest):
    out_ref, held_ref, sem = rest
    load = pltpu.make_async_copy(pair_hbm, held_ref, sem)
    load.start()
    out_ref[...] = part_ref[...]
    load.wait()
    out_ref[(at_ref[0] + BACK[LAST]) % NX, 128:] = forward(held_ref[...], high_ref, low_ref)


def thirds(value, rows):
    high = value.astype(BF16).astype(F32)
    mid = (value - high).astype(BF16).astype(F32)
    low = value - high - mid
    row = lax.broadcasted_iota(jnp.int32, (rows, value.shape[1]), 0)
    return jnp.where(row == 0, high, jnp.where(row == 1, mid, jnp.where(row == 2, low, 0.0)))


def slope_kernel(part_ref, out_ref, loss_ref):
    diff = part_ref[0].astype(F32)
    for x in range(1, NX):
        diff = diff + part_ref[x].astype(F32)
    slope = diff.astype(BF16)
    for x in range(NX):
        out_ref[x] = slope
    square = diff * diff
    loss_ref[...] = jnp.sum(square[:, :128] + square[:, 128:], axis=0, keepdims=True)


def grad_kernel(*refs):
    held_ref, last_ref, slope_ref, loss_ref, at_ref, out_ref, s_ref, term_ref = refs
    contract = (((0,), (0,)), ((), ()))
    for i in range(NX):
        x = (at_ref[0] + BACK[i]) % NX
        s_ref[i * 128 : (i + 1) * 128] = slope_ref[x, :128]
        s_ref[512 + i * 128 : 512 + (i + 1) * 128] = slope_ref[x, 128:]
    for k in range(8):
        at = k * 256
        rows = [held_ref[i, :, at : at + 256] for i in range(NX + 3)]
        rows.insert(NX + LAST, last_ref[:, at : at + 256])
        rows = jnp.concatenate(rows, axis=0)
        term = lax.dot_general(rows, s_ref[...], contract, preferred_element_type=F32)
        for yh in range(2):
            term_ref[(k // 4) * 2 + yh, (k % 4) * 8 : (k % 4 + 1) * 8] = term[
                :, yh * 128 : (yh + 1) * 128
            ].reshape(8, 4, 8, 128)
    loss = thirds(loss_ref[...], 16).astype(BF16)
    for y in range(4):
        term = term_ref[y].reshape(NZ, NC, 4, 8, 128)
        for c in range(NC):
            for x, rows in enumerate(swap_all([term[:, c, q] for q in range(4)])):
                at = place_in_plane(y // 2, c, y % 2, x)
                out_ref[at, :128, :] = rows.reshape(128, 128).astype(BF16)
                out_ref[at, 128:, :] = loss


def gather_kernel(got_ref, pat_ref, out_ref, mid_ref):
    loss = got_ref[0, 128:, :].astype(F32)
    for i in range(1, 32):
        loss = loss + got_ref[i, 128:, :].astype(F32)
    loss = jnp.sum(jnp.sum(loss, axis=0, keepdims=True), axis=1, keepdims=True)
    loss = thirds(jnp.broadcast_to(loss, (1, 128)), 16)
    lane = lax.broadcasted_iota(jnp.int32, (16, 128), 1)
    mid_ref[:, 32:, :] = jnp.broadcast_to(jnp.where(lane == 0, loss, 0.0), (NZ, 16, 128))
    group = lane_group((NZ, 8, 128))
    for x in range(NX):
        rows = jnp.zeros((NZ, 8, 128), F32)
        for c in range(NC):
            total = jnp.zeros((128, 128), F32)
            for y in range(4):
                total += got_ref[place_in_plane(y // 2, c, y % 2, x), :128, :].astype(F32)
            total = total.reshape(NZ, 8, 128)
            for i, which in enumerate(kept_rows(pat_ref[c, :, x])):
                kept = jnp.where(which == group.astype(F32), total, 0.0)
                kept += pltpu.roll(kept, 64, 2)
                kept += pltpu.roll(kept, 32, 2)
                rows = jnp.where(group == i * 2 + c, kept, rows)
        mid_ref[:, x * 8 : (x + 1) * 8, :] = rows
    out_ref[...] = mid_ref[...].astype(BF16)


def final_kernel(got_ref, pat_ref, out_ref, loss_ref):
    total = got_ref[0].astype(F32)
    for z in range(1, NZ):
        total = total + got_ref[z].astype(F32)
    loss = jnp.sum(jnp.sum(total[32:], axis=0, keepdims=True), axis=1, keepdims=True)
    loss_ref[...] = loss / (TOKENS * KVW)
    kept = total[:32]
    row = lax.broadcasted_iota(jnp.int32, (32, 128), 0)
    col = lax.broadcasted_iota(jnp.int32, (32, 128), 1)
    spread = jnp.where(col // 4 == row, 1.0, 0.0).astype(BF16)
    wide = jnp.zeros((128, 128), F32)
    for _ in range(3):
        part = kept.astype(BF16)
        kept = kept - part.astype(F32)
        wide += lax.dot_general(
            part, spread, (((0,), (0,)), ((), ())), preferred_element_type=F32
        )
    first, second = kept_rows(pat_ref[...])
    spot = row_of_four(wide[:64].shape)
    grad = jnp.where(spot == first, wide[:64], 0.0) + jnp.where(spot == second, wide[64:], 0.0)
    out_ref[...] = grad / jnp.sqrt(F32(TOKENS))


def ring(step):
    return [(i, (i + step) % NX) for i in range(NX)]


def shards(hidden, norm_gain, teacher_k, student_k, keep_pattern):
    z, yl, core, yh, x = (lax.axis_index(a) for a in AXES)
    place = (z * NYL + yl) * NC + core
    at = jnp.stack([x, core, yl, place, yh]).astype(jnp.int32)
    patterns = keep_pattern.T

    packed, pat = call(
        pack_kernel,
        (shape((NZ, 64, 128), BF16), shape((64, 128), F32)),
        teacher_k.T,
        student_k.T,
        patterns,
        at,
        scratch=[
            pltpu.VMEM((64, 128), BF16),
            pltpu.VMEM((64, 128), BF16),
            pltpu.VMEM((64, 128), jnp.int32),
            pltpu.SemaphoreType.DMA((3,)),
        ],
        far=(0, 1, 2),
        grant=60,
        name="pack",
    )
    got_w = lax.all_to_all(packed.reshape(128, 8, 128), ZCX, 0, 0, tiled=True)

    split = call(
        norm_kernel,
        (shape((128, 2048), BF16),) * NX,
        hidden,
        norm_gain.reshape(64, 128),
        at,
        scratch=[
            pltpu.VMEM((128, D), BF16),
            pltpu.VMEM((512, 512), BF16),
            pltpu.VMEM((NX, 128, 2048), BF16),
            pltpu.SemaphoreType.DMA((8,)),
            pltpu.SemaphoreType.DMA((2 * NX,)),
        ],
        flops=2 * 2048 * 512 * 512,
        far=(0,),
        out_far=True,
        grant=60,
        name="norm",
    )
    own = [split[0]] + [lax.ppermute(split[i], "x", ring(STEP[i])) for i in range(1, NX)]
    rows_w = call(
        spread_kernel,
        shape((4, 1024, 128), BF16),
        got_w.reshape(1024, 128),
        scratch=[pltpu.VMEM((32, 4, 8, 128), F32)],
        name="spread",
    )
    all_w = lax.all_to_all(rows_w, Y, 0, 0, tiled=True)

    late, _ = lax.optimization_barrier((patterns, rows_w))
    own_pat = call(
        choose_kernel,
        shape((NC, NZ, NX, 8, 128), F32),
        late,
        at,
        scratch=[pltpu.VMEM((NZ, NYL, NC, NX, 8, 128), F32)],
        name="choose",
    )
    own[3], own_pat = lax.optimization_barrier((own[3], own_pat))
    pair = [lax.ppermute(piece, "core", [(0, 1), (1, 0)]) for piece in own]

    high, low = call(decode_kernel, (shape((2048, 256), BF16),) * 2, all_w, name="decode")

    flops = 2 * 1024 * 2048 * 256
    part, held = call(
        forward_most_kernel,
        (shape((NX, 256, 256), BF16), shape((NX + 3, 128, 2048), BF16)),
        *own,
        *(pair[i] for i in SOON),
        high,
        low,
        at,
        scratch=[pltpu.SemaphoreType.DMA((NX + 3,))],
        flops=2 * flops * 7 // 8,
        far=range(NX + 3),
        name="forward_most",
    )
    part, last = call(
        forward_last_kernel,
        (shape((NX, 256, 256), BF16), shape((128, 2048), BF16)),
        pair[LAST],
        part,
        high,
        low,
        at,
        scratch=[pltpu.SemaphoreType.DMA],
        flops=flops // 4,
        far=(0,),
        name="forward_last",
    )
    got_part = lax.all_to_all(part, "x", 0, 0, tiled=True)
    slope, loss_part = call(
        slope_kernel, (shape((NX, 256, 256), BF16), shape((1, 128), F32)), got_part, name="slope"
    )
    slopes = lax.all_to_all(slope, "x", 0, 0, tiled=True)

    term = call(
        grad_kernel,
        shape((32, 144, 128), BF16),
        held,
        last,
        slopes,
        loss_part,
        at,
        scratch=[pltpu.VMEM((1024, 256), BF16), pltpu.VMEM((4, 32, 4, 8, 128), F32)],
        flops=flops,
        name="grad",
    )
    got_term = lax.all_to_all(term, PLANE, 0, 0, tiled=True)
    packed_term = call(
        gather_kernel,
        shape((NZ, 48, 128), BF16),
        got_term,
        own_pat,
        scratch=[pltpu.VMEM((NZ, 48, 128), F32)],
        name="gather",
    )
    got_sum = lax.all_to_all(packed_term, "z", 0, 0, tiled=True)
    grad, loss = call(
        final_kernel,
        (shape((64, 128), F32), shape((1, 1), F32)),
        got_sum,
        pat,
        name="final",
    )
    return grad.T, loss.reshape(())


def solution(mesh):
    fine = Mesh(mesh.devices.reshape(NZ, NYL, NC, NYH, NX), AXES)
    dp, tensor = ("z", "yl", "core"), ("yh", "x")
    in_specs = (P(AXES, None), P(), P(dp, tensor), P(dp, tensor), P(None, tensor))
    out_specs = (P(dp, tensor), P())
    return jax.shard_map(shards, mesh=fine, in_specs=in_specs, out_specs=out_specs, check_vma=False)
```

```python
import jax
import jax.numpy as jnp
from jax import lax
from jax.experimental import pallas as pl
from jax.experimental.pallas import tpu as pltpu
from jax.sharding import Mesh, PartitionSpec as P

F32 = jnp.float32
BF16 = jnp.bfloat16
NZ, NYL, NC, NYH, NX = 16, 2, 2, 2, 4
AXES = ("z", "yl", "core", "yh", "x")
Y = ("yl", "yh")
ZCX = ("z", "core", "x")
PLANE = ("yl", "core", "yh", "x")
D, KVW, TOKENS = 8192, 512, 65536
SHIFT = 34
VMEM = pl.BlockSpec(memory_space=pltpu.VMEM)
SMEM = pl.BlockSpec(memory_space=pltpu.SMEM)
STEP = (0, 2, 1, 3)
BACK = (0, 2, 3, 1)
SOON, LAST = (0, 1, 3), 2


def call(kernel, out_shape, *args, scratch=(), flops=0, name=None, far=(), out_far=False, grant=24):
    size = sum(a.size * a.dtype.itemsize for a in args)
    for o in jax.tree.leaves(out_shape):
        size += o.size * o.dtype.itemsize
    specs = [SMEM if a.shape == (5,) else VMEM for a in args]
    for i in far:
        specs[i] = pl.BlockSpec(memory_space=pl.ANY)
    return pl.pallas_call(
        kernel,
        out_shape=out_shape,
        in_specs=specs,
        out_specs=jax.tree.map(
            lambda _: pl.BlockSpec(memory_space=pl.ANY) if out_far else VMEM, out_shape
        ),
        scratch_shapes=list(scratch),
        name=name,
        cost_estimate=pl.CostEstimate(flops=flops, bytes_accessed=size, transcendentals=0),
        compiler_params=pltpu.CompilerParams(vmem_limit_bytes=grant * 1024 * 1024),
    )(*args)


def shape(dims, dtype):
    return jax.ShapeDtypeStruct(dims, dtype)


def lane_group(dims):
    return lax.broadcasted_iota(jnp.int32, dims, len(dims) - 1) // 32


def place_in_plane(yl, c, yh, x):
    return ((yl * NC + c) * NYH + yh) * NX + x


def swap_groups(parts, place):
    total = None
    for b, part in enumerate(parts):
        shift = (b - place) * 32 % 128
        moved = pltpu.roll(part, shift, part.ndim - 1) if shift else part
        here = jnp.where(lane_group(part.shape) == b, moved, 0.0)
        total = here if total is None else total + here
    return total


def swap_all(parts):
    axis = parts[0].ndim - 1
    group = lane_group(parts[0].shape)
    low, even = group < 2, group % 2 == 0
    half = []
    for a, b in ((0, 2), (1, 3)):
        half.append(jnp.where(low, parts[a], pltpu.roll(parts[b], 64, axis)))
        half.append(jnp.where(low, pltpu.roll(parts[a], 64, axis), parts[b]))
    out = []
    for a, b in ((half[0], half[2]), (half[1], half[3])):
        out.append(jnp.where(even, a, pltpu.roll(b, 32, axis)))
        out.append(jnp.where(even, pltpu.roll(a, 96, axis), b))
    return out


def kept_rows(pat):
    first = jnp.where(pat > 2.5, 1.0, 0.0) + jnp.where(pat > 4.5, 1.0, 0.0)
    second = jnp.where(pat < 2.5, pat + 1.0, jnp.where(pat < 3.5, 2.0, 3.0))
    return first, second


def row_of_four(dims):
    return (lax.broadcasted_iota(jnp.int32, dims, 1) % 4).astype(F32)


def shuffled(place):
    return place % 4 * 8 + place // 4


def norm_kernel(x_hbm, gain_ref, at_ref, *rest):
    outs, (x_ref, move_ref, split_ref, sems, out_sems) = rest[:NX], rest[NX:]
    loads = [
        pltpu.make_async_copy(x_hbm.at[:, cut], x_ref.at[:, cut], sems.at[i])
        for i, cut in enumerate(pl.ds(i * 1024, 1024) for i in range(8))
    ]
    for load in loads:
        load.start()
    src = lax.broadcasted_iota(jnp.int32, (512, 128), 0)
    dst = lax.broadcasted_iota(jnp.int32, (512, 128), 1)
    goal = ((src >> 5 & 3) << 7) + (src >> 7 << 5) + ((src & 3) << 3) + (src >> 2 & 7)
    for x in range(NX):
        move_ref[:, x * 128 : (x + 1) * 128] = jnp.where(goal == dst + x * 128, 1.0, 0.0).astype(BF16)
    total = jnp.zeros((128, 128), F32)
    for g in range(64):
        if g % 8 == 0:
            loads[g // 8].wait()
        part = x_ref[:, g * 128 : (g + 1) * 128].astype(F32)
        total += part * part
    factor = lax.rsqrt(jnp.sum(total, axis=1, keepdims=True) / D + 1e-05)
    factor = jnp.broadcast_to(factor, (128, 128))
    gain = gain_ref[...].astype(F32)
    stores = []
    for yl in range(2):
        for m in range(8):
            tile = yl * 8 + m
            parts = []
            for b in range(4):
                block = 8 * m + 4 * (b // 2) + 2 * yl + b % 2
                part = x_ref[:, block * 128 : (block + 1) * 128].astype(F32)
                parts.append((part * factor * gain[block : block + 1, :]).astype(BF16))
            parts = jnp.concatenate(parts, axis=1)
            seg = jnp.dot(parts, move_ref[...], preferred_element_type=F32).astype(BF16)
            for x in range(NX):
                split_ref[x, :, tile * 128 : (tile + 1) * 128] = seg[:, x * 128 : (x + 1) * 128]
        for i in range(NX):
            cut = pl.ds(yl * 1024, 1024)
            piece = split_ref.at[(at_ref[0] + STEP[i]) % NX]
            stores.append(
                pltpu.make_async_copy(piece.at[:, cut], outs[i].at[:, cut], out_sems.at[yl * NX + i])
            )
            stores[-1].start()
    for store in stores:
        store.wait()


def choose_kernel(pat_ref, at_ref, out_ref, pick_ref):
    pats = pat_ref[...].astype(F32).astype(BF16)
    col = lax.broadcasted_iota(jnp.int32, (64, 128), 0)
    lane = lax.broadcasted_iota(jnp.int32, (64, 128), 1)
    for c in range(NC):
        pick = jnp.where(col - c * 32 == lane % 32, 1.0, 0.0).astype(BF16)
        chosen = lax.dot_general(pats, pick, (((0,), (0,)), ((), ())), preferred_element_type=F32)
        pick_ref[...] = chosen.reshape(NZ, NYL, NC, NX, 8, 128)
        out_ref[c] = pick_ref[:, at_ref[2], at_ref[1]]


def pack_kernel(teacher_hbm, student_hbm, pat_hbm, at_ref, out_ref, rows_ref, *scratch):
    teacher_ref, student_ref, pat_ref, sems = scratch
    place = at_ref[3]
    window = pl.ds(pl.multiple_of(place // 4 * 128, 128), 128)
    loads = [
        pltpu.make_async_copy(pat_hbm.at[:, window], pat_ref, sems.at[0]),
        pltpu.make_async_copy(teacher_hbm, teacher_ref, sems.at[1]),
        pltpu.make_async_copy(student_hbm, student_ref, sems.at[2]),
    ]
    for load in loads:
        load.start()
    for load in loads:
        load.wait()
    row = lax.broadcasted_iota(jnp.int32, (128, 128), 0)
    col = lax.broadcasted_iota(jnp.int32, (128, 128), 1)
    spread = jnp.where(col // 4 + place % 4 * 32 == row, 1.0, 0.0).astype(BF16)
    pat = jnp.dot(pat_ref[...].astype(F32).astype(BF16), spread, preferred_element_type=F32)
    rows_ref[...] = pat
    first, second = kept_rows(pat)
    spot = row_of_four(pat.shape)
    keep = jnp.where((spot == first) | (spot == second), 1.0, 0.0)
    delta = student_ref[...].astype(F32) * keep - teacher_ref[...].astype(F32)
    delta = delta * 2.0**SHIFT
    delta = ((delta * jnp.abs(delta)) * (delta * delta)).astype(BF16)
    dst = lax.broadcasted_iota(jnp.int32, (128, 128), 0)
    src = lax.broadcasted_iota(jnp.int32, (128, 128), 1)
    move = jnp.where(src // 32 * 32 + shuffled(src % 32) == dst, 1.0, 0.0).astype(BF16)
    delta = jnp.concatenate([delta, jnp.zeros_like(delta)], axis=0)
    wide = lax.dot_general(
        move, delta, (((1,), (1,)), ((), ())), preferred_element_type=F32
    ).reshape(4, 4, 8, 128)
    for c in range(NC):
        piece = swap_groups([wide[:, q] for q in range(4)], c).reshape(32, 128).astype(BF16)
        for z in range(NZ):
            out_ref[z, c * 32 : (c + 1) * 32, :] = piece


def spread_kernel(got_ref, out_ref, mid_ref):
    got = got_ref[...].astype(F32).reshape(32, 4, 8, 128)
    for q, rows in enumerate(swap_all([got[:, x] for x in range(NX)])):
        mid_ref[:, q] = rows
    rows = mid_ref[...].reshape(1024, 128).astype(BF16)
    for y in range(4):
        out_ref[y] = rows


def decode_kernel(w_ref, high_ref, low_ref):
    for y in range(4):
        for k in range(4):
            sent = w_ref[y, k * 256 : (k + 1) * 256, :].astype(F32)
            size = lax.rsqrt(lax.rsqrt(jnp.abs(sent))) * 2.0**-SHIFT
            delta = jnp.where(sent < 0, -size, size)
            high = delta.astype(BF16)
            at = (y // 2) * 1024 + k * 256
            lane = (y % 2) * 128
            high_ref[at : at + 256, lane : lane + 128] = high
            low_ref[at : at + 256, lane : lane + 128] = (delta - high.astype(F32)).astype(BF16)


def forward(rows, high_ref, low_ref):
    part = jnp.dot(rows, high_ref[...], preferred_element_type=F32)
    part += jnp.dot(rows, low_ref[...], preferred_element_type=F32)
    return part.astype(BF16)


def forward_most_kernel(*refs):
    near, far, rest = refs[:2], refs[2:7], refs[7:]
    high_ref, low_ref, at_ref, out_ref, held_ref, sems = rest
    loads = [pltpu.make_async_copy(piece, held_ref.at[i], sems.at[i]) for i, piece in enumerate(far)]
    for load in loads:
        load.start()
    for i in range(NX + 3):
        if i < 2:
            rows = near[i][...]
        else:
            loads[i - 2].wait()
            rows = held_ref[i - 2]
        back, row = (BACK[i], 0) if i < NX else (BACK[SOON[i - NX]], 128)
        x = (at_ref[0] + back) % NX
        out_ref[x, row : row + 128] = forward(rows, high_ref, low_ref)
    out_ref[(at_ref[0] + BACK[LAST]) % NX, 128:] = jnp.zeros((128, 256), BF16)


def forward_last_kernel(pair_hbm, part_ref, high_ref, low_ref, at_ref, *rest):
    out_ref, held_ref, sem = rest
    load = pltpu.make_async_copy(pair_hbm, held_ref, sem)
    load.start()
    out_ref[...] = part_ref[...]
    load.wait()
    out_ref[(at_ref[0] + BACK[LAST]) % NX, 128:] = forward(held_ref[...], high_ref, low_ref)


def thirds(value, rows):
    high = value.astype(BF16).astype(F32)
    mid = (value - high).astype(BF16).astype(F32)
    low = value - high - mid
    row = lax.broadcasted_iota(jnp.int32, (rows, value.shape[1]), 0)
    return jnp.where(row == 0, high, jnp.where(row == 1, mid, jnp.where(row == 2, low, 0.0)))


def slope_kernel(part_ref, out_ref, loss_ref):
    diff = part_ref[0].astype(F32)
    for x in range(1, NX):
        diff = diff + part_ref[x].astype(F32)
    slope = diff.astype(BF16)
    for x in range(NX):
        out_ref[x] = slope
    square = diff * diff
    loss_ref[...] = jnp.sum(square[:, :128] + square[:, 128:], axis=0, keepdims=True)


def grad_kernel(*refs):
    near, (held_ref, last_ref, *rest) = refs[:2], refs[2:]
    slope_ref, loss_ref, at_ref, out_ref, s_ref, term_ref = rest
    contract = (((0,), (0,)), ((), ()))
    for i in range(NX):
        x = (at_ref[0] + BACK[i]) % NX
        s_ref[i * 128 : (i + 1) * 128] = slope_ref[x, :128]
        s_ref[512 + i * 128 : 512 + (i + 1) * 128] = slope_ref[x, 128:]
    for k in range(8):
        at = k * 256
        rows = [ref[:, at : at + 256] for ref in near]
        rows += [held_ref[i, :, at : at + 256] for i in range(NX + 1)]
        rows.insert(NX + LAST, last_ref[:, at : at + 256])
        rows = jnp.concatenate(rows, axis=0)
        term = lax.dot_general(rows, s_ref[...], contract, preferred_element_type=F32)
        for yh in range(2):
            term_ref[(k // 4) * 2 + yh, (k % 4) * 8 : (k % 4 + 1) * 8] = term[
                :, yh * 128 : (yh + 1) * 128
            ].reshape(8, 4, 8, 128)
    loss = thirds(loss_ref[...], 16).astype(BF16)
    for y in range(4):
        term = term_ref[y].reshape(NZ, NC, 4, 8, 128)
        for c in range(NC):
            for x, rows in enumerate(swap_all([term[:, c, q] for q in range(4)])):
                at = place_in_plane(y // 2, c, y % 2, x)
                out_ref[at, :128, :] = rows.reshape(128, 128).astype(BF16)
                out_ref[at, 128:, :] = loss


def gather_kernel(got_ref, pat_ref, out_ref, mid_ref):
    loss = got_ref[0, 128:, :].astype(F32)
    for i in range(1, 32):
        loss = loss + got_ref[i, 128:, :].astype(F32)
    loss = jnp.sum(jnp.sum(loss, axis=0, keepdims=True), axis=1, keepdims=True)
    loss = thirds(jnp.broadcast_to(loss, (1, 128)), 16)
    lane = lax.broadcasted_iota(jnp.int32, (16, 128), 1)
    mid_ref[:, 32:, :] = jnp.broadcast_to(jnp.where(lane == 0, loss, 0.0), (NZ, 16, 128))
    group = lane_group((NZ, 8, 128))
    for x in range(NX):
        rows = jnp.zeros((NZ, 8, 128), F32)
        for c in range(NC):
            total = jnp.zeros((128, 128), F32)
            for y in range(4):
                total += got_ref[place_in_plane(y // 2, c, y % 2, x), :128, :].astype(F32)
            total = total.reshape(NZ, 8, 128)
            for i, which in enumerate(kept_rows(pat_ref[c, :, x])):
                kept = jnp.where(which == group.astype(F32), total, 0.0)
                kept += pltpu.roll(kept, 64, 2)
                kept += pltpu.roll(kept, 32, 2)
                rows = jnp.where(group == i * 2 + c, kept, rows)
        mid_ref[:, x * 8 : (x + 1) * 8, :] = rows
    out_ref[...] = mid_ref[...].astype(BF16)


def final_kernel(got_ref, pat_ref, out_ref, loss_ref):
    total = got_ref[0].astype(F32)
    for z in range(1, NZ):
        total = total + got_ref[z].astype(F32)
    loss = jnp.sum(jnp.sum(total[32:], axis=0, keepdims=True), axis=1, keepdims=True)
    loss_ref[...] = loss / (TOKENS * KVW)
    kept = total[:32]
    row = lax.broadcasted_iota(jnp.int32, (32, 128), 0)
    col = lax.broadcasted_iota(jnp.int32, (32, 128), 1)
    spread = jnp.where(col // 4 == row, 1.0, 0.0).astype(BF16)
    wide = jnp.zeros((128, 128), F32)
    for _ in range(3):
        part = kept.astype(BF16)
        kept = kept - part.astype(F32)
        wide += lax.dot_general(
            part, spread, (((0,), (0,)), ((), ())), preferred_element_type=F32
        )
    first, second = kept_rows(pat_ref[...])
    spot = row_of_four(wide[:64].shape)
    grad = jnp.where(spot == first, wide[:64], 0.0) + jnp.where(spot == second, wide[64:], 0.0)
    out_ref[...] = grad / jnp.sqrt(F32(TOKENS))


def ring(step):
    return [(i, (i + step) % NX) for i in range(NX)]


def shards(hidden, norm_gain, teacher_k, student_k, keep_pattern):
    z, yl, core, yh, x = (lax.axis_index(a) for a in AXES)
    place = (z * NYL + yl) * NC + core
    at = jnp.stack([x, core, yl, place, yh]).astype(jnp.int32)
    patterns = keep_pattern.T

    packed, pat = call(
        pack_kernel,
        (shape((NZ, 64, 128), BF16), shape((64, 128), F32)),
        teacher_k.T,
        student_k.T,
        patterns,
        at,
        scratch=[
            pltpu.VMEM((64, 128), BF16),
            pltpu.VMEM((64, 128), BF16),
            pltpu.VMEM((64, 128), jnp.int32),
            pltpu.SemaphoreType.DMA((3,)),
        ],
        far=(0, 1, 2),
        grant=60,
        name="pack",
    )
    got_w = lax.all_to_all(packed.reshape(128, 8, 128), ZCX, 0, 0, tiled=True)

    split = call(
        norm_kernel,
        (shape((128, 2048), BF16),) * NX,
        hidden,
        norm_gain.reshape(64, 128),
        at,
        scratch=[
            pltpu.VMEM((128, D), BF16),
            pltpu.VMEM((512, 512), BF16),
            pltpu.VMEM((NX, 128, 2048), BF16),
            pltpu.SemaphoreType.DMA((8,)),
            pltpu.SemaphoreType.DMA((2 * NX,)),
        ],
        flops=2 * 2048 * 512 * 512,
        far=(0,),
        out_far=True,
        grant=60,
        name="norm",
    )
    own = [split[0]] + [lax.ppermute(split[i], "x", ring(STEP[i])) for i in range(1, NX)]
    rows_w = call(
        spread_kernel,
        shape((4, 1024, 128), BF16),
        got_w.reshape(1024, 128),
        scratch=[pltpu.VMEM((32, 4, 8, 128), F32)],
        name="spread",
    )
    all_w = lax.all_to_all(rows_w, Y, 0, 0, tiled=True)

    late, _ = lax.optimization_barrier((patterns, rows_w))
    own_pat = call(
        choose_kernel,
        shape((NC, NZ, NX, 8, 128), F32),
        late,
        at,
        scratch=[pltpu.VMEM((NZ, NYL, NC, NX, 8, 128), F32)],
        name="choose",
    )
    own[3], own_pat = lax.optimization_barrier((own[3], own_pat))
    pair = [lax.ppermute(piece, "core", [(0, 1), (1, 0)]) for piece in own]

    high, low = call(decode_kernel, (shape((2048, 256), BF16),) * 2, all_w, name="decode")

    flops = 2 * 1024 * 2048 * 256
    part, held = call(
        forward_most_kernel,
        (shape((NX, 256, 256), BF16), shape((NX + 1, 128, 2048), BF16)),
        *own,
        *(pair[i] for i in SOON),
        high,
        low,
        at,
        scratch=[pltpu.SemaphoreType.DMA((NX + 1,))],
        flops=2 * flops * 7 // 8,
        far=range(2, NX + 3),
        name="forward_most",
    )
    part, last = call(
        forward_last_kernel,
        (shape((NX, 256, 256), BF16), shape((128, 2048), BF16)),
        pair[LAST],
        part,
        high,
        low,
        at,
        scratch=[pltpu.SemaphoreType.DMA],
        flops=flops // 4,
        far=(0,),
        name="forward_last",
    )
    got_part = lax.all_to_all(part, "x", 0, 0, tiled=True)
    slope, loss_part = call(
        slope_kernel, (shape((NX, 256, 256), BF16), shape((1, 128), F32)), got_part, name="slope"
    )
    slopes = lax.all_to_all(slope, "x", 0, 0, tiled=True)

    term = call(
        grad_kernel,
        shape((32, 144, 128), BF16),
        own[0],
        own[1],
        held,
        last,
        slopes,
        loss_part,
        at,
        scratch=[pltpu.VMEM((1024, 256), BF16), pltpu.VMEM((4, 32, 4, 8, 128), F32)],
        flops=flops,
        name="grad",
    )
    got_term = lax.all_to_all(term, PLANE, 0, 0, tiled=True)
    packed_term = call(
        gather_kernel,
        shape((NZ, 48, 128), BF16),
        got_term,
        own_pat,
        scratch=[pltpu.VMEM((NZ, 48, 128), F32)],
        name="gather",
    )
    got_sum = lax.all_to_all(packed_term, "z", 0, 0, tiled=True)
    grad, loss = call(
        final_kernel,
        (shape((64, 128), F32), shape((1, 1), F32)),
        got_sum,
        pat,
        name="final",
    )
    return grad.T, loss.reshape(())


def solution(mesh):
    fine = Mesh(mesh.devices.reshape(NZ, NYL, NC, NYH, NX), AXES)
    dp, tensor = ("z", "yl", "core"), ("yh", "x")
    in_specs = (P(AXES, None), P(), P(dp, tensor), P(dp, tensor), P(None, tensor))
    out_specs = (P(dp, tensor), P())
    return jax.shard_map(shards, mesh=fine, in_specs=in_specs, out_specs=out_specs, check_vma=False)
```

```python
import jax
import jax.numpy as jnp
from jax import lax
from jax.experimental import pallas as pl
from jax.experimental.pallas import tpu as pltpu
from jax.sharding import Mesh, PartitionSpec as P

F32 = jnp.float32
BF16 = jnp.bfloat16
NZ, NYL, NC, NYH, NX = 16, 2, 2, 2, 4
AXES = ("z", "yl", "core", "yh", "x")
Y = ("yl", "yh")
ZCX = ("z", "core", "x")
PLANE = ("yl", "core", "yh", "x")
D, KVW, TOKENS = 8192, 512, 65536
SHIFT = 34
VMEM = pl.BlockSpec(memory_space=pltpu.VMEM)
SMEM = pl.BlockSpec(memory_space=pltpu.SMEM)
STEP = (0, 2, 1, 3)
BACK = (0, 2, 3, 1)
SOON, LAST = (0, 1, 3), 2


def call(kernel, out_shape, *args, scratch=(), flops=0, name=None, far=(), out_far=False, grant=24):
    size = sum(a.size * a.dtype.itemsize for a in args)
    for o in jax.tree.leaves(out_shape):
        size += o.size * o.dtype.itemsize
    specs = [SMEM if a.shape in ((1,), (5,)) else VMEM for a in args]
    for i in far:
        specs[i] = pl.BlockSpec(memory_space=pl.ANY)
    return pl.pallas_call(
        kernel,
        out_shape=out_shape,
        in_specs=specs,
        out_specs=jax.tree.map(
            lambda _: pl.BlockSpec(memory_space=pl.ANY) if out_far else VMEM, out_shape
        ),
        scratch_shapes=list(scratch),
        name=name,
        cost_estimate=pl.CostEstimate(flops=flops, bytes_accessed=size, transcendentals=0),
        compiler_params=pltpu.CompilerParams(vmem_limit_bytes=grant * 1024 * 1024),
    )(*args)


def shape(dims, dtype):
    return jax.ShapeDtypeStruct(dims, dtype)


def lane_group(dims):
    return lax.broadcasted_iota(jnp.int32, dims, len(dims) - 1) // 32


def place_in_plane(yl, c, yh, x):
    return ((yl * NC + c) * NYH + yh) * NX + x


def swap_groups(parts, place):
    total = None
    for b, part in enumerate(parts):
        shift = (b - place) * 32 % 128
        moved = pltpu.roll(part, shift, part.ndim - 1) if shift else part
        here = jnp.where(lane_group(part.shape) == b, moved, 0.0)
        total = here if total is None else total + here
    return total


def swap_all(parts):
    axis = parts[0].ndim - 1
    group = lane_group(parts[0].shape)
    low, even = group < 2, group % 2 == 0
    half = []
    for a, b in ((0, 2), (1, 3)):
        half.append(jnp.where(low, parts[a], pltpu.roll(parts[b], 64, axis)))
        half.append(jnp.where(low, pltpu.roll(parts[a], 64, axis), parts[b]))
    out = []
    for a, b in ((half[0], half[2]), (half[1], half[3])):
        out.append(jnp.where(even, a, pltpu.roll(b, 32, axis)))
        out.append(jnp.where(even, pltpu.roll(a, 96, axis), b))
    return out


def kept_rows(pat):
    first = jnp.where(pat > 2.5, 1.0, 0.0) + jnp.where(pat > 4.5, 1.0, 0.0)
    second = jnp.where(pat < 2.5, pat + 1.0, jnp.where(pat < 3.5, 2.0, 3.0))
    return first, second


def row_of_four(dims):
    return (lax.broadcasted_iota(jnp.int32, dims, 1) % 4).astype(F32)


def shuffled(place):
    return place % 4 * 8 + place // 4


def norm_kernel(x_hbm, gain_ref, at_ref, *rest):
    outs, (x_ref, move_ref, split_ref, sems, out_sems) = rest[:NX], rest[NX:]
    loads = [
        pltpu.make_async_copy(x_hbm.at[:, cut], x_ref.at[:, cut], sems.at[i])
        for i, cut in enumerate(pl.ds(i * 1024, 1024) for i in range(8))
    ]
    for load in loads:
        load.start()
    src = lax.broadcasted_iota(jnp.int32, (512, 128), 0)
    dst = lax.broadcasted_iota(jnp.int32, (512, 128), 1)
    goal = ((src >> 5 & 3) << 7) + (src >> 7 << 5) + ((src & 3) << 3) + (src >> 2 & 7)
    for x in range(NX):
        move_ref[:, x * 128 : (x + 1) * 128] = jnp.where(goal == dst + x * 128, 1.0, 0.0).astype(BF16)
    total = jnp.zeros((128, 128), F32)
    for g in range(64):
        if g % 8 == 0:
            loads[g // 8].wait()
        part = x_ref[:, g * 128 : (g + 1) * 128].astype(F32)
        total += part * part
    factor = lax.rsqrt(jnp.sum(total, axis=1, keepdims=True) / D + 1e-05)
    factor = jnp.broadcast_to(factor, (128, 128))
    gain = gain_ref[...].astype(F32)
    stores = []
    for yl in range(2):
        for m in range(8):
            tile = yl * 8 + m
            parts = []
            for b in range(4):
                block = 8 * m + 4 * (b // 2) + 2 * yl + b % 2
                part = x_ref[:, block * 128 : (block + 1) * 128].astype(F32)
                parts.append((part * factor * gain[block : block + 1, :]).astype(BF16))
            parts = jnp.concatenate(parts, axis=1)
            seg = jnp.dot(parts, move_ref[...], preferred_element_type=F32).astype(BF16)
            for x in range(NX):
                split_ref[x, :, tile * 128 : (tile + 1) * 128] = seg[:, x * 128 : (x + 1) * 128]
        for i in range(NX):
            cut = pl.ds(yl * 1024, 1024)
            piece = split_ref.at[(at_ref[0] + STEP[i]) % NX]
            stores.append(
                pltpu.make_async_copy(piece.at[:, cut], outs[i].at[:, cut], out_sems.at[yl * NX + i])
            )
            stores[-1].start()
    for store in stores:
        store.wait()


def choose_kernel(pat_ref, at_ref, out_ref, pick_ref):
    pats = pat_ref[...].astype(F32).astype(BF16)
    col = lax.broadcasted_iota(jnp.int32, (64, 128), 0)
    lane = lax.broadcasted_iota(jnp.int32, (64, 128), 1)
    for c in range(NC):
        pick = jnp.where(col - c * 32 == lane % 32, 1.0, 0.0).astype(BF16)
        chosen = lax.dot_general(pats, pick, (((0,), (0,)), ((), ())), preferred_element_type=F32)
        pick_ref[...] = chosen.reshape(NZ, NYL, NC, NX, 8, 128)
        out_ref[c] = pick_ref[:, at_ref[2], at_ref[1]]


def pack_kernel(teacher_hbm, student_hbm, pat_hbm, at_ref, out_ref, rows_ref, *scratch):
    teacher_ref, student_ref, pat_ref, sems = scratch
    place = at_ref[0]
    window = pl.ds(pl.multiple_of(place // 4 * 128, 128), 128)
    loads = [
        pltpu.make_async_copy(pat_hbm.at[:, window], pat_ref, sems.at[0]),
        pltpu.make_async_copy(teacher_hbm, teacher_ref, sems.at[1]),
        pltpu.make_async_copy(student_hbm, student_ref, sems.at[2]),
    ]
    for load in loads:
        load.start()
    for load in loads:
        load.wait()
    row = lax.broadcasted_iota(jnp.int32, (128, 128), 0)
    col = lax.broadcasted_iota(jnp.int32, (128, 128), 1)
    spread = jnp.where(col // 4 + place % 4 * 32 == row, 1.0, 0.0).astype(BF16)
    pat = jnp.dot(pat_ref[...].astype(F32).astype(BF16), spread, preferred_element_type=F32)
    rows_ref[...] = pat
    first, second = kept_rows(pat)
    spot = row_of_four(pat.shape)
    keep = jnp.where((spot == first) | (spot == second), 1.0, 0.0)
    delta = student_ref[...].astype(F32) * keep - teacher_ref[...].astype(F32)
    delta = delta * 2.0**SHIFT
    delta = ((delta * jnp.abs(delta)) * (delta * delta)).astype(BF16)
    dst = lax.broadcasted_iota(jnp.int32, (128, 128), 0)
    src = lax.broadcasted_iota(jnp.int32, (128, 128), 1)
    move = jnp.where(src // 32 * 32 + shuffled(src % 32) == dst, 1.0, 0.0).astype(BF16)
    delta = jnp.concatenate([delta, jnp.zeros_like(delta)], axis=0)
    wide = lax.dot_general(
        move, delta, (((1,), (1,)), ((), ())), preferred_element_type=F32
    ).reshape(4, 4, 8, 128)
    for c in range(NC):
        piece = swap_groups([wide[:, q] for q in range(4)], c).reshape(32, 128).astype(BF16)
        for z in range(NZ):
            out_ref[z, c * 32 : (c + 1) * 32, :] = piece


def spread_kernel(got_ref, out_ref, mid_ref):
    got = got_ref[...].astype(F32).reshape(32, 4, 8, 128)
    for q, rows in enumerate(swap_all([got[:, x] for x in range(NX)])):
        mid_ref[:, q] = rows
    rows = mid_ref[...].reshape(1024, 128).astype(BF16)
    for y in range(4):
        out_ref[y] = rows


def decode_kernel(w_ref, high_ref, low_ref):
    for y in range(4):
        for k in range(4):
            sent = w_ref[y, k * 256 : (k + 1) * 256, :].astype(F32)
            size = lax.rsqrt(lax.rsqrt(jnp.abs(sent))) * 2.0**-SHIFT
            delta = jnp.where(sent < 0, -size, size)
            high = delta.astype(BF16)
            at = (y // 2) * 1024 + k * 256
            lane = (y % 2) * 128
            high_ref[at : at + 256, lane : lane + 128] = high
            low_ref[at : at + 256, lane : lane + 128] = (delta - high.astype(F32)).astype(BF16)


def forward(rows, high_ref, low_ref):
    part = jnp.dot(rows, high_ref[...], preferred_element_type=F32)
    part += jnp.dot(rows, low_ref[...], preferred_element_type=F32)
    return part.astype(BF16)


def forward_most_kernel(*refs):
    pieces, (high_ref, low_ref, at_ref, out_ref, held_ref, sems) = refs[: NX + 3], refs[NX + 3 :]
    loads = [
        pltpu.make_async_copy(piece, held_ref.at[i], sems.at[i]) for i, piece in enumerate(pieces)
    ]
    for load in loads:
        load.start()
    for i, load in enumerate(loads):
        load.wait()
        back, row = (BACK[i], 0) if i < NX else (BACK[SOON[i - NX]], 128)
        x = (at_ref[0] + back) % NX
        out_ref[x, row : row + 128] = forward(held_ref[i], high_ref, low_ref)
    out_ref[(at_ref[0] + BACK[LAST]) % NX, 128:] = jnp.zeros((128, 256), BF16)


def forward_last_kernel(pair_hbm, part_ref, high_ref, low_ref, at_ref, *rest):
    out_ref, held_ref, sem = rest
    load = pltpu.make_async_copy(pair_hbm, held_ref, sem)
    load.start()
    out_ref[...] = part_ref[...]
    load.wait()
    out_ref[(at_ref[0] + BACK[LAST]) % NX, 128:] = forward(held_ref[...], high_ref, low_ref)


def thirds(value, rows):
    high = value.astype(BF16).astype(F32)
    mid = (value - high).astype(BF16).astype(F32)
    low = value - high - mid
    row = lax.broadcasted_iota(jnp.int32, (rows, value.shape[1]), 0)
    return jnp.where(row == 0, high, jnp.where(row == 1, mid, jnp.where(row == 2, low, 0.0)))


def slope_kernel(part_ref, out_ref, loss_ref):
    diff = part_ref[0].astype(F32)
    for x in range(1, NX):
        diff = diff + part_ref[x].astype(F32)
    slope = diff.astype(BF16)
    for x in range(NX):
        out_ref[x] = slope
    square = diff * diff
    loss_ref[...] = jnp.sum(square[:, :128] + square[:, 128:], axis=0, keepdims=True)


def grad_kernel(*refs):
    held_ref, last_ref, slope_ref, loss_ref, at_ref, out_ref, s_ref, term_ref = refs
    contract = (((0,), (0,)), ((), ()))
    for i in range(NX):
        x = (at_ref[0] + BACK[i]) % NX
        s_ref[i * 128 : (i + 1) * 128] = slope_ref[x, :128]
        s_ref[512 + i * 128 : 512 + (i + 1) * 128] = slope_ref[x, 128:]
    for k in range(8):
        at = k * 256
        rows = [held_ref[i, :, at : at + 256] for i in range(NX + 3)]
        rows.insert(NX + LAST, last_ref[:, at : at + 256])
        rows = jnp.concatenate(rows, axis=0)
        term = lax.dot_general(rows, s_ref[...], contract, preferred_element_type=F32)
        for yh in range(2):
            term_ref[(k // 4) * 2 + yh, (k % 4) * 8 : (k % 4 + 1) * 8] = term[
                :, yh * 128 : (yh + 1) * 128
            ].reshape(8, 4, 8, 128)
    loss = thirds(loss_ref[...], 16).astype(BF16)
    for y in range(4):
        term = term_ref[y].reshape(NZ, NC, 4, 8, 128)
        for c in range(NC):
            for x, rows in enumerate(swap_all([term[:, c, q] for q in range(4)])):
                at = place_in_plane(y // 2, c, y % 2, x)
                out_ref[at, :128, :] = rows.reshape(128, 128).astype(BF16)
                out_ref[at, 128:, :] = loss


def gather_kernel(got_ref, pat_ref, out_ref, mid_ref):
    loss = got_ref[0, 128:, :].astype(F32)
    for i in range(1, 32):
        loss = loss + got_ref[i, 128:, :].astype(F32)
    loss = jnp.sum(jnp.sum(loss, axis=0, keepdims=True), axis=1, keepdims=True)
    loss = thirds(jnp.broadcast_to(loss, (1, 128)), 16)
    lane = lax.broadcasted_iota(jnp.int32, (16, 128), 1)
    mid_ref[:, 32:, :] = jnp.broadcast_to(jnp.where(lane == 0, loss, 0.0), (NZ, 16, 128))
    group = lane_group((NZ, 8, 128))
    for x in range(NX):
        rows = jnp.zeros((NZ, 8, 128), F32)
        for c in range(NC):
            total = jnp.zeros((128, 128), F32)
            for y in range(4):
                total += got_ref[place_in_plane(y // 2, c, y % 2, x), :128, :].astype(F32)
            total = total.reshape(NZ, 8, 128)
            for i, which in enumerate(kept_rows(pat_ref[c, :, x])):
                kept = jnp.where(which == group.astype(F32), total, 0.0)
                kept += pltpu.roll(kept, 64, 2)
                kept += pltpu.roll(kept, 32, 2)
                rows = jnp.where(group == i * 2 + c, kept, rows)
        mid_ref[:, x * 8 : (x + 1) * 8, :] = rows
    out_ref[...] = mid_ref[...].astype(BF16)


def final_kernel(got_ref, pat_ref, out_ref, loss_ref):
    total = got_ref[0].astype(F32)
    for z in range(1, NZ):
        total = total + got_ref[z].astype(F32)
    loss = jnp.sum(jnp.sum(total[32:], axis=0, keepdims=True), axis=1, keepdims=True)
    loss_ref[...] = loss / (TOKENS * KVW)
    kept = total[:32]
    row = lax.broadcasted_iota(jnp.int32, (32, 128), 0)
    col = lax.broadcasted_iota(jnp.int32, (32, 128), 1)
    spread = jnp.where(col // 4 == row, 1.0, 0.0).astype(BF16)
    wide = jnp.zeros((128, 128), F32)
    for _ in range(3):
        part = kept.astype(BF16)
        kept = kept - part.astype(F32)
        wide += lax.dot_general(
            part, spread, (((0,), (0,)), ((), ())), preferred_element_type=F32
        )
    first, second = kept_rows(pat_ref[...])
    spot = row_of_four(wide[:64].shape)
    grad = jnp.where(spot == first, wide[:64], 0.0) + jnp.where(spot == second, wide[64:], 0.0)
    out_ref[...] = grad / jnp.sqrt(F32(TOKENS))


def ring(step):
    return [(i, (i + step) % NX) for i in range(NX)]


def shards(hidden, norm_gain, teacher_k, student_k, keep_pattern):
    z, yl, core, yh, x = (lax.axis_index(a) for a in AXES)
    place = (z * NYL + yl) * NC + core
    at = jnp.stack([x, core, yl, place, yh]).astype(jnp.int32)
    patterns = keep_pattern.T

    packed, pat = call(
        pack_kernel,
        (shape((NZ, 64, 128), BF16), shape((64, 128), F32)),
        teacher_k.T,
        student_k.T,
        patterns,
        place.reshape(1).astype(jnp.int32),
        scratch=[
            pltpu.VMEM((64, 128), BF16),
            pltpu.VMEM((64, 128), BF16),
            pltpu.VMEM((64, 128), jnp.int32),
            pltpu.SemaphoreType.DMA((3,)),
        ],
        far=(0, 1, 2),
        grant=60,
        name="pack",
    )
    got_w = lax.all_to_all(packed.reshape(128, 8, 128), ZCX, 0, 0, tiled=True)

    split = call(
        norm_kernel,
        (shape((128, 2048), BF16),) * NX,
        hidden,
        norm_gain.reshape(64, 128),
        x.reshape(1).astype(jnp.int32),
        scratch=[
            pltpu.VMEM((128, D), BF16),
            pltpu.VMEM((512, 512), BF16),
            pltpu.VMEM((NX, 128, 2048), BF16),
            pltpu.SemaphoreType.DMA((8,)),
            pltpu.SemaphoreType.DMA((2 * NX,)),
        ],
        flops=2 * 2048 * 512 * 512,
        far=(0,),
        out_far=True,
        grant=60,
        name="norm",
    )
    own = [split[0]] + [lax.ppermute(split[i], "x", ring(STEP[i])) for i in range(1, NX)]
    rows_w = call(
        spread_kernel,
        shape((4, 1024, 128), BF16),
        got_w.reshape(1024, 128),
        scratch=[pltpu.VMEM((32, 4, 8, 128), F32)],
        name="spread",
    )
    all_w = lax.all_to_all(rows_w, Y, 0, 0, tiled=True)

    late, _ = lax.optimization_barrier((patterns, rows_w))
    own_pat = call(
        choose_kernel,
        shape((NC, NZ, NX, 8, 128), F32),
        late,
        at,
        scratch=[pltpu.VMEM((NZ, NYL, NC, NX, 8, 128), F32)],
        name="choose",
    )
    own[3], own_pat = lax.optimization_barrier((own[3], own_pat))
    pair = [lax.ppermute(piece, "core", [(0, 1), (1, 0)]) for piece in own]

    high, low = call(decode_kernel, (shape((2048, 256), BF16),) * 2, all_w, name="decode")

    flops = 2 * 1024 * 2048 * 256
    part, held = call(
        forward_most_kernel,
        (shape((NX, 256, 256), BF16), shape((NX + 3, 128, 2048), BF16)),
        *own,
        *(pair[i] for i in SOON),
        high,
        low,
        at,
        scratch=[pltpu.SemaphoreType.DMA((NX + 3,))],
        flops=2 * flops * 7 // 8,
        far=range(NX + 3),
        name="forward_most",
    )
    part, last = call(
        forward_last_kernel,
        (shape((NX, 256, 256), BF16), shape((128, 2048), BF16)),
        pair[LAST],
        part,
        high,
        low,
        at,
        scratch=[pltpu.SemaphoreType.DMA],
        flops=flops // 4,
        far=(0,),
        name="forward_last",
    )
    got_part = lax.all_to_all(part, "x", 0, 0, tiled=True)
    slope, loss_part = call(
        slope_kernel, (shape((NX, 256, 256), BF16), shape((1, 128), F32)), got_part, name="slope"
    )
    slopes = lax.all_to_all(slope, "x", 0, 0, tiled=True)

    term = call(
        grad_kernel,
        shape((32, 144, 128), BF16),
        held,
        last,
        slopes,
        loss_part,
        at,
        scratch=[pltpu.VMEM((1024, 256), BF16), pltpu.VMEM((4, 32, 4, 8, 128), F32)],
        flops=flops,
        name="grad",
    )
    got_term = lax.all_to_all(term, PLANE, 0, 0, tiled=True)
    packed_term = call(
        gather_kernel,
        shape((NZ, 48, 128), BF16),
        got_term,
        own_pat,
        scratch=[pltpu.VMEM((NZ, 48, 128), F32)],
        name="gather",
    )
    got_sum = lax.all_to_all(packed_term, "z", 0, 0, tiled=True)
    grad, loss = call(
        final_kernel,
        (shape((64, 128), F32), shape((1, 1), F32)),
        got_sum,
        pat,
        name="final",
    )
    return grad.T, loss.reshape(())


def solution(mesh):
    fine = Mesh(mesh.devices.reshape(NZ, NYL, NC, NYH, NX), AXES)
    dp, tensor = ("z", "yl", "core"), ("yh", "x")
    in_specs = (P(AXES, None), P(), P(dp, tensor), P(dp, tensor), P(None, tensor))
    out_specs = (P(dp, tensor), P())
    return jax.shard_map(shards, mesh=fine, in_specs=in_specs, out_specs=out_specs, check_vma=False)
```
